32 devices in a mesh: dp: 8 (over y, x, core), tensor: 4 (over z).
Axes of the slice: x: 2, y: 2, z: 4, core: 2. Of those that a mesh axis runs over, the one named last changes fastest.
Arguments:
- tokens_in: bfloat16 [16, 1028, 1024], P('dp', 'tensor'), may hold values from -6 to 6
- cotangent: bfloat16 [16, 1028, 1024], P('dp', 'tensor'), may hold values from -6 to 6
- image_flag: int32 [16], P('dp'), may hold values from 0 to 1, as said below
- key_mask: int32 [16, 1028], P('dp'), may hold values from 0 to 1, as said below
- column_mask: int32 [2736], P('tensor'), may hold values from 0 to 1, as said below
- attention_norm_gain: float32 [1024], replicated, may hold values from 0.5 to 1.5
- attention_norm_bias: float32 [1024], replicated, may hold values from -2 to 2
- w_query: bfloat16 [1024, 1024], P('dp', 'tensor'), may hold values from -0.1875 to 0.1875
- w_key: bfloat16 [1024, 1024], P('dp', 'tensor'), may hold values from -0.1875 to 0.1875
- w_value: bfloat16 [1024, 1024], P('dp', 'tensor'), may hold values from -0.1875 to 0.1875
- query_bias: float32 [1024], P('tensor'), may hold values from -2 to 2
- value_bias: float32 [1024], P('tensor'), may hold values from -2 to 2
- w_out: bfloat16 [1024, 1024], P('tensor', 'dp'), may hold values from -3 to 3
- out_bias: float32 [1024], replicated, may hold values from -2 to 2
- feedforward_norm_gain: float32 [1024], replicated, may hold values from 0.5 to 1.5
- feedforward_norm_bias: float32 [1024], replicated, may hold values from -2 to 2
- w_gate: bfloat16 [1024, 2736], P('dp', 'tensor'), may hold values from -0.1875 to 0.1875
- gate_bias: float32 [2736], P('tensor'), may hold values from -2 to 2
- w_up: bfloat16 [1024, 2736], P('dp', 'tensor'), may hold values from -0.1875 to 0.1875
- up_bias: float32 [2736], P('tensor'), may hold values from -2 to 2
- inner_gain: float32 [2736], P('tensor'), may hold values from 0.5 to 1.5
- inner_shift: float32 [2736], P('tensor'), may hold values from -2 to 2
- w_down: bfloat16 [2736, 1024], P('tensor', 'dp'), may hold values from -0.109375 to 0.109375
- down_bias: float32 [1024], replicated, may hold values from -2 to 2
Outputs:
- output: bfloat16 [16, 1028, 1024], P('dp', 'tensor')
- input_grad: float32 [16, 1028, 1024], P('dp', 'tensor')
- attn_gain_grad: float32 [1024], replicated
- attn_shift_grad: float32 [1024], replicated
- w_query_grad: float32 [1024, 1024], P('dp', 'tensor')
- w_key_grad: float32 [1024, 1024], P('dp', 'tensor')
- w_value_grad: float32 [1024, 1024], P('dp', 'tensor')
- query_bias_grad: float32 [1024], P('tensor')
- value_bias_grad: float32 [1024], P('tensor')
- w_out_grad: float32 [1024, 1024], P('tensor', 'dp')
- out_bias_grad: float32 [1024], replicated
- mlp_gain_grad: float32 [1024], replicated
- mlp_shift_grad: float32 [1024], replicated
- w_gate_grad: float32 [1024, 2736], P('dp', 'tensor')
- gate_bias_grad: float32 [2736], P('tensor')
- w_up_grad: float32 [1024, 2736], P('dp', 'tensor')
- up_bias_grad: float32 [2736], P('tensor')
- inner_gain_grad: float32 [2736], P('tensor')
- inner_shift_grad: float32 [2736], P('tensor')
- w_down_grad: float32 [2736, 1024], P('tensor', 'dp')
- down_bias_grad: float32 [1024], replicated
The draws below stay inside these ranges and needn't reach their ends.
Inputs may be any that keep to these rules, and one draw needn't show every extreme that they name: `image_flag`: exactly one image has flag 0. `key_mask`: each image has exactly 3 zeros. `column_mask`: exactly 6 zeros.
All inputs are finite; a program needn't handle non-finite values.
Results may differ from the reference program's by a relative error of at most 0.03.
Values may be sent and summed in bfloat16 or wider, within the bound.
A program may use at most 256 MiB of HBM per device.

```python
import jax
import jax.numpy as jnp
from jax import lax

D = 1024
HEAD = 64
FF = 2736
PADCOLS = 6
GRID = 32
PADTOK = 3
SEQ = 1028
IMAGES = 16
N_TENSOR = 4


def draw_image_flag(key, part):
    empty = jax.random.randint(key, (), 0, IMAGES)
    return (jnp.arange(IMAGES, dtype=jnp.int32) != empty).astype(jnp.int32)


def ranked_ones(key, rows, length, zeros):
    noise = jax.random.randint(key, (rows, length), 0, 1 << 20) * length + jnp.arange(length, dtype=jnp.int32)[None, :]
    order = jnp.argsort(noise, axis=1, stable=True)
    ranks = jnp.argsort(order, axis=1, stable=True)
    return (ranks >= zeros).astype(jnp.int32)


def draw_key_mask(key, part):
    return ranked_ones(key, IMAGES, SEQ, PADTOK)


def draw_column_mask(key, part):
    return ranked_ones(key, 1, FF, PADCOLS)[0]


def shard_levels(rng, shape, shards, low, top_value):
    def one(position, parts):
        heights = jax.random.uniform(jax.random.fold_in(jax.random.fold_in(rng, 6), position), (parts,), jnp.float32, low / len(shards), top_value / len(shards))
        return jnp.repeat(jnp.exp(heights), shape[position] // parts).reshape((-1,) + (1,) * (len(shape) - position - 1))

    loudness = one(*shards[0])
    for cut in shards[1:]:
        loudness = loudness * one(*cut)
    return loudness


def scatter_about(stream_key, shape, deviation, reach, split=(), held_as=jnp.bfloat16):
    drawn = jax.random.normal(stream_key, shape, jnp.float32) * deviation
    if len(split) > 0:
        drawn = shard_levels(stream_key, shape, split, -0.22, 0.18) * drawn
    return jnp.clip(drawn, min=-reach, max=reach).astype(held_as)


def setup_inputs(seed: int = 0) -> dict:
    key_of = jax.random.split(jax.random.key(seed), 25)
    return {
        "tokens_in": scatter_about(key_of[0], (IMAGES, SEQ, D), 1.0, 6.0, ((0, 8), (1, 4))),
        "cotangent": scatter_about(key_of[1], (IMAGES, SEQ, D), 1.0, 6.0, ((0, 8), (1, 4))),
        "image_flag": draw_image_flag(jax.random.fold_in(key_of[24], 71), 0),
        "key_mask": draw_key_mask(jax.random.fold_in(key_of[24], 71), 0),
        "column_mask": draw_column_mask(jax.random.fold_in(key_of[24], 71), 0),
        "attention_norm_gain": jnp.clip(1.0 + 0.1 * jax.random.normal(key_of[5], (D,), jnp.float32), 0.5, 1.5),
        "attention_norm_bias": scatter_about(key_of[6], (D,), 0.3, 2.0, (), jnp.float32),
        "w_query": scatter_about(key_of[7], (D, D), D ** -0.5, 0.1875, ((0, 8), (1, 4))),
        "w_key": scatter_about(key_of[8], (D, D), D ** -0.5, 0.1875, ((0, 8), (1, 4))),
        "w_value": scatter_about(key_of[9], (D, D), D ** -0.5, 0.1875, ((0, 8), (1, 4))),
        "query_bias": scatter_about(key_of[10], (D,), 0.3, 2.0, ((0, 4),), jnp.float32),
        "value_bias": scatter_about(key_of[11], (D,), 0.3, 2.0, ((0, 4),), jnp.float32),
        "w_out": scatter_about(key_of[12], (D, D), (max(D // 256, 1)) ** -0.5, 3.0, ((0, 4), (1, 8))),
        "out_bias": scatter_about(key_of[13], (D,), 0.3, 2.0, (), jnp.float32),
        "feedforward_norm_gain": jnp.clip(1.0 + 0.1 * jax.random.normal(key_of[14], (D,), jnp.float32), 0.5, 1.5),
        "feedforward_norm_bias": scatter_about(key_of[15], (D,), 0.3, 2.0, (), jnp.float32),
        "w_gate": scatter_about(key_of[16], (D, FF), D ** -0.5, 0.1875, ((0, 8), (1, 4))),
        "gate_bias": scatter_about(key_of[17], (FF,), 0.3, 2.0, ((0, 4),), jnp.float32),
        "w_up": scatter_about(key_of[18], (D, FF), D ** -0.5, 0.1875, ((0, 8), (1, 4))),
        "up_bias": scatter_about(key_of[19], (FF,), 0.3, 2.0, ((0, 4),), jnp.float32),
        "inner_gain": jnp.clip(1.0 + 0.1 * jax.random.normal(key_of[20], (FF,), jnp.float32), 0.5, 1.5),
        "inner_shift": scatter_about(key_of[21], (FF,), 0.3, 2.0, ((0, 4),), jnp.float32),
        "w_down": scatter_about(key_of[22], (FF, D), FF ** -0.5, 0.109375, ((0, 4), (1, 8))),
        "down_bias": scatter_about(key_of[23], (D,), 0.3, 2.0, (), jnp.float32),
    }


@jax.custom_vjp
def low(v):
    return lax.optimization_barrier(v.astype(jnp.bfloat16)).astype(jnp.float32)

@jax.custom_vjp
def low_back(v):
    return v

def low_keep(v):
    return (low(v), None)

def low_pass(kept, grad):
    return (grad,)

def back_keep(v):
    return (v, None)

def back_low(kept, grad):
    return (low(grad),)
low.defvjp(low_keep, low_pass)
low_back.defvjp(back_keep, back_low)
EPS = 1e-06
ROPE_BASE = 10000.0
HIGH = lax.Precision.HIGHEST

def matrix(left, right):
    return jnp.dot(left, right, precision=HIGH, preferred_element_type=jnp.float32)

def layer_norm(values, norm_gain, shift):
    row_mean = lax.optimization_barrier(jnp.mean(values, axis=-1, keepdims=True))
    var = lax.optimization_barrier(jnp.mean(jnp.square(values - row_mean), axis=-1, keepdims=True))
    return (values - row_mean) * lax.rsqrt(var + EPS) * norm_gain + shift

def rotary_tables(length, head):
    quarter = head // 4
    place = jnp.arange(length, dtype=jnp.int32)
    inside = (place >= 1) & (place <= GRID * GRID)
    cell = jnp.maximum(place - 1, 0)
    row_pos = jnp.where(inside, cell // GRID, 0).astype(jnp.float32)
    col_pos = jnp.where(inside, cell % GRID, 0).astype(jnp.float32)
    freq = ROPE_BASE ** (-jnp.arange(quarter, dtype=jnp.float32) / quarter)
    angle = jnp.concatenate([row_pos[:, None] * freq[None, :], col_pos[:, None] * freq[None, :]], axis=1)
    return (jnp.cos(angle)[:, None, :], jnp.sin(angle)[:, None, :])

def rotate(values, cosv, sinv):
    quarter = values.shape[-1] // 4
    first = jnp.concatenate([values[..., :quarter], values[..., 2 * quarter:3 * quarter]], axis=-1)
    second = jnp.concatenate([values[..., quarter:2 * quarter], values[..., 3 * quarter:]], axis=-1)
    new_first = first * cosv - second * sinv
    new_second = second * cosv + first * sinv
    return jnp.concatenate([new_first[..., :quarter], new_second[..., :quarter], new_first[..., quarter:], new_second[..., quarter:]], axis=-1)

def grouped_projection(copies, weight):
    width = weight.shape[1] // N_TENSOR
    return jnp.concatenate([low_back(matrix(copies[group], weight[:, group * width:(group + 1) * width])) for group in range(N_TENSOR)], axis=1)

def grouped_sum(left, weight):
    width = left.shape[1] // N_TENSOR
    total = low(matrix(left[:, :width], weight[:width, :]))
    for group in range(1, N_TENSOR):
        total = total + low(matrix(left[:, group * width:(group + 1) * width], weight[group * width:(group + 1) * width, :]))
    return low_back(total)

def forward(params, token_rows, keys_live, columns):
    attention_norm_gain, attention_norm_bias, w_query, w_key, w_value, query_bias, value_bias, w_out, out_bias, feedforward_norm_gain, feedforward_norm_bias, w_gate, gate_bias, w_up, up_bias, inner_gain, inner_shift, w_down, down_bias = params
    length = token_rows.shape[0]
    heads = w_query.shape[1] // HEAD
    cosv, sinv = rotary_tables(length, HEAD)
    normed_rows = low(layer_norm(token_rows, attention_norm_gain, attention_norm_bias))
    copies = [low_back(normed_rows) for group in range(N_TENSOR)]
    query = low(rotate((grouped_projection(copies, w_query) + query_bias).reshape(length, heads, HEAD), cosv, sinv))
    key = low(rotate(grouped_projection(copies, w_key).reshape(length, heads, HEAD), cosv, sinv))
    value = low((grouped_projection(copies, w_value) + value_bias).reshape(length, heads, HEAD))
    scores = low_back(jnp.einsum('qhd,khd->hqk', query, key, precision=HIGH) * HEAD ** (-0.5))
    scores = jnp.where(keys_live[None, None, :] > 0, scores, -1e+30)
    top = lax.optimization_barrier(jnp.max(scores, axis=-1, keepdims=True))
    expo = jnp.exp(scores - top)
    probs = low(expo / lax.optimization_barrier(jnp.sum(expo, axis=-1, keepdims=True)))
    mixed = low(low_back(jnp.einsum('hqk,khd->qhd', probs, value, precision=HIGH)).reshape(length, heads * HEAD))
    middle_activation = token_rows + grouped_sum(mixed, w_out) + out_bias
    normed_second_rows = low(layer_norm(middle_activation, feedforward_norm_gain, feedforward_norm_bias))
    second_copies = [low_back(normed_second_rows) for group in range(N_TENSOR)]
    gate = grouped_projection(second_copies, w_gate) + gate_bias
    up_part = grouped_projection(second_copies, w_up) + up_bias
    act = gate * jax.nn.sigmoid(gate) * up_part
    count = jnp.sum(columns)
    row_mean = lax.optimization_barrier(jnp.sum(act * columns, axis=-1, keepdims=True)) / count
    var = lax.optimization_barrier(jnp.sum(act * act * columns, axis=-1, keepdims=True)) / count - row_mean * row_mean
    hidden = low(columns * ((act - row_mean) * lax.rsqrt(var + EPS) * inner_gain + inner_shift))
    return middle_activation + grouped_sum(hidden, w_down) + down_bias

def reference(tokens_in, cotangent, image_flag, key_mask, column_mask, attention_norm_gain, attention_norm_bias, w_query, w_key, w_value, query_bias, value_bias, w_out, out_bias, feedforward_norm_gain, feedforward_norm_bias, w_gate, gate_bias, w_up, up_bias, inner_gain, inner_shift, w_down, down_bias):
    params = tuple((item.astype(jnp.float32) for item in (attention_norm_gain, attention_norm_bias, w_query, w_key, w_value, query_bias, value_bias, w_out, out_bias, feedforward_norm_gain, feedforward_norm_bias, w_gate, gate_bias, w_up, up_bias, inner_gain, inner_shift, w_down, down_bias)))
    columns = column_mask.astype(jnp.float32)

    def one_image(totals, item):
        token_rows, cot, flag, keys_live = item

        def apply(prm, tok):
            return forward(prm, tok, keys_live, columns)
        result, pullback = jax.vjp(apply, params, token_rows.astype(jnp.float32))
        grads, token_grad = pullback(cot.astype(jnp.float32) * flag.astype(jnp.float32))
        totals = jax.tree.map(lambda left, right: left + right, totals, grads)
        return (totals, (result.astype(jnp.bfloat16), token_grad))
    zeros = jax.tree.map(jnp.zeros_like, params)
    totals, (output, input_grad) = lax.scan(one_image, zeros, (tokens_in, cotangent, image_flag, key_mask))
    return (output, input_grad, totals[0], totals[1], totals[2], totals[3], totals[4], totals[5], totals[6], totals[7], totals[8], totals[9], totals[10], totals[11], totals[12], totals[13], totals[14], totals[15], totals[16], totals[17], totals[18])
```

```python
import functools
import math

import jax
import jax.numpy as jnp
from jax import lax
from jax.experimental import pallas as pl
from jax.experimental.pallas import tpu as pltpu
from jax.sharding import PartitionSpec as P

HEAD = 64
FF = 2736
PADCOLS = 6
GRID = 32
EPS = 1e-06
ROPE_BASE = 10000.0
LANES = 128
MESH = pl.DeviceIdType.MESH
LOG2E = math.log2(math.e)
LN2 = math.log(2.0)
SCALE = HEAD ** (-0.5)
F32 = jnp.float32
BF16 = jnp.bfloat16


def up_to(size, unit):
    return -(-size // unit) * unit


def rotary_tables(length, head):
    quarter = head // 4
    place = jnp.arange(length, dtype=jnp.int32)
    inside = (place >= 1) & (place <= GRID * GRID)
    cell = jnp.maximum(place - 1, 0)
    row_pos = jnp.where(inside, cell // GRID, 0).astype(F32)
    col_pos = jnp.where(inside, cell % GRID, 0).astype(F32)
    freq = ROPE_BASE ** (-jnp.arange(quarter, dtype=F32) / quarter)
    angle = jnp.concatenate(
        [row_pos[:, None] * freq[None, :], col_pos[:, None] * freq[None, :]], axis=1
    )
    return jnp.cos(angle), jnp.sin(angle)


def lane_tables(length, quarter, block, rows_padded):
    cosv, sinv = rotary_tables(length, HEAD)

    def lay(first, second):
        one = jnp.concatenate(
            [first[:, :quarter], second[:, :quarter], first[:, quarter:], second[:, quarter:]], axis=1
        )
        two = jnp.concatenate([one, one], axis=1)
        cut = two.reshape(length // block, block, 2 * HEAD)
        return jnp.pad(cut, ((0, 0), (0, rows_padded - block), (0, 0))).reshape(-1, 2 * HEAD)

    zero = jnp.zeros_like(sinv)
    return lay(cosv, cosv), lay(-sinv, zero), lay(zero, sinv)


def norm_pieces(values):
    row_mean = jnp.mean(values, axis=-1, keepdims=True)
    var = jnp.mean(jnp.square(values - row_mean), axis=-1, keepdims=True)
    inverse_scale = lax.rsqrt(var + EPS)
    return ((values - row_mean) * inverse_scale, inverse_scale)


def norm_backward(incoming_gradient, centered_normalized, inverse_scale, norm_gain):
    inner = incoming_gradient * norm_gain
    return inverse_scale * (
        inner
        - jnp.mean(inner, axis=-1, keepdims=True)
        - centered_normalized * jnp.mean(inner * centered_normalized, axis=-1, keepdims=True)
    )


def matmul(left, right):
    return jnp.dot(left, right, preferred_element_type=F32)


def matmul_right_t(left, right):
    return lax.dot_general(left, right, (((1,), (1,)), ((), ())), preferred_element_type=F32)


def matmul_left_t(left, right):
    return lax.dot_general(left, right, (((0,), (0,)), ((), ())), preferred_element_type=F32)


class Kind:
    def __init__(self, by_rows, shard, n_dp):
        self.given = shard
        self.n_dp = n_dp
        self.turn = not by_rows and shard[1] % LANES != 0
        if self.turn:
            shard = (shard[1], up_to(shard[0], LANES))
        self.by_rows = by_rows or self.turn
        self.shard = shard
        a, b = shard
        if self.by_rows:
            self.whole, self.two = (n_dp * a, 2 * b), (2 * a, b)
        else:
            self.whole, self.two = (2 * a, n_dp * b), (a, 2 * b)

    def piece(self, ref, slot, chip):
        a, b = self.shard
        if self.by_rows:
            return ref.at[pl.ds(_mult(chip, 2 * a), 2 * a), pl.ds(_mult(slot, b), b)]
        return ref.at[pl.ds(_mult(slot, a), a), pl.ds(_mult(chip, 2 * b), 2 * b)]

    def half(self, two, core):
        a, b = self.shard
        if self.by_rows:
            return two.at[pl.ds(_mult(core, a), a)]
        return two.at[:, pl.ds(_mult(core, b), b)]

    def one(self, ref, slot, chip, core):
        a, b = self.shard
        if self.by_rows:
            return ref.at[pl.ds(_mult(chip * 2 + core, a), a), pl.ds(_mult(slot, b), b)]
        return ref.at[pl.ds(_mult(slot, a), a), pl.ds(_mult(chip * 2 + core, b), b)]

    def enter(self, shard):
        if not self.turn:
            return shard
        return jnp.pad(shard.T, ((0, 0), (0, self.shard[1] - self.given[0])))

    def leave(self, shard):
        return shard[:, : self.given[0]].T if self.turn else shard

    def join(self, whole):
        if not self.turn:
            return whole
        a, b = self.shard
        whole = whole.reshape(self.n_dp * a, 2, b)[:, :, : self.given[0]]
        return whole.transpose(1, 2, 0).reshape(2 * self.given[0], self.n_dp * a)

    def cut(self, whole):
        if not self.turn:
            return whole
        a, b = self.shard
        whole = whole.reshape(2, self.given[0], self.n_dp * a).transpose(2, 0, 1)
        return jnp.pad(whole, ((0, 0), (0, 0), (0, b - self.given[0]))).reshape(self.whole)


def _mult(index, size):
    return index * size if isinstance(index, int) else pl.multiple_of(index * size, size)


class Place:
    def __init__(self, n_dp, n_tensor):
        self.dp = lax.axis_index("dp")
        self.z = lax.axis_index("tensor")
        self.core = lax.rem(self.dp, 2)
        self.chip = lax.div(self.dp, 2)
        self.nz = n_tensor
        self.chips = n_dp // 2
        self.bits = self.chips.bit_length() - 1
        self.home = self.core == lax.div(self.z, n_tensor // 2)
        self.slot = lax.rem(self.z, n_tensor // 2)

    def flip(self, bit):
        low = lax.rem(lax.div(self.chip, 1 << bit), 2)
        return self.chip + (1 - 2 * low) * (1 << bit)

    def across(self):
        return (self.dp + 1 - 2 * self.core, self.z)

    def beside(self, bit):
        return (self.flip(bit) * 2 + self.core, self.z)

    def shifted(self, by):
        return (self.dp, lax.rem(self.z + by, self.nz))

    def barrier(self):
        everyone = [self.across()]
        everyone += [self.shifted(s) for s in range(1, self.nz)]
        everyone += [self.beside(b) for b in range(self.bits)]
        bar = pltpu.get_barrier_semaphore()
        for one in everyone:
            pl.semaphore_signal(bar, inc=1, device_id=one, device_id_type=MESH)
        pl.semaphore_wait(bar, len(everyone))


def remote(src, dst, send, recv, to):
    return pltpu.make_async_remote_copy(
        src_ref=src, dst_ref=dst, send_sem=send, recv_sem=recv, device_id=to, device_id_type=MESH
    )


def flipped(chip, value):
    return lax.bitwise_xor(chip, value)


def gather_kernel(kinds, n_acts, n_packs, n_pairs, sizes, *refs):
    n_dp, n_tensor = sizes
    n_w = len(kinds)
    me = Place(n_dp, n_tensor)
    at = 0
    groups = []
    for count in (n_acts, n_packs, n_pairs, n_w) * 2:
        groups.append(refs[at : at + count])
        at += count
    act_in, pack_in, pair_in, w_in, act_out, pack_out, pair_out, w_out = groups
    (a_send, a_recv, a_fwd, a_back, k_send, k_recv, q_send, q_recv, s_send, s_recv, z_send, z_recv, b_send, b_recv, loc) = refs[at:]
    half_z = n_tensor // 2
    me.barrier()

    def local(src, dst, n):
        return pltpu.make_async_copy(src, dst, loc.at[n])

    for j, kind in enumerate(kinds):
        mine = kind.one(w_out[j], me.slot, me.chip, me.core)

        @pl.when(me.home)
        def _(j=j, mine=mine):
            local(w_in[j], mine, j).start()

        @pl.when(jnp.logical_not(me.home))
        def _(j=j, mine=mine):
            remote(w_in[j], mine, s_send.at[j], s_recv.at[j], me.across()).start()

    def act_copy(n, i):
        target = half_z * me.core + i
        return target, remote(
            act_in[n].at[i], act_out[n].at[me.z], a_send.at[n, i], a_recv.at[n, me.z], (me.dp, target)
        )

    def start_acts(n):
        for i in range(half_z):
            target, copy = act_copy(n, i)
            pl.when(target != me.z)(copy.start)

            @pl.when(target == me.z)
            def _(n=n, i=i):
                local(act_in[n].at[i], act_out[n].at[me.z], n_w + n).start()

    def pass_acts(n):
        @pl.when(me.home)
        def _():
            for s in range(n_tensor):
                src = lax.rem(me.z + s, n_tensor)
                slab = act_out[n].at[src]
                if s == 0:
                    local(slab, slab, n_w + n).wait()
                else:
                    remote(slab, slab, a_send.at[n, 0], a_recv.at[n, src], me.across()).wait_recv()
                remote(slab, slab, a_fwd.at[n, src], a_back.at[n, src], me.across()).start()

    def end_acts(n):
        for i in range(half_z):
            target, copy = act_copy(n, i)
            pl.when(target != me.z)(copy.wait_send)
        for src in range(n_tensor):
            slab = act_out[n].at[src]
            copy = remote(slab, slab, a_fwd.at[n, src], a_back.at[n, src], me.across())

            pl.when(me.home)(copy.wait_send)
            pl.when(jnp.logical_not(me.home))(copy.wait_recv)

    def pack_copy(n, s):
        return remote(
            pack_in[n], pack_out[n].at[me.slot], k_send.at[n, s - 1], k_recv.at[n, me.slot], me.shifted(s)
        )

    for n in range(n_packs):

        @pl.when(me.home)
        def _(n=n):
            local(pack_in[n], pack_out[n].at[me.slot], n_w + n_acts + n).start()
            for s in range(1, n_tensor):
                pack_copy(n, s).start()

    for n in range(n_pairs):
        there = remote(pair_in[n], pair_out[n], q_send.at[n], q_recv.at[n], me.across())

        @pl.when(me.home)
        def _(n=n, there=there):
            local(pair_in[n], pair_out[n], n_w + n_acts + n_packs + n).start()
            there.start()

    if n_acts and n_packs:
        for n in range(n_acts):
            start_acts(n)

    def start_z(j):
        kind = kinds[j]
        mine = kind.one(w_out[j], me.slot, me.chip, me.core)

        @pl.when(me.home)
        def _():
            local(w_in[j], mine, j).wait()
            remote(w_in[j], mine, s_send.at[j], s_recv.at[j], me.across()).wait_recv()
            src = kind.piece(w_out[j], me.slot, me.chip)
            for s in range(1, n_tensor):
                remote(src, src, z_send.at[j, s - 1], z_recv.at[j, me.slot], me.shifted(s)).start()

    def wait_z(j):
        for slot in range(2):
            src = kinds[j].piece(w_out[j], slot, me.chip)
            copy = remote(src, src, z_send.at[j, 0], z_recv.at[j, slot], me.across())
            pl.when(me.core * half_z + slot != me.z)(copy.wait_recv)

    def bit_copies(j, step, slot):
        bit = step if slot == 0 else me.bits - 1 - step
        low = 1 if slot == 0 else 1 << (me.bits - step)

        def held(m):
            return flipped(me.chip, m * low)

        def send(m):
            src = kinds[j].piece(w_out[j], slot, held(m))
            return remote(src, src, b_send.at[j, step, slot, m], b_recv.at[j, step, slot, m], me.beside(bit))

        return send

    def start_bits(j, step):
        for slot in range(2):
            send = bit_copies(j, step, slot)
            _each(1 << step, lambda m: send(m).start())

    def wait_bits(j, step):
        for slot in range(2):
            send = bit_copies(j, step, slot)
            _each(1 << step, lambda m: send(m).wait_recv())

    lag = me.bits + 1
    if n_w:
        start_z(0)
    for tick in range(n_w + lag):
        if tick < n_w:
            wait_z(tick)
            if tick + 1 < n_w:
                start_z(tick + 1)
            elif not n_packs:
                for n in range(n_acts):
                    start_acts(n)
        for step in range(me.bits + 1):
            j = tick - step
            if 0 <= j < n_w:
                if step > 0:
                    wait_bits(j, step - 1)
                if step < me.bits:
                    start_bits(j, step)
        if tick == 0 and n_packs:
            for n in range(n_acts):
                pass_acts(n)
    if not n_packs:
        for n in range(n_acts):
            pass_acts(n)

    for j, kind in enumerate(kinds):
        mine = kind.one(w_out[j], me.slot, me.chip, me.core)
        copy = remote(w_in[j], mine, s_send.at[j], s_recv.at[j], me.across())
        pl.when(jnp.logical_not(me.home))(copy.wait_send)
        src = kind.piece(w_out[j], me.slot, me.chip)
        for s in range(1, n_tensor):
            copy = remote(src, src, z_send.at[j, s - 1], z_recv.at[j, 0], me.shifted(s))
            pl.when(me.home)(copy.wait_send)
        for step in range(me.bits):
            for slot in range(2):
                send = bit_copies(j, step, slot)
                _each(1 << step, lambda m: send(m).wait_send())
    for n in range(n_acts):
        end_acts(n)
    for n in range(n_packs):
        for slot in range(2):
            row = pack_out[n].at[slot]
            copy = remote(pack_in[n], row, k_send.at[n, 0], k_recv.at[n, slot], me.across())
            pl.when(me.core * half_z + slot != me.z)(copy.wait_recv)

        @pl.when(me.home)
        def _(n=n):
            local(pack_in[n], pack_out[n].at[me.slot], n_w + n_acts + n).wait()
            for s in range(1, n_tensor):
                pack_copy(n, s).wait_send()

    for n in range(n_pairs):
        there = remote(pair_in[n], pair_out[n], q_send.at[n], q_recv.at[n], me.across())

        @pl.when(me.home)
        def _(n=n, there=there):
            local(pair_in[n], pair_out[n], n_w + n_acts + n_packs + n).wait()
            there.wait_send()

        pl.when(jnp.logical_not(me.home))(there.wait_recv)


def _each(count, act):
    if count <= 4:
        for m in range(count):
            act(m)
    else:

        @pl.loop(0, count)
        def _(m):
            act(m)


def gather(acts, packs, pairs, weights, kinds, sizes, cid):
    n_dp, n_tensor = sizes
    bits = (n_dp // 2).bit_length() - 1
    n_a, n_k, n_q, n_w = len(acts), len(packs), len(pairs), len(weights)
    shapes = [jax.ShapeDtypeStruct((n_tensor,) + a.shape[1:], a.dtype) for a in acts]
    shapes += [jax.ShapeDtypeStruct((2,) + a.shape, a.dtype) for a in packs]
    shapes += [jax.ShapeDtypeStruct(a.shape, a.dtype) for a in pairs]
    shapes += [jax.ShapeDtypeStruct(k.whole, w.dtype) for k, w in zip(kinds, weights)]
    dma = pltpu.SemaphoreType.DMA
    na, nk, nq = max(n_a, 1), max(n_k, 1), max(n_q, 1)
    most = max(1 << max(bits - 1, 0), 1)
    out = pl.pallas_call(
        functools.partial(gather_kernel, kinds, n_a, n_k, n_q, sizes),
        out_shape=shapes,
        in_specs=[pl.BlockSpec(memory_space=pltpu.HBM)] * (n_a + n_k + n_q + n_w),
        out_specs=[pl.BlockSpec(memory_space=pltpu.HBM)] * len(shapes),
        scratch_shapes=[
            dma((na, n_tensor)),
            dma((na, n_tensor)),
            dma((na, n_tensor)),
            dma((na, n_tensor)),
            dma((nk, n_tensor)),
            dma((nk, 2)),
            dma((nq,)),
            dma((nq,)),
            dma((n_w,)),
            dma((n_w,)),
            dma((n_w, n_tensor)),
            dma((n_w, 2)),
            dma((n_w, bits, 2, most)),
            dma((n_w, bits, 2, most)),
            dma((n_w + n_a + n_k + n_q,)),
        ],
        compiler_params=pltpu.CompilerParams(collective_id=cid, has_side_effects=True),
        name=f"gather{cid}",
    )(*acts, *packs, *pairs, *[k.enter(w) for k, w in zip(kinds, weights)])
    a, k, q = out[:n_a], out[n_a : n_a + n_k], out[n_a + n_k : n_a + n_k + n_q]
    return a, k, q, [kind.join(w) for kind, w in zip(kinds, out[n_a + n_k + n_q :])]


def scatter_kernel(kinds, n_acts, sizes, *refs):
    n_dp, n_tensor = sizes
    n_w = len(kinds)
    me = Place(n_dp, n_tensor)
    half_z = n_tensor // 2
    act_in, vec_in, g_in = refs[:n_acts], refs[n_acts], refs[n_acts + 1 : n_acts + 1 + n_w]
    at = n_acts + 1 + n_w
    act_out, vec_out, g_out = refs[at : at + n_acts], refs[at + n_acts], refs[at + n_acts + 1 : at + n_acts + 1 + n_w]
    at += n_acts + 1 + n_w
    acc, got, gotz, stage = (refs[at + i * n_w : at + (i + 1) * n_w] for i in range(4))
    at += 4 * n_w
    (v_sum, v_got, v_all) = refs[at : at + 3]
    (a_send, a_recv, b_send, b_recv, z_send, z_recv, f_send, f_recv, vb_send, vb_recv, vz_send, vz_recv, vf_send, vf_recv, loc) = refs[at + 3 :]
    me.barrier()

    def local(src, dst, n):
        return pltpu.make_async_copy(src, dst, loc.at[n])

    def order(step, slot):
        if slot == 0:
            return me.bits - 1 - step, 1, 1 << (me.bits - 1 - step)
        return step, 1 << (step + 1), 1 << (me.bits - 1 - step)

    def copies(j, step, slot):
        bit, stride, count = order(step, slot)
        source = g_in[j] if step == 0 else acc[j]

        def send(m):
            src = kinds[j].piece(source, slot, flipped(me.chip, m * stride + (1 << bit)))
            dst = got[j].at[_base(me.bits, step) + m, slot]
            return remote(src, dst, b_send.at[j, step, slot, m], b_recv.at[j, step, slot, m], me.beside(bit))

        return send, count, stride

    def start_bits(j, step):
        for slot in range(2):
            send, count, _ = copies(j, step, slot)
            _each(count, lambda m: send(m).start())

    def add_bits(j, step):
        for slot in range(2):
            send, count, stride = copies(j, step, slot)

            def one(m):
                send(m).wait_recv()
                here = kinds[j].piece(acc[j], slot, flipped(me.chip, m * stride))
                here[...] = (
                    here[...].astype(F32) + got[j][_base(me.bits, step) + m, slot].astype(F32)
                ).astype(BF16)

            _each(count, one)

    def z_copy(j, slot):
        target = half_z * me.core + slot
        index = lax.rem(me.z - target + n_tensor - 1, n_tensor)
        src = kinds[j].piece(acc[j], slot, me.chip)
        return target, remote(src, gotz[j].at[index], z_send.at[j, slot], z_recv.at[j, index], (me.dp, target))

    def start_z(j):
        for slot in range(2):
            target, copy = z_copy(j, slot)
            pl.when(target != me.z)(copy.start)

    def last_copy(j):
        return remote(stage[j], g_out[j], f_send.at[j], f_recv.at[j], me.across())

    def end_z(j):
        @pl.when(me.home)
        def _():
            for index in range(n_tensor - 1):
                slab = gotz[j].at[index]
                remote(slab, slab, z_send.at[j, 0], z_recv.at[j, index], me.across()).wait_recv()

            def total(core):
                value = kinds[j].one(acc[j], me.slot, me.chip, core)[...].astype(F32)
                for index in range(n_tensor - 1):
                    value = value + kinds[j].half(gotz[j].at[index], core)[...].astype(F32)
                return value

            stage[j][...] = total(1 - me.core)
            last_copy(j).start()
            g_out[j][...] = total(me.core)

    def vec_bit(step):
        return remote(v_sum.at[step], v_got.at[step], vb_send.at[step], vb_recv.at[step], me.beside(step))

    def vec_z(s):
        return remote(v_sum.at[me.bits], v_all.at[me.z], vz_send.at[s - 1], vz_recv.at[me.z], me.shifted(s))

    def vec_last():
        return remote(v_sum.at[me.bits + 1], vec_out.at[me.core], vf_send.at[0], vf_recv.at[0], me.across())

    def vec_phase(step):
        if step == 0:
            v_sum[0] = vec_in[...]
            vec_bit(0).start()
        elif step <= me.bits:
            vec_bit(step - 1).wait_recv()
            v_sum[step] = v_sum[step - 1] + v_got[step - 1]
            if step < me.bits:
                vec_bit(step).start()
            else:
                for s in range(1, n_tensor):
                    vec_z(s).start()
                v_all[me.z] = v_sum[me.bits]
        elif step == me.bits + 1:
            for s in range(1, n_tensor):
                src = lax.rem(me.z + s, n_tensor)
                remote(v_all.at[src], v_all.at[src], vz_send.at[0], vz_recv.at[src], me.across()).wait_recv()
            value = v_all[0]
            for s in range(1, n_tensor):
                value = value + v_all[s]
            v_sum[me.bits + 1] = value
            vec_last().start()
            vec_out[me.core] = value
        else:
            there = vec_out.at[1 - me.core]
            remote(there, there, vf_send.at[0], vf_recv.at[0], me.across()).wait_recv()

    def act_copy(n, s):
        place = lax.rem(me.z + s, n_tensor)
        return remote(
            act_in[n].at[place], act_out[n].at[me.slot], a_send.at[n, s - 1], a_recv.at[n, me.slot], (me.dp, place)
        )

    def start_acts(n):
        @pl.when(me.home)
        def _():
            for s in range(1, n_tensor):
                act_copy(n, s).start()
            local(act_in[n].at[me.z], act_out[n].at[me.slot], n_w + n).start()

    for j in range(n_w):
        local(g_in[j], acc[j], j).start()
    for n in range(n_acts):
        start_acts(n)
    phase = 0
    lag = me.bits + 2
    for tick in range(n_w + lag):
        for step in range(lag):
            j = tick - step
            if 0 <= j < n_w:
                if step == 0:
                    start_bits(j, 0)
                    local(g_in[j], acc[j], j).wait()
                elif step <= me.bits:
                    add_bits(j, step - 1)
                    if step < me.bits:
                        start_bits(j, step)
                    else:
                        start_z(j)
                else:
                    end_z(j)
        if phase < me.bits + 3:
            vec_phase(phase)
            phase += 1
    while phase < me.bits + 3:
        vec_phase(phase)
        phase += 1

    for j in range(n_w):
        for step in range(me.bits):
            for slot in range(2):
                send, count, _ = copies(j, step, slot)
                _each(count, lambda m: send(m).wait_send())
        for slot in range(2):
            target, copy = z_copy(j, slot)
            pl.when(target != me.z)(copy.wait_send)
        pl.when(me.home)(last_copy(j).wait_send)
        pl.when(jnp.logical_not(me.home))(last_copy(j).wait_recv)
    for step in range(me.bits):
        vec_bit(step).wait_send()
    for s in range(1, n_tensor):
        vec_z(s).wait_send()
    vec_last().wait_send()
    for n in range(n_acts):

        @pl.when(me.home)
        def _(n=n):
            for s in range(1, n_tensor):
                act_copy(n, s).wait_send()
            local(act_in[n].at[me.z], act_out[n].at[me.slot], n_w + n).wait()

        for slot in range(2):
            row = act_out[n].at[slot]
            copy = remote(row, row, a_send.at[n, 0], a_recv.at[n, slot], me.across())
            pl.when(me.core * half_z + slot != me.z)(copy.wait_recv)


def _base(bits, step):
    return sum(1 << (bits - 1 - s) for s in range(step))


def scatter(acts, vec, grads, kinds, sizes, cid):
    n_dp, n_tensor = sizes
    chips = n_dp // 2
    bits = chips.bit_length() - 1
    n_a, n_w = len(acts), len(grads)
    grads = [kind.cut(g) for kind, g in zip(kinds, grads)]
    shapes = [jax.ShapeDtypeStruct((n_tensor // 2,) + a.shape[1:], a.dtype) for a in acts]
    shapes += [jax.ShapeDtypeStruct((2,) + vec.shape, F32)]
    shapes += [jax.ShapeDtypeStruct(k.shard, F32) for k in kinds]
    dma = pltpu.SemaphoreType.DMA
    hbm = pl.BlockSpec(memory_space=pltpu.HBM)
    vmem = pl.BlockSpec(memory_space=pltpu.VMEM)
    most = max(chips // 2, 1)
    out = pl.pallas_call(
        functools.partial(scatter_kernel, kinds, n_a, sizes),
        out_shape=shapes,
        in_specs=[hbm] * n_a + [vmem] + [hbm] * n_w,
        out_specs=[hbm] * n_a + [vmem] + [vmem] * n_w,
        scratch_shapes=[pltpu.VMEM(k.whole, BF16) for k in kinds]
        + [pltpu.VMEM((chips - 1, 2) + k.two, BF16) for k in kinds]
        + [pltpu.VMEM((n_tensor - 1,) + k.two, BF16) for k in kinds]
        + [pltpu.VMEM(k.shard, F32) for k in kinds]
        + [
            pltpu.VMEM((bits + 2,) + vec.shape, F32),
            pltpu.VMEM((bits,) + vec.shape, F32),
            pltpu.VMEM((n_tensor,) + vec.shape, F32),
            dma((n_a, n_tensor)),
            dma((n_a, 2)),
            dma((n_w, bits, 2, most)),
            dma((n_w, bits, 2, most)),
            dma((n_w, 2)),
            dma((n_w, n_tensor)),
            dma((n_w,)),
            dma((n_w,)),
            dma((bits,)),
            dma((bits,)),
            dma((n_tensor,)),
            dma((n_tensor,)),
            dma((1,)),
            dma((1,)),
            dma((n_w + n_a,)),
        ],
        compiler_params=pltpu.CompilerParams(
            collective_id=cid, has_side_effects=True, vmem_limit_bytes=56 * 2**20
        ),
        name=f"scatter{cid}",
    )(*acts, vec, *grads)
    return out[:n_a], out[n_a], [k.leave(g) for k, g in zip(kinds, out[n_a + 1 :])]


KEYS = 1152
TILE = 352
COLS = 384


def _turn(x, cos, sin_up, sin_down):
    quarter = HEAD // 4
    return (
        x * cos
        + pltpu.roll(x, 2 * HEAD - quarter, 1) * sin_up
        + pltpu.roll(x, quarter, 1) * sin_down
    )


def attention_forward_kernel(
    x_ref, wq_ref, wk_ref, wv_ref, cos_ref, up_ref, down_ref, qb_ref, vb_ref, base_ref,
    qa_ref, ka_ref, va_ref, mix_ref,
):
    rows = x_ref.shape[0]
    tiles = rows // TILE
    lane = lax.broadcasted_iota(jnp.int32, (TILE, 2 * HEAD), 1)
    low = lane < HEAD
    one = jnp.where(lane == HEAD, 1.0, 0.0)
    ones = jnp.where((lane >= HEAD) & (lane < HEAD + 3), 1.0, 0.0)

    @pl.loop(0, tiles)
    def _(t):
        here = pl.ds(pl.multiple_of(t * TILE, TILE), TILE)
        x = x_ref[here, :]
        both = matmul(x, jnp.concatenate([wq_ref[...], wk_ref[...]], axis=1))
        tables = (cos_ref[here, :], up_ref[here, :], down_ref[here, :])
        query = _turn(both[:, : 2 * HEAD] + qb_ref[0], *tables) * (SCALE * LOG2E)
        key = _turn(both[:, 2 * HEAD :], *tables)
        value = matmul(x, wv_ref[...]) + vb_ref[0]
        base = base_ref[here, :].astype(F32)
        for h in range(2):
            if h:
                query, key, value = (pltpu.roll(v, HEAD, 1) for v in (query, key, value))
            qa_ref[h, here, :] = jnp.where(low, query, one).astype(BF16)
            ka_ref[h, here, :] = jnp.where(low, key, base).astype(BF16)
            va_ref[h, here, :] = jnp.where(low, value, ones).astype(BF16)

    rest = pl.ds(rows, KEYS - rows)
    for h in range(2):
        qa_ref[h, rest, :] = jnp.zeros((KEYS - rows, 2 * HEAD), BF16)
        va_ref[h, rest, :] = jnp.zeros((KEYS - rows, 2 * HEAD), BF16)
        ka_ref[h, rest, :] = base_ref[rest, :]

    @pl.loop(0, tiles)
    def _(t):
        here = pl.ds(pl.multiple_of(t * TILE, TILE), TILE)
        outs = []
        for h in range(2):
            q = qa_ref[h, here, :]
            s = matmul_right_t(q, ka_ref[h])
            top = jnp.max(s, axis=1, keepdims=True)
            p = jnp.exp2(s - top).astype(BF16)
            o = matmul(p, va_ref[h])
            total = o[:, HEAD : HEAD + 1]
            outs.append(o / total)
            log = -(top + jnp.log2(total))
            first = log.astype(BF16)
            left = log - first.astype(F32)
            second = left.astype(BF16)
            third = (left - second.astype(F32)).astype(BF16)
            logs = jnp.where(
                lane == HEAD + 1,
                first.astype(F32),
                jnp.where(lane == HEAD + 2, second.astype(F32), third.astype(F32)),
            )
            inside = (lane > HEAD) & (lane <= HEAD + 3)
            qa_ref[h, here, :] = jnp.where(inside, logs, q.astype(F32)).astype(BF16)
        mix_ref[here, :] = jnp.where(low, outs[0], pltpu.roll(outs[1], HEAD, 1)).astype(BF16)


def attention_forward(x, w, tables, query_bias, value_bias, base):
    rows, width = x.shape
    pairs = query_bias.shape[0]
    sub = pairs // 2
    lanes = 2 * HEAD

    def column(part):
        return pl.BlockSpec((width, lanes), lambda g: (0, (g // sub) * (3 * sub) + part * sub + g % sub))

    def whole(shape):
        return pl.BlockSpec(shape, lambda g: (0,) * len(shape))

    bias = pl.BlockSpec((1, 1, lanes), lambda g: (g, 0, 0))
    heads = pl.BlockSpec((2, KEYS, lanes), lambda g: (g, 0, 0))
    return pl.pallas_call(
        attention_forward_kernel,
        grid=(pairs,),
        out_shape=[jax.ShapeDtypeStruct((2 * pairs, KEYS, lanes), BF16)] * 3
        + [jax.ShapeDtypeStruct((rows, pairs * lanes), BF16)],
        in_specs=[whole((rows, width)), column(0), column(1), column(2)]
        + [whole((rows, lanes))] * 3
        + [bias, bias, whole((KEYS, lanes))],
        out_specs=[heads, heads, heads, pl.BlockSpec((rows, lanes), lambda g: (0, g))],
        compiler_params=pltpu.CompilerParams(vmem_limit_bytes=48 * 2**20),
        name="attention_forward",
    )(x, w, w, w, *tables, query_bias, value_bias, base)


def attention_backward_kernel(
    sub, qa_ref, ka_ref, va_ref, do_ref, mix_ref, cos_ref, up_ref, down_ref,
    out_ref, sum_ref, da_ref, dq_ref, dk_ref, dv_ref,
):
    rows = do_ref.shape[0]
    lanes = 2 * HEAD
    tiles = rows // TILE
    lane = lax.broadcasted_iota(jnp.int32, (TILE, lanes), 1)
    low = lane < HEAD
    g = pl.program_id(0)

    da_ref[pl.ds(rows, KEYS - rows), :] = jnp.zeros((KEYS - rows, lanes), BF16)
    for h in range(2):

        @pl.loop(0, tiles)
        def _(t, h=h):
            here = pl.ds(pl.multiple_of(t * TILE, TILE), TILE)
            d = do_ref[here, :].astype(F32)
            mine = low if h == 0 else jnp.logical_not(low)
            delta = -jnp.sum(jnp.where(mine, d * mix_ref[here, :].astype(F32), 0.0), axis=1, keepdims=True)
            if h:
                d = pltpu.roll(d, HEAD, 1)
            first = delta.astype(BF16)
            left = delta - first.astype(F32)
            second = left.astype(BF16)
            third = (left - second.astype(F32)).astype(BF16)
            logs = jnp.where(
                lane == HEAD,
                first.astype(F32),
                jnp.where(lane == HEAD + 1, second.astype(F32), third.astype(F32)),
            )
            da_ref[here, :] = jnp.where(low, d, jnp.where(lane < HEAD + 3, logs, 0.0)).astype(BF16)

        dk_ref[h] = jnp.zeros((KEYS, lanes), F32)
        dv_ref[h] = jnp.zeros((KEYS, lanes), F32)

        @pl.loop(0, KEYS // COLS)
        def _(t, h=h):
            here = pl.ds(pl.multiple_of(t * COLS, COLS), COLS)
            q = qa_ref[h, here, :]
            d = da_ref[here, :]
            p = jnp.exp2(matmul_right_t(ka_ref[h], q))
            ds = (p * matmul_right_t(va_ref[h], d)).astype(BF16)
            dv_ref[h] += matmul(p.astype(BF16), d)
            dk_ref[h] += matmul(ds, q)
            dq_ref[h, here, :] = matmul_left_t(ds, ka_ref[h])

    def put(column, row, ref, factor, turn):
        total = jnp.zeros((1, lanes), F32)
        for t in range(tiles):
            here = pl.ds(t * TILE, TILE)
            value = jnp.where(low, ref[0, here, :], pltpu.roll(ref[1, here, :], HEAD, 1))
            if factor is not None:
                value = value * factor
            if turn:
                value = _turn(value, cos_ref[here, :], -up_ref[here, :], -down_ref[here, :])
            if row is not None:
                total = total + jnp.sum(value, axis=0, keepdims=True)
            at = pl.multiple_of(column * (sub * lanes) + lax.rem(g, sub) * lanes, lanes)
            out_ref[here, pl.ds(at, lanes)] = value.astype(BF16)
        if row is not None:
            sum_ref[0, pl.ds(row, 1), :] = total

    put(0, 0, dq_ref, SCALE, True)
    put(1, None, dk_ref, LN2, True)
    put(2, 1, dv_ref, None, False)


def attention_backward(qa, ka, va, d_mixed, mixed, tables):
    rows = mixed.shape[0]
    lanes = 2 * HEAD
    pairs = mixed.shape[1] // lanes
    sub = pairs // 2
    heads = pl.BlockSpec((2, KEYS, lanes), lambda g: (g, 0, 0))
    pair = pl.BlockSpec((rows, lanes), lambda g: (0, g))
    return pl.pallas_call(
        functools.partial(attention_backward_kernel, sub),
        grid=(pairs,),
        out_shape=[
            jax.ShapeDtypeStruct((rows, 3 * pairs * lanes), BF16),
            jax.ShapeDtypeStruct((pairs, 8, lanes), F32),
        ],
        in_specs=[heads, heads, heads, pair, pair]
        + [pl.BlockSpec((rows, lanes), lambda g: (0, 0))] * 3,
        out_specs=[
            pl.BlockSpec((rows, 3 * sub * lanes), lambda g: (0, g // sub)),
            pl.BlockSpec((1, 8, lanes), lambda g: (g, 0, 0)),
        ],
        scratch_shapes=[
            pltpu.VMEM((KEYS, lanes), BF16),
            pltpu.VMEM((2, KEYS, lanes), F32),
            pltpu.VMEM((2, KEYS, lanes), F32),
            pltpu.VMEM((2, KEYS, lanes), F32),
        ],
        compiler_params=pltpu.CompilerParams(vmem_limit_bytes=48 * 2**20),
        name="attention_backward",
    )(qa, ka, va, d_mixed, mixed, *tables)


def shards(
    tokens_in, cotangent, image_flag, key_mask, column_mask,
    attention_norm_gain, attention_norm_bias, w_query, w_key, w_value, query_bias, value_bias, w_out, out_bias,
    feedforward_norm_gain, feedforward_norm_bias, w_gate, gate_bias, w_up, up_bias, inner_gain, inner_shift,
    w_down, down_bias,
):
    n_dp, n_tensor = lax.axis_size("dp"), lax.axis_size("tensor")
    sizes = (n_dp, n_tensor)
    dp, z = lax.axis_index("dp"), lax.axis_index("tensor")
    core = dp % 2
    block = tokens_in.shape[1]
    width = tokens_in.shape[2]
    length = block * n_tensor
    block_pad = up_to(block, 8)
    rows = block_pad * n_tensor
    n_head = w_query.shape[1]
    n_ff = w_gate.shape[1]
    ff = up_to(n_ff, 16)
    count_live = float(FF - PADCOLS)
    swap = [(i, (i // n_tensor ^ 1) * n_tensor + i % n_tensor) for i in range(n_dp * n_tensor)]

    def other(value):
        return lax.ppermute(value, ("dp", "tensor"), swap)

    shard_qkv = jnp.concatenate([w_query, w_key, w_value], axis=1)
    kind_qkv = Kind(True, shard_qkv.shape, n_dp)
    kind_o = Kind(False, w_out.shape, n_dp)
    kind_f = Kind(False, (ff, w_down.shape[1]), n_dp)

    def pad_ff(vec):
        return jnp.pad(vec, (0, ff - n_ff))

    small = jnp.concatenate(
        [query_bias, value_bias]
        + [pad_ff(v) for v in (gate_bias, up_bias, inner_gain, inner_shift, column_mask.astype(F32))]
    )
    small_rows = up_to(up_to(small.shape[0], LANES) // LANES, 8)
    small = jnp.pad(small, (0, small_rows * LANES - small.shape[0])).reshape(small_rows, LANES)
    own_image = z % (n_tensor // 2)
    pair = jnp.concatenate(
        [
            lax.dynamic_index_in_dim(key_mask, own_image, 0, False).astype(F32),
            lax.dynamic_index_in_dim(image_flag, own_image, 0, True).astype(F32),
        ]
    )
    pair_rows = up_to(up_to(length + 1, LANES) // LANES, 8)
    pair = jnp.pad(pair, (0, pair_rows * LANES - pair.shape[0])).reshape(pair_rows, LANES)

    (image,), (packs,), (mask_flag,), (full_qkv,) = gather(
        [tokens_in], [small], [pair], [shard_qkv], [kind_qkv], sizes, 0
    )

    def turned(weight):
        return jnp.pad(weight.T, ((0, ff - n_ff), (0, 0)))

    (cot,), _, _, (full_g, full_u, full_o, full_d) = gather(
        [cotangent],
        [],
        [],
        [turned(w_gate), turned(w_up), w_out, jnp.pad(w_down, ((0, ff - n_ff), (0, 0)))],
        [kind_f, kind_f, kind_o, kind_f],
        sizes,
        1,
    )

    packs = packs.reshape(2, -1)
    cuts = [n_head] * 2 + [ff] * 5
    parts, at = [], 0
    for size in cuts:
        parts.append(packs[:, at : at + size].reshape(-1))
        at += size
    q_bias, v_bias, g_bias, u_bias, gain, shift, columns = parts
    mask_flag = mask_flag.reshape(-1)
    flag = mask_flag[length]

    def padded(value):
        return jnp.pad(value, ((0, 0), (0, block_pad - block), (0, 0))).reshape(rows, -1)

    def unpadded(value):
        return value.reshape(n_tensor, block_pad, width)[:, :block]

    live = padded(mask_flag[:length].reshape(n_tensor, block, 1)).reshape(rows)
    live = jnp.pad(live, (0, KEYS - rows))
    lane = jnp.arange(LANES)[None, :]
    base = jnp.where(
        lane == HEAD,
        jnp.where(live > 0, 0.0, -1e30)[:, None],
        jnp.where((lane > HEAD) & (lane <= HEAD + 3), 1.0, 0.0),
    ).astype(BF16)
    tables = lane_tables(length, HEAD // 4, block, block_pad)

    token_rows = padded(image).astype(F32)
    xhat1, s1 = norm_pieces(token_rows)
    normed = (xhat1 * attention_norm_gain + attention_norm_bias).astype(BF16)
    pairs = 2 * n_head // (2 * HEAD)
    qa, ka, va, mixed = attention_forward(
        normed, full_qkv, tables, q_bias.reshape(pairs, 1, 2 * HEAD), v_bias.reshape(pairs, 1, 2 * HEAD), base
    )
    part = matmul(mixed, full_o).astype(BF16)
    middle = token_rows + (part.astype(F32) + other(part).astype(F32)) + out_bias
    xhat2, s2 = norm_pieces(middle)
    normed2 = (xhat2 * feedforward_norm_gain + feedforward_norm_bias).astype(BF16)
    gate = matmul_right_t(normed2, full_g) + g_bias
    up = matmul_right_t(normed2, full_u) + u_bias
    sig = jax.nn.sigmoid(gate)
    act = gate * sig * up
    sums = jnp.stack([jnp.sum(act * columns, axis=-1), jnp.sum(act * act * columns, axis=-1)])
    sums = sums + other(sums)
    mean = sums[0][:, None] / count_live
    var = sums[1][:, None] / count_live - mean * mean
    r = lax.rsqrt(var + EPS)
    nhat = (act - mean) * r
    hidden = (columns * (nhat * gain + shift)).astype(BF16)
    part = matmul(hidden, full_d).astype(BF16)
    output = (middle + (part.astype(F32) + other(part).astype(F32)) + down_bias).astype(BF16)

    grad = padded(cot).astype(F32) * flag
    grad_low = grad.astype(BF16)
    g_down = matmul_left_t(hidden, grad_low).astype(BF16)
    dn = columns * lax.dot_general(
        grad_low, full_d, (((1,), (1,)), ((), ())), preferred_element_type=F32
    )
    g_gain = jnp.sum(dn * nhat, axis=0)
    g_shift = jnp.sum(dn, axis=0)
    dnh = dn * gain
    back = jnp.stack([jnp.sum(dnh, axis=-1), jnp.sum(dnh * nhat, axis=-1)])
    back = back + other(back)
    dact = r * (dnh - columns * (back[0][:, None] + nhat * back[1][:, None]) / count_live)
    dgate = dact * up * sig * (1.0 + gate * (1.0 - sig))
    dup = dact * gate * sig
    g_gate_bias = jnp.sum(dgate, axis=0)
    g_up_bias = jnp.sum(dup, axis=0)
    gate_low = dgate.astype(BF16)
    up_low = dup.astype(BF16)
    g_gate = matmul_left_t(gate_low, normed2).astype(BF16)
    g_up = matmul_left_t(up_low, normed2).astype(BF16)
    part = (matmul(gate_low, full_g) + matmul(up_low, full_u)).astype(BF16)
    dnormed2 = part.astype(F32) + other(part).astype(F32)
    g_mlp_gain = jnp.sum(dnormed2 * xhat2, axis=0)
    g_mlp_shift = jnp.sum(dnormed2, axis=0)
    dmiddle = grad + norm_backward(dnormed2, xhat2, s2, feedforward_norm_gain)
    g_out_bias = jnp.sum(dmiddle, axis=0)
    g_down_bias = jnp.sum(grad, axis=0)
    dmid_low = dmiddle.astype(BF16)
    g_out = matmul_left_t(mixed, dmid_low).astype(BF16)
    d_mixed = matmul_right_t(dmid_low, full_o).astype(BF16)
    d_qkv, qv_sums = attention_backward(qa, ka, va, d_mixed, mixed, tables)
    g_qkv = matmul_left_t(normed, d_qkv).astype(BF16)
    part = matmul_right_t(d_qkv, full_qkv).astype(BF16)
    dnormed = part.astype(F32) + other(part).astype(F32)
    g_attn_gain = jnp.sum(dnormed * xhat1, axis=0)
    g_attn_shift = jnp.sum(dnormed, axis=0)
    input_grad = dmiddle + norm_backward(dnormed, xhat1, s1, attention_norm_gain)

    def by_slot(vec):
        return vec.reshape(2, -1)

    vec = jnp.concatenate(
        [g_attn_gain, g_attn_shift, g_out_bias, g_mlp_gain, g_mlp_shift, g_down_bias]
        + [
            jnp.concatenate(
                [by_slot(v) for v in (qv_sums[:, 0], qv_sums[:, 1], g_gate_bias, g_up_bias, g_gain, g_shift)], axis=1
            ).reshape(-1)
        ]
    )
    vec_size = vec.shape[0]
    vec_rows = up_to(up_to(vec_size, LANES) // LANES, 8)
    vec = jnp.pad(vec, (0, vec_rows * LANES - vec_size)).reshape(vec_rows, LANES)
    (out_rows, in_rows), vec, (s_down, s_gate, s_up, s_out, s_qkv) = scatter(
        [unpadded(output), unpadded(input_grad.astype(BF16))],
        vec,
        [g_down, g_gate, g_up, g_out, g_qkv],
        [kind_f, kind_f, kind_f, kind_o, kind_qkv],
        sizes,
        2,
    )
    vec = vec.reshape(2, -1)
    wide = vec[0, : 6 * width].reshape(6, width)
    owner = z // (n_tensor // 2)
    tall = lax.dynamic_index_in_dim(vec, owner, 0, False)[6 * width : vec_size].reshape(2, -1)
    tall = lax.dynamic_index_in_dim(tall, z % (n_tensor // 2), 0, False)
    pieces, at = [], 0
    for size in [n_head] * 2 + [ff] * 4:
        pieces.append(tall[at : at + size])
        at += size
    return (
        out_rows,
        in_rows.astype(F32),
        wide[0],
        wide[1],
        s_qkv[:, :n_head],
        s_qkv[:, n_head : 2 * n_head],
        s_qkv[:, 2 * n_head :],
        pieces[0],
        pieces[1],
        s_out,
        wide[2],
        wide[3],
        wide[4],
        s_gate[:n_ff].T,
        pieces[2][:n_ff],
        s_up[:n_ff].T,
        pieces[3][:n_ff],
        pieces[4][:n_ff],
        pieces[5][:n_ff],
        s_down[:n_ff],
        wide[5],
    )


def solution(mesh):
    act, row, col, vec = P("dp", "tensor", None), P("dp", "tensor"), P("tensor", "dp"), P("tensor")
    in_specs = (
        act, act, P("dp"), P("dp", None), vec, P(), P(), row, row, row, vec, vec, col, P(), P(), P(),
        row, vec, row, vec, vec, vec, col, P(),
    )
    out_specs = (
        act, act, P(), P(), row, row, row, vec, vec, col, P(), P(), P(), row, vec, row, vec, vec, vec, col, P(),
    )
    return jax.shard_map(shards, mesh=mesh, in_specs=in_specs, out_specs=out_specs, check_vma=False)
```

```python
import functools
import math

import jax
import jax.numpy as jnp
from jax import lax
from jax.experimental import pallas as pl
from jax.experimental.pallas import tpu as pltpu
from jax.sharding import PartitionSpec as P

HEAD = 64
FF = 2736
PADCOLS = 6
GRID = 32
EPS = 1e-06
ROPE_BASE = 10000.0
LANES = 128
MESH = pl.DeviceIdType.MESH
LOG2E = math.log2(math.e)
LN2 = math.log(2.0)
SCALE = HEAD ** (-0.5)
F32 = jnp.float32
BF16 = jnp.bfloat16


def up_to(size, unit):
    return -(-size // unit) * unit


def rotary_tables(length, head):
    quarter = head // 4
    place = jnp.arange(length, dtype=jnp.int32)
    inside = (place >= 1) & (place <= GRID * GRID)
    cell = jnp.maximum(place - 1, 0)
    row_pos = jnp.where(inside, cell // GRID, 0).astype(F32)
    col_pos = jnp.where(inside, cell % GRID, 0).astype(F32)
    freq = ROPE_BASE ** (-jnp.arange(quarter, dtype=F32) / quarter)
    angle = jnp.concatenate(
        [row_pos[:, None] * freq[None, :], col_pos[:, None] * freq[None, :]], axis=1
    )
    return jnp.cos(angle), jnp.sin(angle)


def lane_tables(length, quarter, block, rows_padded):
    cosv, sinv = rotary_tables(length, HEAD)

    def lay(first, second):
        one = jnp.concatenate(
            [first[:, :quarter], second[:, :quarter], first[:, quarter:], second[:, quarter:]], axis=1
        )
        two = jnp.concatenate([one, one], axis=1)
        cut = two.reshape(length // block, block, 2 * HEAD)
        return jnp.pad(cut, ((0, 0), (0, rows_padded - block), (0, 0))).reshape(-1, 2 * HEAD)

    zero = jnp.zeros_like(sinv)
    return lay(cosv, cosv), lay(-sinv, zero), lay(zero, sinv)


def norm_pieces(values):
    row_mean = jnp.mean(values, axis=-1, keepdims=True)
    var = jnp.mean(jnp.square(values - row_mean), axis=-1, keepdims=True)
    inverse_scale = lax.rsqrt(var + EPS)
    return ((values - row_mean) * inverse_scale, inverse_scale)


def norm_backward(incoming_gradient, centered_normalized, inverse_scale, norm_gain):
    inner = incoming_gradient * norm_gain
    return inverse_scale * (
        inner
        - jnp.mean(inner, axis=-1, keepdims=True)
        - centered_normalized * jnp.mean(inner * centered_normalized, axis=-1, keepdims=True)
    )


def matmul(left, right):
    return jnp.dot(left, right, preferred_element_type=F32)


def matmul_right_t(left, right):
    return lax.dot_general(left, right, (((1,), (1,)), ((), ())), preferred_element_type=F32)


def matmul_left_t(left, right):
    return lax.dot_general(left, right, (((0,), (0,)), ((), ())), preferred_element_type=F32)


class Kind:
    def __init__(self, by_rows, shard, n_dp):
        self.given = shard
        self.n_dp = n_dp
        self.turn = not by_rows and shard[1] % LANES != 0
        if self.turn:
            shard = (shard[1], up_to(shard[0], LANES))
        self.by_rows = by_rows or self.turn
        self.shard = shard
        a, b = shard
        if self.by_rows:
            self.whole, self.two = (n_dp * a, 2 * b), (2 * a, b)
        else:
            self.whole, self.two = (2 * a, n_dp * b), (a, 2 * b)

    def piece(self, ref, slot, chip):
        a, b = self.shard
        if self.by_rows:
            return ref.at[pl.ds(_mult(chip, 2 * a), 2 * a), pl.ds(_mult(slot, b), b)]
        return ref.at[pl.ds(_mult(slot, a), a), pl.ds(_mult(chip, 2 * b), 2 * b)]

    def half(self, two, core):
        a, b = self.shard
        if self.by_rows:
            return two.at[pl.ds(_mult(core, a), a)]
        return two.at[:, pl.ds(_mult(core, b), b)]

    def one(self, ref, slot, chip, core):
        a, b = self.shard
        if self.by_rows:
            return ref.at[pl.ds(_mult(chip * 2 + core, a), a), pl.ds(_mult(slot, b), b)]
        return ref.at[pl.ds(_mult(slot, a), a), pl.ds(_mult(chip * 2 + core, b), b)]

    def enter(self, shard):
        if not self.turn:
            return shard
        return jnp.pad(shard.T, ((0, 0), (0, self.shard[1] - self.given[0])))

    def leave(self, shard):
        return shard[:, : self.given[0]].T if self.turn else shard

    def join(self, whole):
        if not self.turn:
            return whole
        a, b = self.shard
        whole = whole.reshape(self.n_dp * a, 2, b)[:, :, : self.given[0]]
        return whole.transpose(1, 2, 0).reshape(2 * self.given[0], self.n_dp * a)

    def cut(self, whole):
        if not self.turn:
            return whole
        a, b = self.shard
        whole = whole.reshape(2, self.given[0], self.n_dp * a).transpose(2, 0, 1)
        return jnp.pad(whole, ((0, 0), (0, 0), (0, b - self.given[0]))).reshape(self.whole)


def _mult(index, size):
    return index * size if isinstance(index, int) else pl.multiple_of(index * size, size)


class Place:
    def __init__(self, n_dp, n_tensor):
        self.dp = lax.axis_index("dp")
        self.z = lax.axis_index("tensor")
        self.core = lax.rem(self.dp, 2)
        self.chip = lax.div(self.dp, 2)
        self.nz = n_tensor
        self.chips = n_dp // 2
        self.bits = self.chips.bit_length() - 1
        self.home = self.core == lax.div(self.z, n_tensor // 2)
        self.slot = lax.rem(self.z, n_tensor // 2)

    def flip(self, bit):
        low = lax.rem(lax.div(self.chip, 1 << bit), 2)
        return self.chip + (1 - 2 * low) * (1 << bit)

    def across(self):
        return (self.dp + 1 - 2 * self.core, self.z)

    def beside(self, bit):
        return (self.flip(bit) * 2 + self.core, self.z)

    def shifted(self, by):
        return (self.dp, lax.rem(self.z + by, self.nz))

    def barrier(self):
        everyone = [self.across()]
        everyone += [self.shifted(s) for s in range(1, self.nz)]
        everyone += [self.beside(b) for b in range(self.bits)]
        bar = pltpu.get_barrier_semaphore()
        for one in everyone:
            pl.semaphore_signal(bar, inc=1, device_id=one, device_id_type=MESH)
        pl.semaphore_wait(bar, len(everyone))


def remote(src, dst, send, recv, to):
    return pltpu.make_async_remote_copy(
        src_ref=src, dst_ref=dst, send_sem=send, recv_sem=recv, device_id=to, device_id_type=MESH
    )


def flipped(chip, value):
    return lax.bitwise_xor(chip, value)


class Gather:
    def __init__(self, me, kinds, w_in, w_out, sems):
        self.me, self.kinds, self.w_in, self.w_out = me, kinds, w_in, w_out
        self.s_send, self.s_recv, self.z_send, self.z_recv, self.b_send, self.b_recv, self.loc = sems

    @staticmethod
    def semaphores(n_w, sizes):
        dma = pltpu.SemaphoreType.DMA
        bits = (sizes[0] // 2).bit_length() - 1
        most = max(1 << max(bits - 1, 0), 1)
        return [
            dma((n_w,)),
            dma((n_w,)),
            dma((n_w, sizes[1])),
            dma((n_w, 2)),
            dma((n_w, bits, 2, most)),
            dma((n_w, bits, 2, most)),
            dma((n_w,)),
        ]

    def _hop(self, j):
        me = self.me
        mine = self.kinds[j].one(self.w_out[j], me.slot, me.chip, me.core)
        return (
            pltpu.make_async_copy(self.w_in[j], mine, self.loc.at[j]),
            remote(self.w_in[j], mine, self.s_send.at[j], self.s_recv.at[j], me.across()),
        )

    def first_hop(self, j):
        stay, leave = self._hop(j)
        pl.when(self.me.home)(stay.start)
        pl.when(jnp.logical_not(self.me.home))(leave.start)

    def _along(self, j, s):
        me = self.me
        src = self.kinds[j].piece(self.w_out[j], me.slot, me.chip)
        return remote(src, src, self.z_send.at[j, s - 1], self.z_recv.at[j, me.slot], me.shifted(s))

    def start_z(self, j):
        @pl.when(self.me.home)
        def _():
            stay, leave = self._hop(j)
            stay.wait()
            leave.wait_recv()
            for s in range(1, self.me.nz):
                self._along(j, s).start()

    def wait_z(self, j):
        me = self.me
        for slot in range(2):
            src = self.kinds[j].piece(self.w_out[j], slot, me.chip)
            copy = remote(src, src, self.z_send.at[j, 0], self.z_recv.at[j, slot], me.across())
            pl.when(me.core * (me.nz // 2) + slot != me.z)(copy.wait_recv)

    def _bits(self, j, step, slot):
        me = self.me
        bit = step if slot == 0 else me.bits - 1 - step
        low = 1 if slot == 0 else 1 << (me.bits - step)

        def send(m):
            src = self.kinds[j].piece(self.w_out[j], slot, flipped(me.chip, m * low))
            return remote(
                src, src, self.b_send.at[j, step, slot, m], self.b_recv.at[j, step, slot, m], me.beside(bit)
            )

        return send

    def start_bits(self, j, step):
        for slot in range(2):
            send = self._bits(j, step, slot)
            _each(1 << step, lambda m: send(m).start())

    def wait_bits(self, j, step):
        for slot in range(2):
            send = self._bits(j, step, slot)
            _each(1 << step, lambda m: send(m).wait_recv())

    def finish(self, j):
        me = self.me
        pl.when(jnp.logical_not(me.home))(self._hop(j)[1].wait_send)
        for s in range(1, me.nz):
            pl.when(me.home)(self._along(j, s).wait_send)
        for step in range(me.bits):
            for slot in range(2):
                send = self._bits(j, step, slot)
                _each(1 << step, lambda m: send(m).wait_send())


class Inward:
    def __init__(self, me, src, dst, sems):
        self.me, self.src, self.dst = me, src, dst
        self.send, self.recv, self.fwd, self.back, self.loc = sems

    @staticmethod
    def semaphores(sizes):
        dma = pltpu.SemaphoreType.DMA
        return [dma((sizes[1],)), dma((sizes[1],)), dma((sizes[1],)), dma((sizes[1],)), dma((1,))]

    def _copy(self, i):
        me = self.me
        target = me.nz // 2 * me.core + i
        return target, remote(
            self.src.at[i], self.dst.at[me.z], self.send.at[i], self.recv.at[me.z], (me.dp, target)
        )

    def _stay(self, i):
        return pltpu.make_async_copy(self.src.at[i], self.dst.at[self.me.z], self.loc.at[0])

    def _onward(self, place):
        slab = self.dst.at[place]
        return remote(slab, slab, self.fwd.at[place], self.back.at[place], self.me.across())

    def start(self):
        for i in range(self.me.nz // 2):
            target, copy = self._copy(i)
            pl.when(target != self.me.z)(copy.start)
            pl.when(target == self.me.z)(self._stay(i).start)

    def pass_on(self):
        me = self.me

        @pl.when(me.home)
        def _():
            for s in range(me.nz):
                place = lax.rem(me.z + s, me.nz)
                if s == 0:
                    self._stay(0).wait()
                else:
                    slab = self.dst.at[place]
                    remote(slab, slab, self.send.at[0], self.recv.at[place], me.across()).wait_recv()
                self._onward(place).start()

    def ready(self):
        for place in range(self.me.nz):
            pl.when(jnp.logical_not(self.me.home))(self._onward(place).wait_recv)

    def finish(self):
        for i in range(self.me.nz // 2):
            target, copy = self._copy(i)
            pl.when(target != self.me.z)(copy.wait_send)
        for place in range(self.me.nz):
            pl.when(self.me.home)(self._onward(place).wait_send)


class Packs:
    def __init__(self, me, src, dst, pair_src, pair_dst, sems):
        self.me, self.src, self.dst, self.pair_src, self.pair_dst = me, src, dst, pair_src, pair_dst
        self.send, self.recv, self.loc = sems

    @staticmethod
    def semaphores(sizes):
        dma = pltpu.SemaphoreType.DMA
        return [dma((sizes[1],)), dma((3,)), dma((2,))]

    def _copy(self, s):
        me = self.me
        return remote(self.src, self.dst.at[me.slot], self.send.at[s], self.recv.at[me.slot], me.shifted(s))

    def _stay(self):
        return pltpu.make_async_copy(self.src, self.dst.at[self.me.slot], self.loc.at[0])

    def _pair(self):
        return (
            pltpu.make_async_copy(self.pair_src, self.pair_dst, self.loc.at[1]),
            remote(self.pair_src, self.pair_dst, self.send.at[0], self.recv.at[2], self.me.across()),
        )

    def start(self):
        @pl.when(self.me.home)
        def _():
            self._stay().start()
            for s in range(1, self.me.nz):
                self._copy(s).start()
            stay, there = self._pair()
            stay.start()
            there.start()

    def ready(self):
        me = self.me
        for slot in range(2):
            row = self.dst.at[slot]
            copy = remote(row, row, self.send.at[0], self.recv.at[slot], me.across())
            pl.when(me.core * (me.nz // 2) + slot != me.z)(copy.wait_recv)
        stay, there = self._pair()

        @pl.when(me.home)
        def _():
            self._stay().wait()
            stay.wait()

        pl.when(jnp.logical_not(me.home))(there.wait_recv)

    def finish(self):
        @pl.when(self.me.home)
        def _():
            for s in range(1, self.me.nz):
                self._copy(s).wait_send()
            self._pair()[1].wait_send()


def _each(count, act):
    if count <= 4:
        for m in range(count):
            act(m)
    else:

        @pl.loop(0, count)
        def _(m):
            act(m)


def scatter_kernel(kinds, n_acts, sizes, *refs):
    n_dp, n_tensor = sizes
    n_w = len(kinds)
    me = Place(n_dp, n_tensor)
    half_z = n_tensor // 2
    act_in, vec_in, g_in = refs[:n_acts], refs[n_acts], refs[n_acts + 1 : n_acts + 1 + n_w]
    at = n_acts + 1 + n_w
    act_out, vec_out, g_out = refs[at : at + n_acts], refs[at + n_acts], refs[at + n_acts + 1 : at + n_acts + 1 + n_w]
    at += n_acts + 1 + n_w
    acc, got, gotz, stage = (refs[at + i * n_w : at + (i + 1) * n_w] for i in range(4))
    at += 4 * n_w
    (v_sum, v_got, v_all) = refs[at : at + 3]
    (a_send, a_recv, b_send, b_recv, z_send, z_recv, f_send, f_recv, vb_send, vb_recv, vz_send, vz_recv, vf_send, vf_recv, loc) = refs[at + 3 :]
    me.barrier()

    def local(src, dst, n):
        return pltpu.make_async_copy(src, dst, loc.at[n])

    def order(step, slot):
        if slot == 0:
            return me.bits - 1 - step, 1, 1 << (me.bits - 1 - step)
        return step, 1 << (step + 1), 1 << (me.bits - 1 - step)

    def copies(j, step, slot):
        bit, stride, count = order(step, slot)
        source = g_in[j] if step == 0 else acc[j]

        def send(m):
            src = kinds[j].piece(source, slot, flipped(me.chip, m * stride + (1 << bit)))
            dst = got[j].at[_base(me.bits, step) + m, slot]
            return remote(src, dst, b_send.at[j, step, slot, m], b_recv.at[j, step, slot, m], me.beside(bit))

        return send, count, stride

    def start_bits(j, step):
        for slot in range(2):
            send, count, _ = copies(j, step, slot)
            _each(count, lambda m: send(m).start())

    def add_bits(j, step):
        for slot in range(2):
            send, count, stride = copies(j, step, slot)

            def one(m):
                send(m).wait_recv()
                here = kinds[j].piece(acc[j], slot, flipped(me.chip, m * stride))
                here[...] = (
                    here[...].astype(F32) + got[j][_base(me.bits, step) + m, slot].astype(F32)
                ).astype(BF16)

            _each(count, one)

    def z_copy(j, slot):
        target = half_z * me.core + slot
        index = lax.rem(me.z - target + n_tensor - 1, n_tensor)
        src = kinds[j].piece(acc[j], slot, me.chip)
        return target, remote(src, gotz[j].at[index], z_send.at[j, slot], z_recv.at[j, index], (me.dp, target))

    def start_z(j):
        for slot in range(2):
            target, copy = z_copy(j, slot)
            pl.when(target != me.z)(copy.start)

    def last_copy(j):
        return remote(stage[j], g_out[j], f_send.at[j], f_recv.at[j], me.across())

    def end_z(j):
        @pl.when(me.home)
        def _():
            for index in range(n_tensor - 1):
                slab = gotz[j].at[index]
                remote(slab, slab, z_send.at[j, 0], z_recv.at[j, index], me.across()).wait_recv()

            def total(core):
                value = kinds[j].one(acc[j], me.slot, me.chip, core)[...].astype(F32)
                for index in range(n_tensor - 1):
                    value = value + kinds[j].half(gotz[j].at[index], core)[...].astype(F32)
                return value

            stage[j][...] = total(1 - me.core)
            last_copy(j).start()
            g_out[j][...] = total(me.core)

    def vec_bit(step):
        return remote(v_sum.at[step], v_got.at[step], vb_send.at[step], vb_recv.at[step], me.beside(step))

    def vec_z(s):
        return remote(v_sum.at[me.bits], v_all.at[me.z], vz_send.at[s - 1], vz_recv.at[me.z], me.shifted(s))

    def vec_last():
        return remote(v_sum.at[me.bits + 1], vec_out.at[me.core], vf_send.at[0], vf_recv.at[0], me.across())

    def vec_phase(step):
        if step == 0:
            v_sum[0] = vec_in[...]
            vec_bit(0).start()
        elif step <= me.bits:
            vec_bit(step - 1).wait_recv()
            v_sum[step] = v_sum[step - 1] + v_got[step - 1]
            if step < me.bits:
                vec_bit(step).start()
            else:
                for s in range(1, n_tensor):
                    vec_z(s).start()
                v_all[me.z] = v_sum[me.bits]
        elif step == me.bits + 1:
            for s in range(1, n_tensor):
                src = lax.rem(me.z + s, n_tensor)
                remote(v_all.at[src], v_all.at[src], vz_send.at[0], vz_recv.at[src], me.across()).wait_recv()
            value = v_all[0]
            for s in range(1, n_tensor):
                value = value + v_all[s]
            v_sum[me.bits + 1] = value
            vec_last().start()
            vec_out[me.core] = value
        else:
            there = vec_out.at[1 - me.core]
            remote(there, there, vf_send.at[0], vf_recv.at[0], me.across()).wait_recv()

    def act_copy(n, s):
        place = lax.rem(me.z + s, n_tensor)
        return remote(
            act_in[n].at[place], act_out[n].at[me.slot], a_send.at[n, s - 1], a_recv.at[n, me.slot], (me.dp, place)
        )

    def start_acts(n):
        @pl.when(me.home)
        def _():
            for s in range(1, n_tensor):
                act_copy(n, s).start()
            local(act_in[n].at[me.z], act_out[n].at[me.slot], n_w + n).start()

    for j in range(n_w):
        local(g_in[j], acc[j], j).start()
    for n in range(n_acts):
        start_acts(n)
    phase = 0
    lag = me.bits + 2
    for tick in range(n_w + lag):
        for step in range(lag):
            j = tick - step
            if 0 <= j < n_w:
                if step == 0:
                    start_bits(j, 0)
                    local(g_in[j], acc[j], j).wait()
                elif step <= me.bits:
                    add_bits(j, step - 1)
                    if step < me.bits:
                        start_bits(j, step)
                    else:
                        start_z(j)
                else:
                    end_z(j)
        if phase < me.bits + 3:
            vec_phase(phase)
            phase += 1
    while phase < me.bits + 3:
        vec_phase(phase)
        phase += 1

    for j in range(n_w):
        for step in range(me.bits):
            for slot in range(2):
                send, count, _ = copies(j, step, slot)
                _each(count, lambda m: send(m).wait_send())
        for slot in range(2):
            target, copy = z_copy(j, slot)
            pl.when(target != me.z)(copy.wait_send)
        pl.when(me.home)(last_copy(j).wait_send)
        pl.when(jnp.logical_not(me.home))(last_copy(j).wait_recv)
    for step in range(me.bits):
        vec_bit(step).wait_send()
    for s in range(1, n_tensor):
        vec_z(s).wait_send()
    vec_last().wait_send()
    for n in range(n_acts):

        @pl.when(me.home)
        def _(n=n):
            for s in range(1, n_tensor):
                act_copy(n, s).wait_send()
            local(act_in[n].at[me.z], act_out[n].at[me.slot], n_w + n).wait()

        for slot in range(2):
            row = act_out[n].at[slot]
            copy = remote(row, row, a_send.at[n, 0], a_recv.at[n, slot], me.across())
            pl.when(me.core * half_z + slot != me.z)(copy.wait_recv)


def _base(bits, step):
    return sum(1 << (bits - 1 - s) for s in range(step))


def scatter(acts, vec, grads, kinds, sizes, cid):
    n_dp, n_tensor = sizes
    chips = n_dp // 2
    bits = chips.bit_length() - 1
    n_a, n_w = len(acts), len(grads)
    grads = [kind.cut(g) for kind, g in zip(kinds, grads)]
    shapes = [jax.ShapeDtypeStruct((n_tensor // 2,) + a.shape[1:], a.dtype) for a in acts]
    shapes += [jax.ShapeDtypeStruct((2,) + vec.shape, F32)]
    shapes += [jax.ShapeDtypeStruct(k.shard, F32) for k in kinds]
    dma = pltpu.SemaphoreType.DMA
    hbm = pl.BlockSpec(memory_space=pltpu.HBM)
    vmem = pl.BlockSpec(memory_space=pltpu.VMEM)
    most = max(chips // 2, 1)
    out = pl.pallas_call(
        functools.partial(scatter_kernel, kinds, n_a, sizes),
        out_shape=shapes,
        in_specs=[hbm] * n_a + [vmem] + [hbm] * n_w,
        out_specs=[hbm] * n_a + [vmem] + [vmem] * n_w,
        scratch_shapes=[pltpu.VMEM(k.whole, BF16) for k in kinds]
        + [pltpu.VMEM((chips - 1, 2) + k.two, BF16) for k in kinds]
        + [pltpu.VMEM((n_tensor - 1,) + k.two, BF16) for k in kinds]
        + [pltpu.VMEM(k.shard, F32) for k in kinds]
        + [
            pltpu.VMEM((bits + 2,) + vec.shape, F32),
            pltpu.VMEM((bits,) + vec.shape, F32),
            pltpu.VMEM((n_tensor,) + vec.shape, F32),
            dma((n_a, n_tensor)),
            dma((n_a, 2)),
            dma((n_w, bits, 2, most)),
            dma((n_w, bits, 2, most)),
            dma((n_w, 2)),
            dma((n_w, n_tensor)),
            dma((n_w,)),
            dma((n_w,)),
            dma((bits,)),
            dma((bits,)),
            dma((n_tensor,)),
            dma((n_tensor,)),
            dma((1,)),
            dma((1,)),
            dma((n_w + n_a,)),
        ],
        compiler_params=pltpu.CompilerParams(
            collective_id=cid, has_side_effects=True, vmem_limit_bytes=56 * 2**20
        ),
        name=f"scatter{cid}",
    )(*acts, vec, *grads)
    return out[:n_a], out[n_a], [k.leave(g) for k, g in zip(kinds, out[n_a + 1 :])]


KEYS = 1152
TILE = 272
COLS = 384


def _turn(x, cos, sin_up, sin_down):
    quarter = HEAD // 4
    return (
        x * cos
        + pltpu.roll(x, 2 * HEAD - quarter, 1) * sin_up
        + pltpu.roll(x, quarter, 1) * sin_down
    )


def front_kernel(
    kinds, sizes,
    tok_in, cot_in, pack_in, base_in, qkv_in, o_in, g_in, u_in, d_in,
    gain_ref, bias_ref, cos_ref, up_ref, down_ref,
    tok, cot, pack, base, w_qkv, w_o, w_g, w_u, w_d, normed, qa_ref, ka_ref, va_ref, mix_ref,
    *sems,
):
    me = Place(*sizes)
    nz = sizes[1]
    gather = Gather(me, kinds, (qkv_in, o_in, g_in, u_in, d_in), (w_qkv, w_o, w_g, w_u, w_d), sems[:7])
    tokens = Inward(me, tok_in, tok, sems[7:12])
    cots = Inward(me, cot_in, cot, sems[12:17])
    packs = Packs(me, pack_in, pack, base_in, base, sems[17:20])
    n_w = len(kinds)
    me.barrier()
    for j in range(n_w):
        gather.first_hop(j)
    gather.start_z(0)
    tokens.start()
    packs.start()
    gather.wait_z(0)
    for step in range(me.bits):
        if step > 0:
            gather.wait_bits(0, step - 1)
        gather.start_bits(0, step)
    tokens.pass_on()
    gather.start_z(1)

    def on_the_way():
        for j in range(1, n_w):
            gather.wait_z(j)
            if j + 1 < n_w:
                gather.start_z(j + 1)
            else:
                cots.start()
            gather.start_bits(j, 0)
            yield
            for step in range(1, me.bits):
                gather.wait_bits(j, step - 1)
                gather.start_bits(j, step)
                yield

    events = on_the_way()
    tokens.ready()
    packs.ready()

    block = tok.shape[1]
    rows = block * nz
    width = tok.shape[2]
    lanes = 2 * HEAD
    lane = lax.broadcasted_iota(jnp.int32, (block, lanes), 1)
    low = lane < HEAD
    one = jnp.where(lane == HEAD, 1.0, 0.0)
    ones = jnp.where((lane >= HEAD) & (lane < HEAD + 3), 1.0, 0.0)

    @pl.loop(0, nz)
    def _(t):
        x = tok[t].astype(F32)
        mean = jnp.sum(x, axis=1, keepdims=True) * (1.0 / width)
        x = x - mean
        var = jnp.sum(x * x, axis=1, keepdims=True) * (1.0 / width)
        x = x * lax.rsqrt(var + EPS)
        normed[pl.ds(pl.multiple_of(t * block, block), block), :] = (x * gain_ref[...] + bias_ref[...]).astype(BF16)

    gather.wait_bits(0, me.bits - 1)
    pairs = mix_ref.shape[1] // lanes
    sub = pairs // 2

    def project(g):
        at = (g // sub) * (3 * sub) + g % sub

        def column(part):
            return w_qkv[:, (at + part * sub) * lanes : (at + part * sub + 1) * lanes]

        q_bias = pack[g // sub, g % sub : g % sub + 1, :]
        v_bias = pack[g // sub, sub + g % sub : sub + g % sub + 1, :]

        @pl.loop(0, nz)
        def _(t):
            here = pl.ds(pl.multiple_of(t * block, block), block)
            x = normed[here, :]
            both = matmul(x, jnp.concatenate([column(0), column(1)], axis=1))
            tables = (cos_ref[here, :], up_ref[here, :], down_ref[here, :])
            query = _turn(both[:, :lanes] + q_bias, *tables) * (SCALE * LOG2E)
            key = _turn(both[:, lanes:], *tables)
            value = matmul(x, column(2)) + v_bias
            mask = base[here, :].astype(F32)
            for h in range(2):
                if h:
                    query, key, value = (pltpu.roll(v, HEAD, 1) for v in (query, key, value))
                qa_ref[2 * g + h, here, :] = jnp.where(low, query, one).astype(BF16)
                ka_ref[2 * g + h, here, :] = jnp.where(low, key, mask).astype(BF16)
                va_ref[2 * g + h, here, :] = jnp.where(low, value, ones).astype(BF16)

        rest = pl.ds(rows, KEYS - rows)
        for h in range(2):
            qa_ref[2 * g + h, rest, :] = jnp.zeros((KEYS - rows, lanes), BF16)
            va_ref[2 * g + h, rest, :] = jnp.zeros((KEYS - rows, lanes), BF16)
            ka_ref[2 * g + h, rest, :] = base[rest, :]

    def attend(g):
        @pl.loop(0, nz)
        def _(t):
            here = pl.ds(pl.multiple_of(t * block, block), block)
            outs = []
            for h in range(2):
                q = qa_ref[2 * g + h, here, :]
                s = matmul_right_t(q, ka_ref[2 * g + h])
                top = jnp.max(s, axis=1, keepdims=True)
                p = jnp.exp2(s - top).astype(BF16)
                o = matmul(p, va_ref[2 * g + h])
                total = o[:, HEAD : HEAD + 1]
                outs.append(o / total)
                log = -(top + jnp.log2(total))
                first = log.astype(BF16)
                left = log - first.astype(F32)
                second = left.astype(BF16)
                third = (left - second.astype(F32)).astype(BF16)
                logs = jnp.where(
                    lane == HEAD + 1,
                    first.astype(F32),
                    jnp.where(lane == HEAD + 2, second.astype(F32), third.astype(F32)),
                )
                inside = (lane > HEAD) & (lane <= HEAD + 3)
                qa_ref[2 * g + h, here, :] = jnp.where(inside, logs, q.astype(F32)).astype(BF16)
            mix_ref[here, g * lanes : (g + 1) * lanes] = jnp.where(
                low, outs[0], pltpu.roll(outs[1], HEAD, 1)
            ).astype(BF16)

    next(events, None)
    for g in range(pairs):
        project(g)
        next(events, None)
        attend(g)
        next(events, None)
    for _ in events:
        pass
    cots.pass_on()
    for j in range(1, n_w):
        gather.wait_bits(j, me.bits - 1)
    cots.ready()
    for j in range(n_w):
        gather.finish(j)
    tokens.finish()
    cots.finish()
    packs.finish()


def front(tokens, cotangent, pack, base, weights, kinds, gain, bias, tables, n_head, sizes, cid):
    nz = sizes[1]
    block, width = tokens.shape[1:]
    rows = block * nz
    lanes = 2 * HEAD
    heads = 2 * n_head // HEAD
    hbm = pl.BlockSpec(memory_space=pltpu.HBM)
    vmem = pl.BlockSpec(memory_space=pltpu.VMEM)
    shape = jax.ShapeDtypeStruct
    weights = [k.enter(w) for k, w in zip(kinds, weights)]
    shapes = [
        shape((nz, block, width), BF16),
        shape((nz, block, width), BF16),
        shape((2,) + pack.shape, F32),
        shape(base.shape, BF16),
        *[shape(k.whole, BF16) for k in kinds],
        shape((rows, width), BF16),
        *[shape((heads, KEYS, lanes), BF16)] * 3,
        shape((rows, heads * HEAD), BF16),
    ]
    out = pl.pallas_call(
        functools.partial(front_kernel, kinds, sizes),
        out_shape=shapes,
        in_specs=[hbm] * 9 + [vmem] * 5,
        out_specs=[vmem, hbm, vmem, vmem, vmem, hbm, hbm, hbm, hbm] + [vmem] * 5,
        scratch_shapes=Gather.semaphores(len(kinds), sizes)
        + Inward.semaphores(sizes)
        + Inward.semaphores(sizes)
        + Packs.semaphores(sizes),
        compiler_params=pltpu.CompilerParams(
            collective_id=cid, has_side_effects=True, vmem_limit_bytes=48 * 2**20
        ),
        name="front",
    )(tokens, cotangent, pack, base, *weights, gain[None], bias[None], *tables)
    return out[:4], [k.join(w) for k, w in zip(kinds, out[4:9])], out[9:]


def attention_backward_kernel(
    sub, qa_ref, ka_ref, va_ref, do_ref, mix_ref, cos_ref, up_ref, down_ref,
    out_ref, sum_ref, da_ref, dq_ref, dk_ref, dv_ref,
):
    rows = do_ref.shape[0]
    lanes = 2 * HEAD
    tiles = rows // TILE
    lane = lax.broadcasted_iota(jnp.int32, (TILE, lanes), 1)
    low = lane < HEAD
    g = pl.program_id(0)

    da_ref[pl.ds(rows, KEYS - rows), :] = jnp.zeros((KEYS - rows, lanes), BF16)
    for h in range(2):

        @pl.loop(0, tiles)
        def _(t, h=h):
            here = pl.ds(pl.multiple_of(t * TILE, TILE), TILE)
            d = do_ref[here, :].astype(F32)
            mine = low if h == 0 else jnp.logical_not(low)
            delta = -jnp.sum(jnp.where(mine, d * mix_ref[here, :].astype(F32), 0.0), axis=1, keepdims=True)
            if h:
                d = pltpu.roll(d, HEAD, 1)
            first = delta.astype(BF16)
            left = delta - first.astype(F32)
            second = left.astype(BF16)
            third = (left - second.astype(F32)).astype(BF16)
            logs = jnp.where(
                lane == HEAD,
                first.astype(F32),
                jnp.where(lane == HEAD + 1, second.astype(F32), third.astype(F32)),
            )
            da_ref[here, :] = jnp.where(low, d, jnp.where(lane < HEAD + 3, logs, 0.0)).astype(BF16)

        dk_ref[h] = jnp.zeros((KEYS, lanes), F32)
        dv_ref[h] = jnp.zeros((KEYS, lanes), F32)

        @pl.loop(0, KEYS // COLS)
        def _(t, h=h):
            here = pl.ds(pl.multiple_of(t * COLS, COLS), COLS)
            q = qa_ref[h, here, :]
            d = da_ref[here, :]
            p = jnp.exp2(matmul_right_t(ka_ref[h], q))
            ds = (p * matmul_right_t(va_ref[h], d)).astype(BF16)
            dv_ref[h] += matmul(p.astype(BF16), d)
            dk_ref[h] += matmul(ds, q)
            dq_ref[h, here, :] = matmul_left_t(ds, ka_ref[h])

    def put(column, row, ref, factor, turn):
        total = jnp.zeros((1, lanes), F32)
        for t in range(tiles):
            here = pl.ds(t * TILE, TILE)
            value = jnp.where(low, ref[0, here, :], pltpu.roll(ref[1, here, :], HEAD, 1))
            if factor is not None:
                value = value * factor
            if turn:
                value = _turn(value, cos_ref[here, :], -up_ref[here, :], -down_ref[here, :])
            if row is not None:
                total = total + jnp.sum(value, axis=0, keepdims=True)
            at = pl.multiple_of(column * (sub * lanes) + lax.rem(g, sub) * lanes, lanes)
            out_ref[here, pl.ds(at, lanes)] = value.astype(BF16)
        if row is not None:
            sum_ref[0, pl.ds(row, 1), :] = total

    put(0, 0, dq_ref, SCALE, True)
    put(1, None, dk_ref, LN2, True)
    put(2, 1, dv_ref, None, False)


def attention_backward(qa, ka, va, d_mixed, mixed, tables):
    rows = mixed.shape[0]
    lanes = 2 * HEAD
    pairs = mixed.shape[1] // lanes
    sub = pairs // 2
    heads = pl.BlockSpec((2, KEYS, lanes), lambda g: (g, 0, 0))
    pair = pl.BlockSpec((rows, lanes), lambda g: (0, g))
    return pl.pallas_call(
        functools.partial(attention_backward_kernel, sub),
        grid=(pairs,),
        out_shape=[
            jax.ShapeDtypeStruct((rows, 3 * pairs * lanes), BF16),
            jax.ShapeDtypeStruct((pairs, 8, lanes), F32),
        ],
        in_specs=[heads, heads, heads, pair, pair]
        + [pl.BlockSpec((rows, lanes), lambda g: (0, 0))] * 3,
        out_specs=[
            pl.BlockSpec((rows, 3 * sub * lanes), lambda g: (0, g // sub)),
            pl.BlockSpec((1, 8, lanes), lambda g: (g, 0, 0)),
        ],
        scratch_shapes=[
            pltpu.VMEM((KEYS, lanes), BF16),
            pltpu.VMEM((2, KEYS, lanes), F32),
            pltpu.VMEM((2, KEYS, lanes), F32),
            pltpu.VMEM((2, KEYS, lanes), F32),
        ],
        compiler_params=pltpu.CompilerParams(vmem_limit_bytes=48 * 2**20),
        name="attention_backward",
    )(qa, ka, va, d_mixed, mixed, *tables)


def shards(
    tokens_in, cotangent, image_flag, key_mask, column_mask,
    attention_norm_gain, attention_norm_bias, w_query, w_key, w_value, query_bias, value_bias, w_out, out_bias,
    feedforward_norm_gain, feedforward_norm_bias, w_gate, gate_bias, w_up, up_bias, inner_gain, inner_shift,
    w_down, down_bias,
):
    n_dp, n_tensor = lax.axis_size("dp"), lax.axis_size("tensor")
    sizes = (n_dp, n_tensor)
    dp, z = lax.axis_index("dp"), lax.axis_index("tensor")
    core = dp % 2
    block = tokens_in.shape[1]
    width = tokens_in.shape[2]
    length = block * n_tensor
    block_pad = up_to(block, 16)
    rows = block_pad * n_tensor
    n_head = w_query.shape[1]
    n_ff = w_gate.shape[1]
    ff = up_to(n_ff, 16)
    count_live = float(FF - PADCOLS)
    swap = [(i, (i // n_tensor ^ 1) * n_tensor + i % n_tensor) for i in range(n_dp * n_tensor)]

    def other(value):
        return lax.ppermute(value, ("dp", "tensor"), swap)

    shard_qkv = jnp.concatenate([w_query, w_key, w_value], axis=1)
    kind_qkv = Kind(True, shard_qkv.shape, n_dp)
    kind_o = Kind(False, w_out.shape, n_dp)
    kind_f = Kind(False, (ff, w_down.shape[1]), n_dp)

    def pad_ff(vec):
        return jnp.pad(vec, (0, ff - n_ff))

    def turned(weight):
        return jnp.pad(weight.T, ((0, ff - n_ff), (0, 0)))

    def pad_rows(value):
        return jnp.pad(value, ((0, 0), (0, block_pad - block), (0, 0)))

    def unpadded(value):
        return value.reshape(n_tensor, block_pad, width)[:, :block]

    small = jnp.concatenate(
        [query_bias, value_bias]
        + [pad_ff(v) for v in (gate_bias, up_bias, inner_gain, inner_shift, column_mask.astype(F32))]
    )
    small_rows = up_to(up_to(small.shape[0], LANES) // LANES, 8)
    small = jnp.pad(small, (0, small_rows * LANES - small.shape[0])).reshape(small_rows, LANES)
    own_image = z % (n_tensor // 2)
    live = lax.dynamic_index_in_dim(key_mask, own_image, 0, False)
    live = jnp.pad(live.reshape(n_tensor, block), ((0, 0), (0, block_pad - block))).reshape(rows)
    live = jnp.pad(live, (0, KEYS - rows))
    lane = jnp.arange(LANES)[None, :]
    base = jnp.where(
        lane == HEAD,
        jnp.where(live > 0, 0.0, -1e30)[:, None],
        jnp.where(
            (lane > HEAD) & (lane <= HEAD + 3),
            1.0,
            jnp.where(lane == LANES - 1, lax.dynamic_index_in_dim(image_flag, own_image, 0, False).astype(F32), 0.0),
        ),
    ).astype(BF16)
    tables = lane_tables(length, HEAD // 4, block, block_pad)

    (image, cot, packs, base), full, (normed, qa, ka, va, mixed) = front(
        pad_rows(tokens_in),
        pad_rows(cotangent),
        small,
        base,
        [shard_qkv, w_out, turned(w_gate), turned(w_up), jnp.pad(w_down, ((0, ff - n_ff), (0, 0)))],
        [kind_qkv, kind_o, kind_f, kind_f, kind_f],
        attention_norm_gain,
        attention_norm_bias,
        tables,
        n_head,
        sizes,
        0,
    )
    full_qkv, full_o, full_g, full_u, full_d = full
    packs = packs.reshape(2, -1)
    cuts = [n_head] * 2 + [ff] * 5
    parts, at = [], 0
    for size in cuts:
        parts.append(packs[:, at : at + size].reshape(-1))
        at += size
    _, _, g_bias, u_bias, gain, shift, columns = parts
    flag = base[0, LANES - 1].astype(F32)
    token_rows = image.reshape(rows, width).astype(F32)
    xhat1, s1 = norm_pieces(token_rows)
    part = matmul(mixed, full_o).astype(BF16)
    middle = token_rows + (part.astype(F32) + other(part).astype(F32)) + out_bias
    xhat2, s2 = norm_pieces(middle)
    normed2 = (xhat2 * feedforward_norm_gain + feedforward_norm_bias).astype(BF16)
    gate = matmul_right_t(normed2, full_g) + g_bias
    up = matmul_right_t(normed2, full_u) + u_bias
    sig = jax.nn.sigmoid(gate)
    act = gate * sig * up
    sums = jnp.stack([jnp.sum(act * columns, axis=-1), jnp.sum(act * act * columns, axis=-1)])
    sums = sums + other(sums)
    mean = sums[0][:, None] / count_live
    var = sums[1][:, None] / count_live - mean * mean
    r = lax.rsqrt(var + EPS)
    nhat = (act - mean) * r
    hidden = (columns * (nhat * gain + shift)).astype(BF16)
    part = matmul(hidden, full_d).astype(BF16)
    output = (middle + (part.astype(F32) + other(part).astype(F32)) + down_bias).astype(BF16)

    grad = cot.reshape(rows, width).astype(F32) * flag
    grad_low = grad.astype(BF16)
    g_down = matmul_left_t(hidden, grad_low).astype(BF16)
    dn = columns * lax.dot_general(
        grad_low, full_d, (((1,), (1,)), ((), ())), preferred_element_type=F32
    )
    g_gain = jnp.sum(dn * nhat, axis=0)
    g_shift = jnp.sum(dn, axis=0)
    dnh = dn * gain
    back = jnp.stack([jnp.sum(dnh, axis=-1), jnp.sum(dnh * nhat, axis=-1)])
    back = back + other(back)
    dact = r * (dnh - columns * (back[0][:, None] + nhat * back[1][:, None]) / count_live)
    dgate = dact * up * sig * (1.0 + gate * (1.0 - sig))
    dup = dact * gate * sig
    g_gate_bias = jnp.sum(dgate, axis=0)
    g_up_bias = jnp.sum(dup, axis=0)
    gate_low = dgate.astype(BF16)
    up_low = dup.astype(BF16)
    g_gate = matmul_left_t(gate_low, normed2).astype(BF16)
    g_up = matmul_left_t(up_low, normed2).astype(BF16)
    part = (matmul(gate_low, full_g) + matmul(up_low, full_u)).astype(BF16)
    dnormed2 = part.astype(F32) + other(part).astype(F32)
    g_mlp_gain = jnp.sum(dnormed2 * xhat2, axis=0)
    g_mlp_shift = jnp.sum(dnormed2, axis=0)
    dmiddle = grad + norm_backward(dnormed2, xhat2, s2, feedforward_norm_gain)
    g_out_bias = jnp.sum(dmiddle, axis=0)
    g_down_bias = jnp.sum(grad, axis=0)
    dmid_low = dmiddle.astype(BF16)
    g_out = matmul_left_t(mixed, dmid_low).astype(BF16)
    d_mixed = matmul_right_t(dmid_low, full_o).astype(BF16)
    d_qkv, qv_sums = attention_backward(qa, ka, va, d_mixed, mixed, tables)
    g_qkv = matmul_left_t(normed, d_qkv).astype(BF16)
    part = matmul_right_t(d_qkv, full_qkv).astype(BF16)
    dnormed = part.astype(F32) + other(part).astype(F32)
    g_attn_gain = jnp.sum(dnormed * xhat1, axis=0)
    g_attn_shift = jnp.sum(dnormed, axis=0)
    input_grad = dmiddle + norm_backward(dnormed, xhat1, s1, attention_norm_gain)

    def by_slot(vec):
        return vec.reshape(2, -1)

    vec = jnp.concatenate(
        [g_attn_gain, g_attn_shift, g_out_bias, g_mlp_gain, g_mlp_shift, g_down_bias]
        + [
            jnp.concatenate(
                [by_slot(v) for v in (qv_sums[:, 0], qv_sums[:, 1], g_gate_bias, g_up_bias, g_gain, g_shift)], axis=1
            ).reshape(-1)
        ]
    )
    vec_size = vec.shape[0]
    vec_rows = up_to(up_to(vec_size, LANES) // LANES, 8)
    vec = jnp.pad(vec, (0, vec_rows * LANES - vec_size)).reshape(vec_rows, LANES)
    (out_rows, in_rows), vec, (s_down, s_gate, s_up, s_out, s_qkv) = scatter(
        [unpadded(output), unpadded(input_grad.astype(BF16))],
        vec,
        [g_down, g_gate, g_up, g_out, g_qkv],
        [kind_f, kind_f, kind_f, kind_o, kind_qkv],
        sizes,
        2,
    )
    vec = vec.reshape(2, -1)
    wide = vec[0, : 6 * width].reshape(6, width)
    owner = z // (n_tensor // 2)
    tall = lax.dynamic_index_in_dim(vec, owner, 0, False)[6 * width : vec_size].reshape(2, -1)
    tall = lax.dynamic_index_in_dim(tall, z % (n_tensor // 2), 0, False)
    pieces, at = [], 0
    for size in [n_head] * 2 + [ff] * 4:
        pieces.append(tall[at : at + size])
        at += size
    return (
        out_rows,
        in_rows.astype(F32),
        wide[0],
        wide[1],
        s_qkv[:, :n_head],
        s_qkv[:, n_head : 2 * n_head],
        s_qkv[:, 2 * n_head :],
        pieces[0],
        pieces[1],
        s_out,
        wide[2],
        wide[3],
        wide[4],
        s_gate[:n_ff].T,
        pieces[2][:n_ff],
        s_up[:n_ff].T,
        pieces[3][:n_ff],
        pieces[4][:n_ff],
        pieces[5][:n_ff],
        s_down[:n_ff],
        wide[5],
    )


def solution(mesh):
    act, row, col, vec = P("dp", "tensor", None), P("dp", "tensor"), P("tensor", "dp"), P("tensor")
    in_specs = (
        act, act, P("dp"), P("dp", None), vec, P(), P(), row, row, row, vec, vec, col, P(), P(), P(),
        row, vec, row, vec, vec, vec, col, P(),
    )
    out_specs = (
        act, act, P(), P(), row, row, row, vec, vec, col, P(), P(), P(), row, vec, row, vec, vec, vec, col, P(),
    )
    return jax.shard_map(shards, mesh=mesh, in_specs=in_specs, out_specs=out_specs, check_vma=False)
```

```python
import functools
import math

import jax
import jax.numpy as jnp
from jax import lax
from jax.experimental import pallas as pl
from jax.experimental.pallas import tpu as pltpu
from jax.sharding import PartitionSpec as P

HEAD = 64
FF = 2736
PADCOLS = 6
GRID = 32
EPS = 1e-06
ROPE_BASE = 10000.0
LANES = 128
MESH = pl.DeviceIdType.MESH
LOG2E = math.log2(math.e)
LN2 = math.log(2.0)
SCALE = HEAD ** (-0.5)
F32 = jnp.float32
BF16 = jnp.bfloat16


def up_to(size, unit):
    return -(-size // unit) * unit


def rotary_tables(length, head):
    quarter = head // 4
    place = jnp.arange(length, dtype=jnp.int32)
    inside = (place >= 1) & (place <= GRID * GRID)
    cell = jnp.maximum(place - 1, 0)
    row_pos = jnp.where(inside, cell // GRID, 0).astype(F32)
    col_pos = jnp.where(inside, cell % GRID, 0).astype(F32)
    freq = ROPE_BASE ** (-jnp.arange(quarter, dtype=F32) / quarter)
    angle = jnp.concatenate(
        [row_pos[:, None] * freq[None, :], col_pos[:, None] * freq[None, :]], axis=1
    )
    return jnp.cos(angle), jnp.sin(angle)


def lane_tables(length, quarter, block, rows_padded):
    cosv, sinv = rotary_tables(length, HEAD)

    def lay(first, second):
        one = jnp.concatenate(
            [first[:, :quarter], second[:, :quarter], first[:, quarter:], second[:, quarter:]], axis=1
        )
        two = jnp.concatenate([one, one], axis=1)
        cut = two.reshape(length // block, block, 2 * HEAD)
        return jnp.pad(cut, ((0, 0), (0, rows_padded - block), (0, 0))).reshape(-1, 2 * HEAD)

    zero = jnp.zeros_like(sinv)
    return lay(cosv, cosv), lay(-sinv, zero), lay(zero, sinv)


def norm_pieces(values):
    row_mean = jnp.mean(values, axis=-1, keepdims=True)
    var = jnp.mean(jnp.square(values - row_mean), axis=-1, keepdims=True)
    inverse_scale = lax.rsqrt(var + EPS)
    return ((values - row_mean) * inverse_scale, inverse_scale)


def norm_backward(incoming_gradient, centered_normalized, inverse_scale, norm_gain):
    inner = incoming_gradient * norm_gain
    return inverse_scale * (
        inner
        - jnp.mean(inner, axis=-1, keepdims=True)
        - centered_normalized * jnp.mean(inner * centered_normalized, axis=-1, keepdims=True)
    )


def matmul(left, right):
    return jnp.dot(left, right, preferred_element_type=F32)


def matmul_right_t(left, right):
    return lax.dot_general(left, right, (((1,), (1,)), ((), ())), preferred_element_type=F32)


def matmul_left_t(left, right):
    return lax.dot_general(left, right, (((0,), (0,)), ((), ())), preferred_element_type=F32)


class Kind:
    def __init__(self, by_rows, shard, n_dp):
        self.given = shard
        self.n_dp = n_dp
        self.turn = not by_rows and shard[1] % LANES != 0
        if self.turn:
            shard = (shard[1], up_to(shard[0], LANES))
        self.by_rows = by_rows or self.turn
        self.shard = shard
        a, b = shard
        if self.by_rows:
            self.whole, self.two = (n_dp * a, 2 * b), (2 * a, b)
        else:
            self.whole, self.two = (2 * a, n_dp * b), (a, 2 * b)

    def piece(self, ref, slot, chip):
        a, b = self.shard
        if self.by_rows:
            return ref.at[pl.ds(_mult(chip, 2 * a), 2 * a), pl.ds(_mult(slot, b), b)]
        return ref.at[pl.ds(_mult(slot, a), a), pl.ds(_mult(chip, 2 * b), 2 * b)]

    def half(self, two, core):
        a, b = self.shard
        if self.by_rows:
            return two.at[pl.ds(_mult(core, a), a)]
        return two.at[:, pl.ds(_mult(core, b), b)]

    def one(self, ref, slot, chip, core):
        a, b = self.shard
        if self.by_rows:
            return ref.at[pl.ds(_mult(chip * 2 + core, a), a), pl.ds(_mult(slot, b), b)]
        return ref.at[pl.ds(_mult(slot, a), a), pl.ds(_mult(chip * 2 + core, b), b)]

    def enter(self, shard):
        if not self.turn:
            return shard
        return jnp.pad(shard.T, ((0, 0), (0, self.shard[1] - self.given[0])))

    def leave(self, shard):
        return shard[:, : self.given[0]].T if self.turn else shard

    def join(self, whole):
        if not self.turn:
            return whole
        a, b = self.shard
        whole = whole.reshape(self.n_dp * a, 2, b)[:, :, : self.given[0]]
        return whole.transpose(1, 2, 0).reshape(2 * self.given[0], self.n_dp * a)

    def cut(self, whole):
        if not self.turn:
            return whole
        a, b = self.shard
        whole = whole.reshape(2, self.given[0], self.n_dp * a).transpose(2, 0, 1)
        return jnp.pad(whole, ((0, 0), (0, 0), (0, b - self.given[0]))).reshape(self.whole)


def _mult(index, size):
    return index * size if isinstance(index, int) else pl.multiple_of(index * size, size)


class Place:
    def __init__(self, n_dp, n_tensor):
        self.dp = lax.axis_index("dp")
        self.z = lax.axis_index("tensor")
        self.core = lax.rem(self.dp, 2)
        self.chip = lax.div(self.dp, 2)
        self.nz = n_tensor
        self.chips = n_dp // 2
        self.bits = self.chips.bit_length() - 1
        self.home = self.core == lax.div(self.z, n_tensor // 2)
        self.slot = lax.rem(self.z, n_tensor // 2)

    def flip(self, bit):
        low = lax.rem(lax.div(self.chip, 1 << bit), 2)
        return self.chip + (1 - 2 * low) * (1 << bit)

    def across(self):
        return (self.dp + 1 - 2 * self.core, self.z)

    def beside(self, bit):
        return (self.flip(bit) * 2 + self.core, self.z)

    def shifted(self, by):
        return (self.dp, lax.rem(self.z + by, self.nz))

    def barrier(self):
        everyone = [self.across()]
        everyone += [self.shifted(s) for s in range(1, self.nz)]
        everyone += [self.beside(b) for b in range(self.bits)]
        bar = pltpu.get_barrier_semaphore()
        for one in everyone:
            pl.semaphore_signal(bar, inc=1, device_id=one, device_id_type=MESH)
        pl.semaphore_wait(bar, len(everyone))


def remote(src, dst, send, recv, to):
    return pltpu.make_async_remote_copy(
        src_ref=src, dst_ref=dst, send_sem=send, recv_sem=recv, device_id=to, device_id_type=MESH
    )


def flipped(chip, value):
    return lax.bitwise_xor(chip, value)


class Gather:
    def __init__(self, me, kinds, w_in, w_out, sems):
        self.me, self.kinds, self.w_in, self.w_out = me, kinds, w_in, w_out
        self.s_send, self.s_recv, self.z_send, self.z_recv, self.b_send, self.b_recv, self.loc = sems

    @staticmethod
    def semaphores(n_w, sizes):
        dma = pltpu.SemaphoreType.DMA
        bits = (sizes[0] // 2).bit_length() - 1
        most = max(1 << max(bits - 1, 0), 1)
        return [
            dma((n_w,)),
            dma((n_w,)),
            dma((n_w, sizes[1])),
            dma((n_w, 2)),
            dma((n_w, bits, 2, most)),
            dma((n_w, bits, 2, most)),
            dma((n_w,)),
        ]

    def _hop(self, j):
        me = self.me
        mine = self.kinds[j].one(self.w_out[j], me.slot, me.chip, me.core)
        return (
            pltpu.make_async_copy(self.w_in[j], mine, self.loc.at[j]),
            remote(self.w_in[j], mine, self.s_send.at[j], self.s_recv.at[j], me.across()),
        )

    def first_hop(self, j):
        stay, leave = self._hop(j)
        pl.when(self.me.home)(stay.start)
        pl.when(jnp.logical_not(self.me.home))(leave.start)

    def _along(self, j, s):
        me = self.me
        src = self.kinds[j].piece(self.w_out[j], me.slot, me.chip)
        return remote(src, src, self.z_send.at[j, s - 1], self.z_recv.at[j, me.slot], me.shifted(s))

    def start_z(self, j):
        @pl.when(self.me.home)
        def _():
            stay, leave = self._hop(j)
            stay.wait()
            leave.wait_recv()
            for s in range(1, self.me.nz):
                self._along(j, s).start()

    def wait_z(self, j):
        me = self.me
        for slot in range(2):
            src = self.kinds[j].piece(self.w_out[j], slot, me.chip)
            copy = remote(src, src, self.z_send.at[j, 0], self.z_recv.at[j, slot], me.across())
            pl.when(me.core * (me.nz // 2) + slot != me.z)(copy.wait_recv)

    def _bits(self, j, step, slot):
        me = self.me
        bit = step if slot == 0 else me.bits - 1 - step
        low = 1 if slot == 0 else 1 << (me.bits - step)

        def send(m):
            src = self.kinds[j].piece(self.w_out[j], slot, flipped(me.chip, m * low))
            return remote(
                src, src, self.b_send.at[j, step, slot, m], self.b_recv.at[j, step, slot, m], me.beside(bit)
            )

        return send

    def start_bits(self, j, step):
        for slot in range(2):
            send = self._bits(j, step, slot)
            _each(1 << step, lambda m: send(m).start())

    def wait_bits(self, j, step):
        for slot in range(2):
            send = self._bits(j, step, slot)
            _each(1 << step, lambda m: send(m).wait_recv())

    def finish(self, j):
        me = self.me
        pl.when(jnp.logical_not(me.home))(self._hop(j)[1].wait_send)
        for s in range(1, me.nz):
            pl.when(me.home)(self._along(j, s).wait_send)
        for step in range(me.bits):
            for slot in range(2):
                send = self._bits(j, step, slot)
                _each(1 << step, lambda m: send(m).wait_send())


class Inward:
    def __init__(self, me, src, dst, sems):
        self.me, self.src, self.dst = me, src, dst
        self.send, self.recv, self.fwd, self.back, self.loc = sems

    @staticmethod
    def semaphores(sizes):
        dma = pltpu.SemaphoreType.DMA
        return [dma((sizes[1],)), dma((sizes[1],)), dma((sizes[1],)), dma((sizes[1],)), dma((1,))]

    def _copy(self, i):
        me = self.me
        target = me.nz // 2 * me.core + i
        return target, remote(
            self.src.at[i], self.dst.at[me.z], self.send.at[i], self.recv.at[me.z], (me.dp, target)
        )

    def _stay(self, i):
        return pltpu.make_async_copy(self.src.at[i], self.dst.at[self.me.z], self.loc.at[0])

    def _onward(self, place):
        slab = self.dst.at[place]
        return remote(slab, slab, self.fwd.at[place], self.back.at[place], self.me.across())

    def start(self):
        for i in range(self.me.nz // 2):
            target, copy = self._copy(i)
            pl.when(target != self.me.z)(copy.start)
            pl.when(target == self.me.z)(self._stay(i).start)

    def pass_on(self):
        me = self.me

        @pl.when(me.home)
        def _():
            for s in range(me.nz):
                place = lax.rem(me.z + s, me.nz)
                if s == 0:
                    self._stay(0).wait()
                else:
                    slab = self.dst.at[place]
                    remote(slab, slab, self.send.at[0], self.recv.at[place], me.across()).wait_recv()
                self._onward(place).start()

    def ready(self):
        for place in range(self.me.nz):
            pl.when(jnp.logical_not(self.me.home))(self._onward(place).wait_recv)

    def finish(self):
        for i in range(self.me.nz // 2):
            target, copy = self._copy(i)
            pl.when(target != self.me.z)(copy.wait_send)
        for place in range(self.me.nz):
            pl.when(self.me.home)(self._onward(place).wait_send)


class Packs:
    def __init__(self, me, src, dst, pair_src, pair_dst, sems):
        self.me, self.src, self.dst, self.pair_src, self.pair_dst = me, src, dst, pair_src, pair_dst
        self.send, self.recv, self.loc = sems

    @staticmethod
    def semaphores(sizes):
        dma = pltpu.SemaphoreType.DMA
        return [dma((sizes[1],)), dma((3,)), dma((2,))]

    def _copy(self, s):
        me = self.me
        return remote(self.src, self.dst.at[me.slot], self.send.at[s], self.recv.at[me.slot], me.shifted(s))

    def _stay(self):
        return pltpu.make_async_copy(self.src, self.dst.at[self.me.slot], self.loc.at[0])

    def _pair(self):
        return (
            pltpu.make_async_copy(self.pair_src, self.pair_dst, self.loc.at[1]),
            remote(self.pair_src, self.pair_dst, self.send.at[0], self.recv.at[2], self.me.across()),
        )

    def start(self):
        @pl.when(self.me.home)
        def _():
            self._stay().start()
            for s in range(1, self.me.nz):
                self._copy(s).start()
            stay, there = self._pair()
            stay.start()
            there.start()

    def ready(self):
        me = self.me
        for slot in range(2):
            row = self.dst.at[slot]
            copy = remote(row, row, self.send.at[0], self.recv.at[slot], me.across())
            pl.when(me.core * (me.nz // 2) + slot != me.z)(copy.wait_recv)
        stay, there = self._pair()

        @pl.when(me.home)
        def _():
            self._stay().wait()
            stay.wait()

        pl.when(jnp.logical_not(me.home))(there.wait_recv)

    def finish(self):
        @pl.when(self.me.home)
        def _():
            for s in range(1, self.me.nz):
                self._copy(s).wait_send()
            self._pair()[1].wait_send()


def _each(count, act):
    if count <= 4:
        for m in range(count):
            act(m)
    else:

        @pl.loop(0, count)
        def _(m):
            act(m)


class Scatter:
    def __init__(self, me, kinds, g_in, keep, got, gotz, stage, g_out, sems):
        self.me, self.kinds, self.g_in, self.keep, self.got = me, kinds, g_in, keep, got
        self.gotz, self.stage, self.g_out = gotz, stage, g_out
        self.b_send, self.b_recv, self.z_send, self.z_recv, self.f_send, self.f_recv, self.loc = sems

    @staticmethod
    def semaphores(n_w, sizes):
        dma = pltpu.SemaphoreType.DMA
        chips = sizes[0] // 2
        bits = chips.bit_length() - 1
        return [
            dma((n_w, bits, 2, chips // 2)),
            dma((n_w, bits, 2, chips // 2)),
            dma((n_w, 2)),
            dma((n_w, sizes[1])),
            dma((n_w,)),
            dma((n_w,)),
            dma((n_w, 2, chips // 2)),
        ]

    def _count(self, step):
        return 1 << (self.me.bits - 1 - step)

    def _base(self, step):
        return sum(self._count(s) for s in range(step))

    def _first(self, j, slot, m, sent):
        bits = self.me.bits
        if slot == 0:
            flip = m + (1 << (bits - 1)) * sent
        else:
            flip = m * 2 + sent
        return self.kinds[j].piece(self.g_in[j], slot, flipped(self.me.chip, flip))

    def _held(self, j, step, slot, m, sent):
        index = m + self._count(step) * sent if slot == 0 else 2 * m + sent
        return self.got[j].at[self._base(step - 1) + index, slot]

    def _copy(self, j, step, slot, m):
        me = self.me
        bit = me.bits - 1 - step if slot == 0 else step
        src = self._first(j, slot, m, 1) if step == 0 else self._held(j, step, slot, m, 1)
        return remote(
            src,
            self.got[j].at[self._base(step) + m, slot],
            self.b_send.at[j, step, slot, m],
            self.b_recv.at[j, step, slot, m],
            me.beside(bit),
        )

    def _load(self, j, slot, m):
        return pltpu.make_async_copy(self._first(j, slot, m, 0), self.keep[j].at[slot, m], self.loc.at[j, slot, m])

    def start(self, j, step):
        for slot in range(2):
            _each(self._count(step), lambda m: self._copy(j, step, slot, m).start())
        if step == 0 and self.keep[j] is not None:
            for slot in range(2):
                _each(self._count(step), lambda m: self._load(j, slot, m).start())

    def add(self, j, step):
        for slot in range(2):

            def one(m):
                self._copy(j, step, slot, m).wait_recv()
                if step > 0:
                    mine = self._held(j, step, slot, m, 0)
                elif self.keep[j] is not None:
                    self._load(j, slot, m).wait()
                    mine = self.keep[j].at[slot, m]
                else:
                    mine = self._first(j, slot, m, 0)
                here = self.got[j].at[self._base(step) + m, slot]
                here[...] = (here[...].astype(F32) + mine[...].astype(F32)).astype(BF16)

            _each(self._count(step), one)

    def _last(self, j, slot):
        return self.got[j].at[self._base(self.me.bits - 1), slot]

    def _z(self, j, slot):
        me = self.me
        target = me.nz // 2 * me.core + slot
        index = lax.rem(me.z - target + me.nz - 1, me.nz)
        return target, remote(
            self._last(j, slot), self.gotz[j].at[index], self.z_send.at[j, slot], self.z_recv.at[j, index], (me.dp, target)
        )

    def start_z(self, j):
        for slot in range(2):
            target, copy = self._z(j, slot)
            pl.when(target != self.me.z)(copy.start)

    def _hand(self, j):
        return remote(self.stage[j], self.g_out[j], self.f_send.at[j], self.f_recv.at[j], self.me.across())

    def end_z(self, j):
        me = self.me

        @pl.when(me.home)
        def _():
            for index in range(me.nz - 1):
                slab = self.gotz[j].at[index]
                remote(slab, slab, self.z_send.at[j, 0], self.z_recv.at[j, index], me.across()).wait_recv()

            def total(core):
                value = self.kinds[j].half(self._last(j, me.slot), core)[...].astype(F32)
                for index in range(me.nz - 1):
                    value = value + self.kinds[j].half(self.gotz[j].at[index], core)[...].astype(F32)
                return value

            self.stage[j][...] = total(1 - me.core)
            self._hand(j).start()
            self.g_out[j][...] = total(me.core)

    def finish(self, j):
        me = self.me
        for step in range(me.bits):
            for slot in range(2):
                _each(self._count(step), lambda m: self._copy(j, step, slot, m).wait_send())
        for slot in range(2):
            target, copy = self._z(j, slot)
            pl.when(target != me.z)(copy.wait_send)
        hand = self._hand(j)
        pl.when(me.home)(hand.wait_send)
        pl.when(jnp.logical_not(me.home))(hand.wait_recv)


class Sums:
    def __init__(self, me, v_sum, v_got, v_all, out, sems):
        self.me, self.v_sum, self.v_got, self.v_all, self.out = me, v_sum, v_got, v_all, out
        self.b_send, self.b_recv, self.z_send, self.z_recv, self.f_send, self.f_recv = sems

    @staticmethod
    def semaphores(sizes):
        dma = pltpu.SemaphoreType.DMA
        bits = (sizes[0] // 2).bit_length() - 1
        return [dma((bits,)), dma((bits,)), dma((sizes[1],)), dma((sizes[1],)), dma((1,)), dma((1,))]

    @staticmethod
    def scratch(shape, sizes):
        bits = (sizes[0] // 2).bit_length() - 1
        return [
            pltpu.VMEM((bits + 2,) + shape, F32),
            pltpu.VMEM((bits,) + shape, F32),
            pltpu.VMEM((sizes[1],) + shape, F32),
        ]

    def _bit(self, step):
        return remote(
            self.v_sum.at[step], self.v_got.at[step], self.b_send.at[step], self.b_recv.at[step], self.me.beside(step)
        )

    def _z(self, s):
        me = self.me
        return remote(
            self.v_sum.at[me.bits], self.v_all.at[me.z], self.z_send.at[s], self.z_recv.at[me.z], me.shifted(s)
        )

    def _last(self):
        me = self.me
        return remote(self.v_sum.at[me.bits + 1], self.out.at[me.core], self.f_send.at[0], self.f_recv.at[0], me.across())

    def phases(self):
        me = self.me
        self._bit(0).start()
        yield
        for step in range(1, me.bits + 1):
            self._bit(step - 1).wait_recv()
            self.v_sum[step] = self.v_sum[step - 1] + self.v_got[step - 1]
            if step < me.bits:
                self._bit(step).start()
                yield
        for s in range(1, me.nz):
            self._z(s).start()
        self.v_all[me.z] = self.v_sum[me.bits]
        yield
        for s in range(1, me.nz):
            slab = self.v_all.at[lax.rem(me.z + s, me.nz)]
            place = lax.rem(me.z + s, me.nz)
            remote(slab, slab, self.z_send.at[0], self.z_recv.at[place], me.across()).wait_recv()
        value = self.v_all[0]
        for s in range(1, me.nz):
            value = value + self.v_all[s]
        self.v_sum[me.bits + 1] = value
        self._last().start()
        self.out[me.core] = value
        yield
        there = self.out.at[1 - me.core]
        remote(there, there, self.f_send.at[0], self.f_recv.at[0], me.across()).wait_recv()
        for step in range(me.bits):
            self._bit(step).wait_send()
        for s in range(1, me.nz):
            self._z(s).wait_send()
        self._last().wait_send()


class Outward:
    def __init__(self, me, src, dst, sems):
        self.me, self.src, self.dst = me, src, dst
        self.send, self.recv, self.loc = sems

    @staticmethod
    def semaphores(sizes):
        dma = pltpu.SemaphoreType.DMA
        return [dma((sizes[1],)), dma((2,)), dma((1,))]

    def _copy(self, place):
        me = self.me
        return remote(
            self.src.at[place], self.dst.at[me.slot], self.send.at[place], self.recv.at[me.slot], (me.dp, place)
        )

    def _stay(self, place):
        return pltpu.make_async_copy(self.src.at[place], self.dst.at[self.me.slot], self.loc.at[0])

    def start(self, place):
        me = self.me
        pl.when(jnp.logical_and(me.home, place != me.z))(lambda: self._copy(place).start())
        pl.when(jnp.logical_and(me.home, place == me.z))(lambda: self._stay(place).start())

    def finish(self):
        me = self.me
        for place in range(me.nz):
            pl.when(jnp.logical_and(me.home, place != me.z))(lambda place=place: self._copy(place).wait_send())
            pl.when(jnp.logical_and(me.home, place == me.z))(lambda place=place: self._stay(place).wait())
        for slot in range(2):
            row = self.dst.at[slot]
            copy = remote(row, row, self.send.at[0], self.recv.at[slot], me.across())
            pl.when(me.core * (me.nz // 2) + slot != me.z)(copy.wait_recv)


KEYS = 1152
TILE = 272
COLS = 384


def _turn(x, cos, sin_up, sin_down):
    quarter = HEAD // 4
    return (
        x * cos
        + pltpu.roll(x, 2 * HEAD - quarter, 1) * sin_up
        + pltpu.roll(x, quarter, 1) * sin_down
    )


def front_kernel(
    kinds, sizes,
    tok_in, cot_in, pack_in, base_in, qkv_in, o_in, g_in, u_in, d_in,
    gain_ref, bias_ref, cos_ref, up_ref, down_ref,
    tok, cot, pack, base, w_qkv, w_o, w_g, w_u, w_d, normed, qa_ref, ka_ref, va_ref, mix_ref,
    *sems,
):
    me = Place(*sizes)
    nz = sizes[1]
    gather = Gather(me, kinds, (qkv_in, o_in, g_in, u_in, d_in), (w_qkv, w_o, w_g, w_u, w_d), sems[:7])
    tokens = Inward(me, tok_in, tok, sems[7:12])
    cots = Inward(me, cot_in, cot, sems[12:17])
    packs = Packs(me, pack_in, pack, base_in, base, sems[17:20])
    n_w = len(kinds)
    me.barrier()
    for j in range(n_w):
        gather.first_hop(j)
    gather.start_z(0)
    tokens.start()
    packs.start()
    gather.wait_z(0)
    for step in range(me.bits):
        if step > 0:
            gather.wait_bits(0, step - 1)
        gather.start_bits(0, step)
    tokens.pass_on()
    gather.start_z(1)

    def on_the_way():
        for j in range(1, n_w):
            gather.wait_z(j)
            if j + 1 < n_w:
                gather.start_z(j + 1)
            else:
                cots.start()
            gather.start_bits(j, 0)
            yield
            for step in range(1, me.bits):
                gather.wait_bits(j, step - 1)
                gather.start_bits(j, step)
                yield

    events = on_the_way()
    tokens.ready()
    packs.ready()

    block = tok.shape[1]
    rows = block * nz
    width = tok.shape[2]
    lanes = 2 * HEAD
    lane = lax.broadcasted_iota(jnp.int32, (block, lanes), 1)
    low = lane < HEAD
    one = jnp.where(lane == HEAD, 1.0, 0.0)
    ones = jnp.where((lane >= HEAD) & (lane < HEAD + 3), 1.0, 0.0)

    @pl.loop(0, nz)
    def _(t):
        x = tok[t].astype(F32)
        mean = jnp.sum(x, axis=1, keepdims=True) * (1.0 / width)
        x = x - mean
        var = jnp.sum(x * x, axis=1, keepdims=True) * (1.0 / width)
        x = x * lax.rsqrt(var + EPS)
        normed[pl.ds(pl.multiple_of(t * block, block), block), :] = (x * gain_ref[...] + bias_ref[...]).astype(BF16)

    gather.wait_bits(0, me.bits - 1)
    pairs = mix_ref.shape[1] // lanes
    sub = pairs // 2

    def project(g):
        at = (g // sub) * (3 * sub) + g % sub

        def column(part):
            return w_qkv[:, (at + part * sub) * lanes : (at + part * sub + 1) * lanes]

        q_bias = pack[g // sub, g % sub : g % sub + 1, :]
        v_bias = pack[g // sub, sub + g % sub : sub + g % sub + 1, :]

        @pl.loop(0, nz)
        def _(t):
            here = pl.ds(pl.multiple_of(t * block, block), block)
            x = normed[here, :]
            both = matmul(x, jnp.concatenate([column(0), column(1)], axis=1))
            tables = (cos_ref[here, :], up_ref[here, :], down_ref[here, :])
            query = _turn(both[:, :lanes] + q_bias, *tables) * (SCALE * LOG2E)
            key = _turn(both[:, lanes:], *tables)
            value = matmul(x, column(2)) + v_bias
            mask = base[here, :].astype(F32)
            for h in range(2):
                if h:
                    query, key, value = (pltpu.roll(v, HEAD, 1) for v in (query, key, value))
                qa_ref[2 * g + h, here, :] = jnp.where(low, query, one).astype(BF16)
                ka_ref[2 * g + h, here, :] = jnp.where(low, key, mask).astype(BF16)
                va_ref[2 * g + h, here, :] = jnp.where(low, value, ones).astype(BF16)

        rest = pl.ds(rows, KEYS - rows)
        for h in range(2):
            qa_ref[2 * g + h, rest, :] = jnp.zeros((KEYS - rows, lanes), BF16)
            va_ref[2 * g + h, rest, :] = jnp.zeros((KEYS - rows, lanes), BF16)
            ka_ref[2 * g + h, rest, :] = base[rest, :]

    def attend(g):
        @pl.loop(0, nz)
        def _(t):
            here = pl.ds(pl.multiple_of(t * block, block), block)
            outs = []
            for h in range(2):
                q = qa_ref[2 * g + h, here, :]
                s = matmul_right_t(q, ka_ref[2 * g + h])
                top = jnp.max(s, axis=1, keepdims=True)
                p = jnp.exp2(s - top).astype(BF16)
                o = matmul(p, va_ref[2 * g + h])
                total = o[:, HEAD : HEAD + 1]
                outs.append(o / total)
                log = -(top + jnp.log2(total))
                first = log.astype(BF16)
                left = log - first.astype(F32)
                second = left.astype(BF16)
                third = (left - second.astype(F32)).astype(BF16)
                logs = jnp.where(
                    lane == HEAD + 1,
                    first.astype(F32),
                    jnp.where(lane == HEAD + 2, second.astype(F32), third.astype(F32)),
                )
                inside = (lane > HEAD) & (lane <= HEAD + 3)
                qa_ref[2 * g + h, here, :] = jnp.where(inside, logs, q.astype(F32)).astype(BF16)
            mix_ref[here, g * lanes : (g + 1) * lanes] = jnp.where(
                low, outs[0], pltpu.roll(outs[1], HEAD, 1)
            ).astype(BF16)

    next(events, None)
    for g in range(pairs):
        project(g)
        next(events, None)
        attend(g)
        next(events, None)
    for _ in events:
        pass
    cots.pass_on()
    for j in range(1, n_w):
        gather.wait_bits(j, me.bits - 1)
    cots.ready()
    for j in range(n_w):
        gather.finish(j)
    tokens.finish()
    cots.finish()
    packs.finish()


def front(tokens, cotangent, pack, base, weights, kinds, gain, bias, tables, n_head, sizes, cid):
    nz = sizes[1]
    block, width = tokens.shape[1:]
    rows = block * nz
    lanes = 2 * HEAD
    heads = 2 * n_head // HEAD
    hbm = pl.BlockSpec(memory_space=pltpu.HBM)
    vmem = pl.BlockSpec(memory_space=pltpu.VMEM)
    shape = jax.ShapeDtypeStruct
    weights = [k.enter(w) for k, w in zip(kinds, weights)]
    shapes = [
        shape((nz, block, width), BF16),
        shape((nz, block, width), BF16),
        shape((2,) + pack.shape, F32),
        shape(base.shape, BF16),
        *[shape(k.whole, BF16) for k in kinds],
        shape((rows, width), BF16),
        *[shape((heads, KEYS, lanes), BF16)] * 3,
        shape((rows, heads * HEAD), BF16),
    ]
    out = pl.pallas_call(
        functools.partial(front_kernel, kinds, sizes),
        out_shape=shapes,
        in_specs=[hbm] * 9 + [vmem] * 5,
        out_specs=[vmem, hbm, vmem, vmem, vmem, hbm, hbm, hbm, hbm] + [vmem] * 5,
        scratch_shapes=Gather.semaphores(len(kinds), sizes)
        + Inward.semaphores(sizes)
        + Inward.semaphores(sizes)
        + Packs.semaphores(sizes),
        compiler_params=pltpu.CompilerParams(
            collective_id=cid, has_side_effects=True, vmem_limit_bytes=48 * 2**20
        ),
        name="front",
    )(tokens, cotangent, pack, base, *weights, gain[None], bias[None], *tables)
    return out[:4], [k.join(w) for k, w in zip(kinds, out[4:9])], out[9:]


def back_kernel(
    kinds, sizes, n_late,
    out_in, g_d, g_g, g_u, g_o, qa_in, ka_in, va_in, do_in, mix_in, normed_in, w_in, x_in, dmid_in,
    cos_ref, up_ref, down_ref, gain_ref, vec_ref,
    out_rows, in_rows, vec_out, s_d, s_g, s_u, s_o, s_qkv,
    *rest,
):
    me = Place(*sizes)
    nz, bits = me.nz, me.bits
    n_w = len(kinds)
    keep = rest[: n_w - 1] + (None,)
    rest = rest[n_w - 1 :]
    got, gotz, stage = (rest[i * n_w : (i + 1) * n_w] for i in range(3))
    rest = rest[3 * n_w :]
    v_sum, v_got, v_all = rest[:3]
    (qa, ka, va, do, mix, normed, w, x_ref, dmid, d_qkv, g_qkv, part, theirs, da, dq, dk, dv, dgain, dshift) = rest[3:22]
    sems = rest[22:]
    scatter = Scatter(
        me, kinds, (g_d, g_g, g_u, g_o, g_qkv), keep, got, gotz, stage, (s_d, s_g, s_u, s_o, s_qkv), sems[:7]
    )
    sums = Sums(me, v_sum, v_got, v_all, vec_out, sems[7:13])
    outs = Outward(me, out_in, out_rows, sems[13:16])
    ins = Outward(me, theirs, in_rows, sems[16:19])
    pair_sem, late_sem, tile_sem, p_send, p_recv = sems[19:24]

    block, width = x_ref.shape[1:]
    rows = block * nz
    lanes = 2 * HEAD
    pairs = mix_in.shape[1] // lanes
    sub = pairs // 2
    lane = lax.broadcasted_iota(jnp.int32, (block, lanes), 1)
    low = lane < HEAD

    def loads(g):
        slot = g % 2
        heads = pl.ds(2 * g, 2)
        cols = pl.ds(g * lanes, lanes)
        return [
            pltpu.make_async_copy(qa_in.at[heads], qa.at[slot], pair_sem.at[slot, 0]),
            pltpu.make_async_copy(ka_in.at[heads], ka.at[slot], pair_sem.at[slot, 1]),
            pltpu.make_async_copy(va_in.at[heads], va.at[slot], pair_sem.at[slot, 2]),
            pltpu.make_async_copy(do_in.at[:, cols], do.at[slot], pair_sem.at[slot, 3]),
            pltpu.make_async_copy(mix_in.at[:, cols], mix.at[slot], pair_sem.at[slot, 4]),
        ]

    late = [
        pltpu.make_async_copy(normed_in, normed, late_sem.at[0]),
        pltpu.make_async_copy(w_in, w, late_sem.at[1]),
    ]

    def tile_loads(t):
        slot = t % 2
        return [
            pltpu.make_async_copy(x_in.at[t], x_ref.at[slot], tile_sem.at[slot, 0]),
            pltpu.make_async_copy(dmid_in.at[t], dmid.at[slot], tile_sem.at[slot, 1]),
        ]

    me.barrier()
    scatter.start(0, 0)
    for copy in loads(0):
        copy.start()
    for place in range(nz):
        outs.start(place)
    for copy in late:
        copy.start()
    for t in range(2):
        for copy in tile_loads(t):
            copy.start()
    v_sum[0] = vec_ref[...]

    def on_the_way():
        for j in range(n_w - 1):
            for step in range(bits):
                scatter.add(j, step)
                if step + 1 < bits:
                    scatter.start(j, step + 1)
                else:
                    scatter.start_z(j)
                if step == 0 and j + 1 < n_w - 1:
                    scatter.start(j + 1, 0)
                yield
            if j > 0:
                scatter.end_z(j - 1)
                yield
        scatter.end_z(n_w - 2)
        yield

    events = on_the_way()

    def head(g, h):
        slot = g % 2

        @pl.loop(0, nz)
        def _(t):
            here = pl.ds(pl.multiple_of(t * block, block), block)
            d = do[slot, here, :].astype(F32)
            mine = low if h == 0 else jnp.logical_not(low)
            delta = -jnp.sum(
                jnp.where(mine, d * mix[slot, here, :].astype(F32), 0.0), axis=1, keepdims=True
            )
            if h:
                d = pltpu.roll(d, HEAD, 1)
            first = delta.astype(BF16)
            left = delta - first.astype(F32)
            second = left.astype(BF16)
            third = (left - second.astype(F32)).astype(BF16)
            logs = jnp.where(
                lane == HEAD,
                first.astype(F32),
                jnp.where(lane == HEAD + 1, second.astype(F32), third.astype(F32)),
            )
            da[here, :] = jnp.where(low, d, jnp.where(lane < HEAD + 3, logs, 0.0)).astype(BF16)

        dk[h] = jnp.zeros((KEYS, lanes), F32)
        dv[h] = jnp.zeros((KEYS, lanes), F32)

        @pl.loop(0, KEYS // COLS)
        def _(t):
            here = pl.ds(pl.multiple_of(t * COLS, COLS), COLS)
            q = qa[slot, h, here, :]
            d = da[here, :]
            p = jnp.exp2(matmul_right_t(ka[slot, h], q))
            ds = (p * matmul_right_t(va[slot, h], d)).astype(BF16)
            dv[h] += matmul(p.astype(BF16), d)
            dk[h] += matmul(ds, q)
            dq[h, here, :] = matmul_left_t(ds, ka[slot, h])

    def put(g, part_of, row, ref, factor, turn):
        at = ((g // sub) * (3 * sub) + part_of * sub + g % sub) * lanes

        def one(t, total):
            here = pl.ds(pl.multiple_of(t * block, block), block)
            value = jnp.where(low, ref[0, here, :], pltpu.roll(ref[1, here, :], HEAD, 1))
            if factor is not None:
                value = value * factor
            if turn:
                value = _turn(value, cos_ref[here, :], -up_ref[here, :], -down_ref[here, :])
            d_qkv[here, at : at + lanes] = value.astype(BF16)
            return total + jnp.sum(value, axis=0, keepdims=True)

        total = lax.fori_loop(0, nz, one, jnp.zeros((1, lanes), F32))
        if row is not None:
            v_sum[0, row : row + 1, :] = total

    da[pl.ds(rows, KEYS - rows), :] = jnp.zeros((KEYS - rows, lanes), BF16)

    def weight_gradient(slot):
        chunk = kinds[-1].two[0]
        columns = pl.ds(slot * 3 * sub * lanes, 3 * sub * lanes)
        grad = d_qkv[:, slot * 3 * sub * lanes : (slot + 1) * 3 * sub * lanes]
        step = max(chunk, lanes)
        for c in range(width // step):
            left = normed[:, c * step : (c + 1) * step]
            g_qkv[c * step : (c + 1) * step, columns] = matmul_left_t(left, grad).astype(BF16)

    for g in range(pairs):
        for copy in loads(g):
            copy.wait()
        if g + 1 < pairs:
            for copy in loads(g + 1):
                copy.start()
        for h in range(2):
            head(g, h)
            next(events, None)
        base_row = n_late + (g // sub) * (2 * sub) + g % sub
        put(g, 0, base_row, dq, SCALE, True)
        put(g, 1, None, dk, LN2, True)
        put(g, 2, base_row + sub, dv, None, False)
        if g == 0:
            for copy in late:
                copy.wait()
        if g % sub == sub - 1:
            weight_gradient(g // sub)
        next(events, None)

    def swap(t):
        return remote(part.at[t], theirs.at[t], p_send.at[t], p_recv.at[t], me.across())

    for t in range(nz):
        here = slice(t * block, (t + 1) * block)
        part[t] = matmul_right_t(d_qkv[here, :], w[...]).astype(BF16)
        swap(t).start()
    for _ in range(2):
        next(events, None)
    dgain[...] = jnp.zeros_like(dgain)
    dshift[...] = jnp.zeros_like(dshift)
    for t in range(nz):
        for copy in tile_loads(t):
            copy.wait()
        x = x_ref[t % 2].astype(F32)
        x = x - jnp.sum(x, axis=1, keepdims=True) * (1.0 / width)
        var = jnp.sum(x * x, axis=1, keepdims=True) * (1.0 / width)
        scale = lax.rsqrt(var + EPS)
        x = x * scale
        swap(t).wait_recv()
        dn = part[t].astype(F32) + theirs[t].astype(F32)
        dgain[...] += jnp.sum(dn * x, axis=0, keepdims=True)
        dshift[...] += jnp.sum(dn, axis=0, keepdims=True)
        v = dn * gain_ref[...]
        mean = jnp.sum(v, axis=1, keepdims=True) * (1.0 / width)
        along = jnp.sum(v * x, axis=1, keepdims=True) * (1.0 / width)
        theirs[t] = (dmid[t % 2] + scale * (v - mean - x * along)).astype(BF16)
        ins.start(t)
        if t + 2 < nz:
            for copy in tile_loads(t + 2):
                copy.start()
    per = width // lanes
    for i in range(per):
        v_sum[0, i : i + 1, :] = dgain[:, i * lanes : (i + 1) * lanes]
        v_sum[0, per + i : per + i + 1, :] = dshift[:, i * lanes : (i + 1) * lanes]
    small = sums.phases()
    next(small, None)
    started = False
    for _ in events:
        next(small, None)
    last = n_w - 1
    scatter.start(last, 0)
    for step in range(bits):
        next(small, None)
        scatter.add(last, step)
        if step + 1 < bits:
            scatter.start(last, step + 1)
        else:
            scatter.start_z(last)
    for _ in small:
        pass
    scatter.end_z(last)
    for t in range(nz):
        swap(t).wait_send()
    outs.finish()
    ins.finish()
    for j in range(n_w):
        scatter.finish(j)


def back(out_act, grads, heads, d_mixed, mixed, normed, w, x, dmid, tables, gain, vec, kinds, n_late, sizes, cid):
    n_dp, nz = sizes
    chips = n_dp // 2
    n_w = len(kinds)
    block, width = x.shape[1:]
    rows = block * nz
    lanes = 2 * HEAD
    hbm = pl.BlockSpec(memory_space=pltpu.HBM)
    vmem = pl.BlockSpec(memory_space=pltpu.VMEM)
    shape = jax.ShapeDtypeStruct
    dma = pltpu.SemaphoreType.DMA
    grads = [k.cut(g) for k, g in zip(kinds, grads)]
    out = pl.pallas_call(
        functools.partial(back_kernel, kinds, sizes, n_late),
        out_shape=[shape((nz // 2, block, width), BF16)] * 2
        + [shape((2,) + vec.shape, F32)]
        + [shape(k.shard, F32) for k in kinds],
        in_specs=[hbm] * 14 + [vmem] * 5,
        out_specs=[hbm, hbm] + [vmem] * (1 + n_w),
        scratch_shapes=[pltpu.VMEM((2, chips // 2) + k.two, BF16) for k in kinds[:-1]]
        + [pltpu.VMEM((chips - 1, 2) + k.two, BF16) for k in kinds]
        + [pltpu.VMEM((nz - 1,) + k.two, BF16) for k in kinds]
        + [pltpu.VMEM(k.shard, F32) for k in kinds]
        + Sums.scratch(vec.shape, sizes)
        + [pltpu.VMEM((2, 2, KEYS, lanes), BF16)] * 3
        + [pltpu.VMEM((2, rows, lanes), BF16)] * 2
        + [
            pltpu.VMEM((rows, width), BF16),
            pltpu.VMEM(w.shape, BF16),
            pltpu.VMEM((2, block, width), BF16),
            pltpu.VMEM((2, block, width), F32),
            pltpu.VMEM((rows, w.shape[1]), BF16),
            pltpu.VMEM((width, w.shape[1]), BF16),
            pltpu.VMEM((nz, block, width), BF16),
            pltpu.VMEM((nz, block, width), BF16),
            pltpu.VMEM((KEYS, lanes), BF16),
        ]
        + [pltpu.VMEM((2, KEYS, lanes), F32)] * 3
        + [pltpu.VMEM((1, width), F32)] * 2
        + Scatter.semaphores(n_w, sizes)
        + Sums.semaphores(sizes)
        + Outward.semaphores(sizes)
        + Outward.semaphores(sizes)
        + [dma((2, 5)), dma((2,)), dma((2, 2)), dma((nz,)), dma((nz,))],
        compiler_params=pltpu.CompilerParams(
            collective_id=cid, has_side_effects=True, vmem_limit_bytes=62 * 2**20
        ),
        name="back",
    )(out_act, *grads, *heads, d_mixed, mixed, normed, w, x, dmid, *tables, gain[None], vec)
    return out[:2], out[2], [k.leave(g) for k, g in zip(kinds, out[3:])]


def shards(
    tokens_in, cotangent, image_flag, key_mask, column_mask,
    attention_norm_gain, attention_norm_bias, w_query, w_key, w_value, query_bias, value_bias, w_out, out_bias,
    feedforward_norm_gain, feedforward_norm_bias, w_gate, gate_bias, w_up, up_bias, inner_gain, inner_shift,
    w_down, down_bias,
):
    n_dp, n_tensor = lax.axis_size("dp"), lax.axis_size("tensor")
    sizes = (n_dp, n_tensor)
    dp, z = lax.axis_index("dp"), lax.axis_index("tensor")
    core = dp % 2
    block = tokens_in.shape[1]
    width = tokens_in.shape[2]
    length = block * n_tensor
    block_pad = up_to(block, 16)
    rows = block_pad * n_tensor
    n_head = w_query.shape[1]
    n_ff = w_gate.shape[1]
    ff = up_to(n_ff, 16)
    count_live = float(FF - PADCOLS)
    swap = [(i, (i // n_tensor ^ 1) * n_tensor + i % n_tensor) for i in range(n_dp * n_tensor)]

    def other(value):
        return lax.ppermute(value, ("dp", "tensor"), swap)

    shard_qkv = jnp.concatenate([w_query, w_key, w_value], axis=1)
    kind_qkv = Kind(True, shard_qkv.shape, n_dp)
    kind_o = Kind(False, w_out.shape, n_dp)
    kind_f = Kind(False, (ff, w_down.shape[1]), n_dp)

    def pad_ff(vec):
        return jnp.pad(vec, (0, ff - n_ff))

    def turned(weight):
        return jnp.pad(weight.T, ((0, ff - n_ff), (0, 0)))

    def pad_rows(value):
        return jnp.pad(value, ((0, 0), (0, block_pad - block), (0, 0)))

    small = jnp.concatenate(
        [query_bias, value_bias]
        + [pad_ff(v) for v in (gate_bias, up_bias, inner_gain, inner_shift, column_mask.astype(F32))]
    )
    small_rows = up_to(up_to(small.shape[0], LANES) // LANES, 8)
    small = jnp.pad(small, (0, small_rows * LANES - small.shape[0])).reshape(small_rows, LANES)
    own_image = z % (n_tensor // 2)
    live = lax.dynamic_index_in_dim(key_mask, own_image, 0, False)
    live = jnp.pad(live.reshape(n_tensor, block), ((0, 0), (0, block_pad - block))).reshape(rows)
    live = jnp.pad(live, (0, KEYS - rows))
    lane = jnp.arange(LANES)[None, :]
    base = jnp.where(
        lane == HEAD,
        jnp.where(live > 0, 0.0, -1e30)[:, None],
        jnp.where(
            (lane > HEAD) & (lane <= HEAD + 3),
            1.0,
            jnp.where(lane == LANES - 1, lax.dynamic_index_in_dim(image_flag, own_image, 0, False).astype(F32), 0.0),
        ),
    ).astype(BF16)
    tables = lane_tables(length, HEAD // 4, block, block_pad)

    (image, cot, packs, base), full, (normed, qa, ka, va, mixed) = front(
        pad_rows(tokens_in),
        pad_rows(cotangent),
        small,
        base,
        [shard_qkv, w_out, turned(w_gate), turned(w_up), jnp.pad(w_down, ((0, ff - n_ff), (0, 0)))],
        [kind_qkv, kind_o, kind_f, kind_f, kind_f],
        attention_norm_gain,
        attention_norm_bias,
        tables,
        n_head,
        sizes,
        0,
    )
    full_qkv, full_o, full_g, full_u, full_d = full
    packs = packs.reshape(2, -1)
    cuts = [n_head] * 2 + [ff] * 5
    parts, at = [], 0
    for size in cuts:
        parts.append(packs[:, at : at + size].reshape(-1))
        at += size
    _, _, g_bias, u_bias, gain, shift, columns = parts
    flag = base[0, LANES - 1].astype(F32)
    token_rows = image.reshape(rows, width).astype(F32)
    xhat1, s1 = norm_pieces(token_rows)
    part = matmul(mixed, full_o).astype(BF16)
    middle = token_rows + (part.astype(F32) + other(part).astype(F32)) + out_bias
    xhat2, s2 = norm_pieces(middle)
    normed2 = (xhat2 * feedforward_norm_gain + feedforward_norm_bias).astype(BF16)
    gate = matmul_right_t(normed2, full_g) + g_bias
    up = matmul_right_t(normed2, full_u) + u_bias
    sig = jax.nn.sigmoid(gate)
    act = gate * sig * up
    sums = jnp.stack([jnp.sum(act * columns, axis=-1), jnp.sum(act * act * columns, axis=-1)])
    sums = sums + other(sums)
    mean = sums[0][:, None] / count_live
    var = sums[1][:, None] / count_live - mean * mean
    r = lax.rsqrt(var + EPS)
    nhat = (act - mean) * r
    hidden = (columns * (nhat * gain + shift)).astype(BF16)
    part = matmul(hidden, full_d).astype(BF16)
    output = (middle + (part.astype(F32) + other(part).astype(F32)) + down_bias).astype(BF16)

    grad = cot.reshape(rows, width).astype(F32) * flag
    grad_low = grad.astype(BF16)
    g_down = matmul_left_t(hidden, grad_low).astype(BF16)
    dn = columns * lax.dot_general(
        grad_low, full_d, (((1,), (1,)), ((), ())), preferred_element_type=F32
    )
    g_gain = jnp.sum(dn * nhat, axis=0)
    g_shift = jnp.sum(dn, axis=0)
    dnh = dn * gain
    rsums = jnp.stack([jnp.sum(dnh, axis=-1), jnp.sum(dnh * nhat, axis=-1)])
    rsums = rsums + other(rsums)
    dact = r * (dnh - columns * (rsums[0][:, None] + nhat * rsums[1][:, None]) / count_live)
    dgate = dact * up * sig * (1.0 + gate * (1.0 - sig))
    dup = dact * gate * sig
    g_gate_bias = jnp.sum(dgate, axis=0)
    g_up_bias = jnp.sum(dup, axis=0)
    gate_low = dgate.astype(BF16)
    up_low = dup.astype(BF16)
    g_gate = matmul_left_t(gate_low, normed2).astype(BF16)
    g_up = matmul_left_t(up_low, normed2).astype(BF16)
    part = (matmul(gate_low, full_g) + matmul(up_low, full_u)).astype(BF16)
    dnormed2 = part.astype(F32) + other(part).astype(F32)
    g_mlp_gain = jnp.sum(dnormed2 * xhat2, axis=0)
    g_mlp_shift = jnp.sum(dnormed2, axis=0)
    dmiddle = grad + norm_backward(dnormed2, xhat2, s2, feedforward_norm_gain)
    g_out_bias = jnp.sum(dmiddle, axis=0)
    g_down_bias = jnp.sum(grad, axis=0)
    dmid_low = dmiddle.astype(BF16)
    g_out = matmul_left_t(mixed, dmid_low).astype(BF16)
    d_mixed = matmul_right_t(dmid_low, full_o).astype(BF16)
    early = jnp.concatenate([g_out_bias, g_mlp_gain, g_mlp_shift, g_down_bias])
    late_rows = 2 * width // LANES
    qv_rows = 4 * n_head // LANES
    tall = jnp.concatenate(
        [v.reshape(2, -1) for v in (g_gate_bias, g_up_bias, g_gain, g_shift)], axis=1
    ).reshape(-1)
    vec = jnp.concatenate([jnp.zeros(((late_rows + qv_rows) * LANES,), F32), early, tall])
    vec_rows = up_to(up_to(vec.shape[0], LANES) // LANES, 8)
    vec = jnp.pad(vec, (0, vec_rows * LANES - vec.shape[0])).reshape(vec_rows, LANES)
    (out_rows, in_rows), vec, (s_down, s_gate, s_up, s_out, s_qkv) = back(
        output.reshape(n_tensor, block_pad, width),
        [g_down, g_gate, g_up, g_out],
        [qa, ka, va],
        d_mixed,
        mixed,
        normed,
        full_qkv,
        image,
        dmiddle.reshape(n_tensor, block_pad, width),
        tables,
        attention_norm_gain,
        vec,
        [kind_f, kind_f, kind_f, kind_o, kind_qkv],
        late_rows,
        sizes,
        1,
    )
    out_rows, in_rows = out_rows[:, :block], in_rows[:, :block]
    vec = vec.reshape(2, -1)
    owner = z // (n_tensor // 2)
    mine = lax.dynamic_index_in_dim(vec, owner, 0, False)
    d_at = (late_rows + qv_rows) * LANES
    wide = jnp.concatenate([vec[0, : 2 * width], vec[0, d_at : d_at + 4 * width]]).reshape(6, width)
    qv = lax.dynamic_index_in_dim(mine[late_rows * LANES : d_at].reshape(2, -1), z % (n_tensor // 2), 0, False)
    tall = mine[d_at + 4 * width : d_at + 4 * width + 8 * ff].reshape(2, -1)
    tall = lax.dynamic_index_in_dim(tall, z % (n_tensor // 2), 0, False)
    pieces, at = [qv[:n_head], qv[n_head:]], 0
    for size in [ff] * 4:
        pieces.append(tall[at : at + size])
        at += size
    return (
        out_rows,
        in_rows.astype(F32),
        wide[0],
        wide[1],
        s_qkv[:, :n_head],
        s_qkv[:, n_head : 2 * n_head],
        s_qkv[:, 2 * n_head :],
        pieces[0],
        pieces[1],
        s_out,
        wide[2],
        wide[3],
        wide[4],
        s_gate[:n_ff].T,
        pieces[2][:n_ff],
        s_up[:n_ff].T,
        pieces[3][:n_ff],
        pieces[4][:n_ff],
        pieces[5][:n_ff],
        s_down[:n_ff],
        wide[5],
    )


def solution(mesh):
    act, row, col, vec = P("dp", "tensor", None), P("dp", "tensor"), P("tensor", "dp"), P("tensor")
    in_specs = (
        act, act, P("dp"), P("dp", None), vec, P(), P(), row, row, row, vec, vec, col, P(), P(), P(),
        row, vec, row, vec, vec, vec, col, P(),
    )
    out_specs = (
        act, act, P(), P(), row, row, row, vec, vec, col, P(), P(), P(), row, vec, row, vec, vec, vec, col, P(),
    )
    return jax.shard_map(shards, mesh=mesh, in_specs=in_specs, out_specs=out_specs, check_vma=False)
```

```python
import functools
import math

import jax
import jax.numpy as jnp
import numpy as np
from jax import lax
from jax.experimental import pallas as pl
from jax.experimental.pallas import tpu as pltpu
from jax.sharding import PartitionSpec as P

HEAD = 64
FF = 2736
PADCOLS = 6
GRID = 32
EPS = 1e-06
ROPE_BASE = 10000.0
LANES = 128
MESH = pl.DeviceIdType.MESH
LOG2E = math.log2(math.e)
LN2 = math.log(2.0)
SCALE = HEAD ** (-0.5)
F32 = jnp.float32
BF16 = jnp.bfloat16


def up_to(size, unit):
    return -(-size // unit) * unit


def rotary_tables(length, head):
    quarter = head // 4
    place = np.arange(length, dtype=np.int32)
    inside = (place >= 1) & (place <= GRID * GRID)
    cell = np.maximum(place - 1, 0)
    row_pos = np.where(inside, cell // GRID, 0).astype(np.float32)
    col_pos = np.where(inside, cell % GRID, 0).astype(np.float32)
    freq = ROPE_BASE ** (-np.arange(quarter, dtype=np.float32) / quarter)
    angle = np.concatenate(
        [row_pos[:, None] * freq[None, :], col_pos[:, None] * freq[None, :]], axis=1
    )
    return np.cos(angle), np.sin(angle)


def lane_tables(length, quarter, block, rows_padded):
    cosv, sinv = rotary_tables(length, HEAD)

    def lay(first, second):
        one = np.concatenate(
            [first[:, :quarter], second[:, :quarter], first[:, quarter:], second[:, quarter:]], axis=1
        )
        two = np.concatenate([one, one], axis=1)
        cut = two.reshape(length // block, block, 2 * HEAD)
        return np.pad(cut, ((0, 0), (0, rows_padded - block), (0, 0))).reshape(-1, 2 * HEAD)

    zero = np.zeros_like(sinv)
    return [jnp.asarray(t, F32) for t in (lay(cosv, cosv), lay(-sinv, zero), lay(zero, sinv))]


def norm_pieces(values):
    row_mean = jnp.mean(values, axis=-1, keepdims=True)
    var = jnp.mean(jnp.square(values - row_mean), axis=-1, keepdims=True)
    inverse_scale = lax.rsqrt(var + EPS)
    return ((values - row_mean) * inverse_scale, inverse_scale)


def norm_backward(incoming_gradient, centered_normalized, inverse_scale, norm_gain):
    inner = incoming_gradient * norm_gain
    return inverse_scale * (
        inner
        - jnp.mean(inner, axis=-1, keepdims=True)
        - centered_normalized * jnp.mean(inner * centered_normalized, axis=-1, keepdims=True)
    )


def matmul(left, right):
    return jnp.dot(left, right, preferred_element_type=F32)


def matmul_right_t(left, right):
    return lax.dot_general(left, right, (((1,), (1,)), ((), ())), preferred_element_type=F32)


def matmul_left_t(left, right):
    return lax.dot_general(left, right, (((0,), (0,)), ((), ())), preferred_element_type=F32)


class Kind:
    def __init__(self, by_rows, shard, n_dp):
        self.given = shard
        self.n_dp = n_dp
        self.turn = not by_rows and shard[1] % LANES != 0
        if self.turn:
            shard = (shard[1], up_to(shard[0], LANES))
        self.by_rows = by_rows or self.turn
        self.shard = shard
        a, b = shard
        if self.by_rows:
            self.whole, self.two = (n_dp * a, 2 * b), (2 * a, b)
        else:
            self.whole, self.two = (2 * a, n_dp * b), (a, 2 * b)

    def piece(self, ref, slot, chip):
        a, b = self.shard
        if self.by_rows:
            return ref.at[pl.ds(_mult(chip, 2 * a), 2 * a), pl.ds(_mult(slot, b), b)]
        return ref.at[pl.ds(_mult(slot, a), a), pl.ds(_mult(chip, 2 * b), 2 * b)]

    def half(self, two, core):
        a, b = self.shard
        if self.by_rows:
            return two.at[pl.ds(_mult(core, a), a)]
        return two.at[:, pl.ds(_mult(core, b), b)]

    def one(self, ref, slot, chip, core):
        a, b = self.shard
        if self.by_rows:
            return ref.at[pl.ds(_mult(chip * 2 + core, a), a), pl.ds(_mult(slot, b), b)]
        return ref.at[pl.ds(_mult(slot, a), a), pl.ds(_mult(chip * 2 + core, b), b)]

    def enter(self, shard):
        if not self.turn:
            return shard
        return jnp.pad(shard.T, ((0, 0), (0, self.shard[1] - self.given[0])))

    def leave(self, shard):
        return shard[:, : self.given[0]].T if self.turn else shard

    def join(self, whole):
        if not self.turn:
            return whole
        a, b = self.shard
        whole = whole.reshape(self.n_dp * a, 2, b)[:, :, : self.given[0]]
        return whole.transpose(1, 2, 0).reshape(2 * self.given[0], self.n_dp * a)

    def cut(self, whole):
        if not self.turn:
            return whole
        a, b = self.shard
        whole = whole.reshape(2, self.given[0], self.n_dp * a).transpose(2, 0, 1)
        return jnp.pad(whole, ((0, 0), (0, 0), (0, b - self.given[0]))).reshape(self.whole)


def _mult(index, size):
    return index * size if isinstance(index, int) else pl.multiple_of(index * size, size)


class Place:
    def __init__(self, n_dp, n_tensor):
        self.dp = lax.axis_index("dp")
        self.z = lax.axis_index("tensor")
        self.core = lax.rem(self.dp, 2)
        self.chip = lax.div(self.dp, 2)
        self.nz = n_tensor
        self.chips = n_dp // 2
        self.bits = self.chips.bit_length() - 1
        self.home = self.core == lax.div(self.z, n_tensor // 2)
        self.slot = lax.rem(self.z, n_tensor // 2)

    def flip(self, bit):
        low = lax.rem(lax.div(self.chip, 1 << bit), 2)
        return self.chip + (1 - 2 * low) * (1 << bit)

    def across(self):
        return (self.dp + 1 - 2 * self.core, self.z)

    def beside(self, bit):
        return (self.flip(bit) * 2 + self.core, self.z)

    def shifted(self, by):
        return (self.dp, lax.rem(self.z + by, self.nz))

    def opposite(self):
        return (self.dp, lax.rem(self.z + self.nz // 2, self.nz))

    def neighbour(self):
        return (self.dp, self.z + 1 - 2 * self.slot)

    def barrier(self):
        everyone = [self.across()]
        everyone += [self.shifted(s) for s in range(1, self.nz)]
        everyone += [self.beside(b) for b in range(self.bits)]
        bar = pltpu.get_barrier_semaphore()
        for one in everyone:
            pl.semaphore_signal(bar, inc=1, device_id=one, device_id_type=MESH)
        pl.semaphore_wait(bar, len(everyone))


def remote(src, dst, send, recv, to):
    return pltpu.make_async_remote_copy(
        src_ref=src, dst_ref=dst, send_sem=send, recv_sem=recv, device_id=to, device_id_type=MESH
    )


def flipped(chip, value):
    return lax.bitwise_xor(chip, value)


class Gather:
    def __init__(self, me, kinds, w_in, w_out, sems):
        self.me, self.kinds, self.w_in, self.w_out = me, kinds, w_in, w_out
        self.s_send, self.s_recv, self.z_send, self.z_recv, self.b_send, self.b_recv, self.loc = sems

    @staticmethod
    def semaphores(n_w, sizes):
        dma = pltpu.SemaphoreType.DMA
        bits = (sizes[0] // 2).bit_length() - 1
        most = max(1 << max(bits - 1, 0), 1)
        return [
            dma((n_w,)),
            dma((n_w,)),
            dma((n_w, 2)),
            dma((n_w, 2)),
            dma((n_w, bits, 2, most)),
            dma((n_w, bits, 2, most)),
            dma((n_w,)),
        ]

    def _hop(self, j):
        me = self.me
        mine = self.kinds[j].one(self.w_out[j], me.slot, me.chip, me.core)
        return (
            pltpu.make_async_copy(self.w_in[j], mine, self.loc.at[j]),
            remote(self.w_in[j], mine, self.s_send.at[j], self.s_recv.at[j], me.across()),
        )

    def first_hop(self, j):
        stay, leave = self._hop(j)
        pl.when(self.me.home)(stay.start)
        pl.when(jnp.logical_not(self.me.home))(leave.start)

    def _along(self, j, slot, number, to):
        src = self.kinds[j].piece(self.w_out[j], slot, self.me.chip)
        return remote(src, src, self.z_send.at[j, number], self.z_recv.at[j, slot], to)

    def start_z(self, j):
        me = self.me

        @pl.when(me.home)
        def _():
            stay, leave = self._hop(j)
            stay.wait()
            leave.wait_recv()
            self._along(j, me.slot, 0, me.opposite()).start()
            self._along(j, me.slot, 1, me.neighbour()).start()

    def pass_z(self, j):
        me = self.me

        @pl.when(jnp.logical_not(me.home))
        def _():
            self._along(j, me.slot, 0, me.neighbour()).wait_recv()
            self._along(j, me.slot, 0, me.neighbour()).start()

    def wait_z(self, j):
        self._along(j, 1 - self.me.slot, 0, self.me.neighbour()).wait_recv()

    def _bits(self, j, step, slot):
        me = self.me
        bit = step if slot == 0 else me.bits - 1 - step
        low = 1 if slot == 0 else 1 << (me.bits - step)

        def send(m):
            src = self.kinds[j].piece(self.w_out[j], slot, flipped(me.chip, m * low))
            return remote(
                src, src, self.b_send.at[j, step, slot, m], self.b_recv.at[j, step, slot, m], me.beside(bit)
            )

        return send

    def start_bits(self, j, step):
        for slot in range(2):
            send = self._bits(j, step, slot)
            _each(1 << step, lambda m: send(m).start())

    def wait_bits(self, j, step):
        for slot in range(2):
            send = self._bits(j, step, slot)
            _each(1 << step, lambda m: send(m).wait_recv())

    def finish(self, j):
        me = self.me
        pl.when(jnp.logical_not(me.home))(self._hop(j)[1].wait_send)
        copy = self._along(j, me.slot, 0, me.neighbour())
        copy.wait_send()
        copy = self._along(j, me.slot, 1, me.neighbour())
        pl.when(me.home)(copy.wait_send)
        for step in range(me.bits):
            for slot in range(2):
                send = self._bits(j, step, slot)
                _each(1 << step, lambda m: send(m).wait_send())


class Inward:
    def __init__(self, me, src, dst, sems):
        self.me, self.src, self.dst = me, src, dst
        self.send, self.recv, self.fwd, self.back, self.loc = sems

    @staticmethod
    def semaphores(sizes):
        dma = pltpu.SemaphoreType.DMA
        return [dma((sizes[1],)), dma((sizes[1],)), dma((sizes[1],)), dma((sizes[1],)), dma((1,))]

    def _copy(self, i):
        me = self.me
        target = me.nz // 2 * me.core + i
        return target, remote(
            self.src.at[i], self.dst.at[me.z], self.send.at[i], self.recv.at[me.z], (me.dp, target)
        )

    def _stay(self, i):
        return pltpu.make_async_copy(self.src.at[i], self.dst.at[self.me.z], self.loc.at[0])

    def _onward(self, place):
        slab = self.dst.at[place]
        return remote(slab, slab, self.fwd.at[place], self.back.at[place], self.me.across())

    def start(self):
        for i in range(self.me.nz // 2):
            target, copy = self._copy(i)
            pl.when(target != self.me.z)(copy.start)
            pl.when(target == self.me.z)(self._stay(i).start)

    def pass_on(self):
        me = self.me

        @pl.when(me.home)
        def _():
            for s in range(me.nz):
                place = lax.rem(me.z + s, me.nz)
                if s == 0:
                    self._stay(0).wait()
                else:
                    slab = self.dst.at[place]
                    remote(slab, slab, self.send.at[0], self.recv.at[place], me.across()).wait_recv()
                self._onward(place).start()

    def ready(self):
        for place in range(self.me.nz):
            pl.when(jnp.logical_not(self.me.home))(self._onward(place).wait_recv)

    def finish(self):
        for i in range(self.me.nz // 2):
            target, copy = self._copy(i)
            pl.when(target != self.me.z)(copy.wait_send)
        for place in range(self.me.nz):
            pl.when(self.me.home)(self._onward(place).wait_send)


class Packs:
    def __init__(self, me, src, dst, pair_src, pair_dst, sems):
        self.me, self.src, self.dst, self.pair_src, self.pair_dst = me, src, dst, pair_src, pair_dst
        self.send, self.recv, self.loc = sems

    @staticmethod
    def semaphores(sizes):
        dma = pltpu.SemaphoreType.DMA
        return [dma((sizes[1],)), dma((3,)), dma((2,))]

    def _copy(self, s):
        me = self.me
        return remote(self.src, self.dst.at[me.slot], self.send.at[s], self.recv.at[me.slot], me.shifted(s))

    def _stay(self):
        return pltpu.make_async_copy(self.src, self.dst.at[self.me.slot], self.loc.at[0])

    def _pair(self):
        return (
            pltpu.make_async_copy(self.pair_src, self.pair_dst, self.loc.at[1]),
            remote(self.pair_src, self.pair_dst, self.send.at[0], self.recv.at[2], self.me.across()),
        )

    def start(self):
        @pl.when(self.me.home)
        def _():
            self._stay().start()
            for s in range(1, self.me.nz):
                self._copy(s).start()
            stay, there = self._pair()
            stay.start()
            there.start()

    def ready(self):
        me = self.me
        for slot in range(2):
            row = self.dst.at[slot]
            copy = remote(row, row, self.send.at[0], self.recv.at[slot], me.across())
            pl.when(me.core * (me.nz // 2) + slot != me.z)(copy.wait_recv)
        stay, there = self._pair()

        @pl.when(me.home)
        def _():
            self._stay().wait()
            stay.wait()

        pl.when(jnp.logical_not(me.home))(there.wait_recv)

    def finish(self):
        @pl.when(self.me.home)
        def _():
            for s in range(1, self.me.nz):
                self._copy(s).wait_send()
            self._pair()[1].wait_send()


def _each(count, act):
    if count <= 4:
        for m in range(count):
            act(m)
    else:

        @pl.loop(0, count)
        def _(m):
            act(m)


class Scatter:
    def __init__(self, me, kinds, g_in, keep, got, gotz, stage, g_out, before, sems):
        self.me, self.kinds, self.g_in, self.keep, self.got = me, kinds, g_in, keep, got
        self.before = before
        self.gotz, self.stage, self.g_out = gotz, stage, g_out
        self.b_send, self.b_recv, self.z_send, self.z_recv, self.f_send, self.f_recv, self.loc = sems

    @staticmethod
    def semaphores(n_w, sizes):
        dma = pltpu.SemaphoreType.DMA
        chips = sizes[0] // 2
        bits = chips.bit_length() - 1
        return [
            dma((n_w, bits, 2, chips // 2)),
            dma((n_w, bits, 2, chips // 2)),
            dma((n_w, 2)),
            dma((n_w, 2)),
            dma((n_w,)),
            dma((n_w,)),
            dma((n_w, 2, chips // 2)),
        ]

    def _count(self, step):
        return 1 << (self.me.bits - 1 - step)

    def _base(self, step):
        return sum(self._count(s) for s in range(step))

    def _first(self, j, slot, m, sent):
        bits = self.me.bits
        if slot == 0:
            flip = m + (1 << (bits - 1)) * sent
        else:
            flip = m * 2 + sent
        return self.kinds[j].piece(self.g_in[j], slot, flipped(self.me.chip, flip))

    def _held(self, j, step, slot, m, sent):
        index = m + self._count(step) * sent if slot == 0 else 2 * m + sent
        return self.got[j].at[self._base(step - 1) + index, slot]

    def _copy(self, j, step, slot, m):
        me = self.me
        bit = me.bits - 1 - step if slot == 0 else step
        src = self._first(j, slot, m, 1) if step == 0 else self._held(j, step, slot, m, 1)
        return remote(
            src,
            self.got[j].at[self._base(step) + m, slot],
            self.b_send.at[j, step, slot, m],
            self.b_recv.at[j, step, slot, m],
            me.beside(bit),
        )

    def _came(self, j, slot, m):
        return pltpu.make_async_copy(
            self.before[j][slot].at[m], self.got[j].at[m, slot], self.b_recv.at[j, 0, slot, m]
        )

    def _load(self, j, slot, m):
        return pltpu.make_async_copy(self._first(j, slot, m, 0), self.keep[j].at[slot, m], self.loc.at[j, slot, m])

    def start(self, j, step):
        for slot in range(2):
            if step == 0 and self.before[j] is not None:
                _each(self._count(step), lambda m: self._came(j, slot, m).start())
            else:
                _each(self._count(step), lambda m: self._copy(j, step, slot, m).start())
        if step == 0 and self.keep[j] is not None:
            for slot in range(2):
                _each(self._count(step), lambda m: self._load(j, slot, m).start())

    def add(self, j, step):
        for slot in range(2):

            def one(m):
                if step == 0 and self.before[j] is not None:
                    self._came(j, slot, m).wait()
                else:
                    self._copy(j, step, slot, m).wait_recv()
                if step > 0:
                    mine = self._held(j, step, slot, m, 0)
                elif self.keep[j] is not None:
                    self._load(j, slot, m).wait()
                    mine = self.keep[j].at[slot, m]
                else:
                    mine = self._first(j, slot, m, 0)
                here = self.got[j].at[self._base(step) + m, slot]
                here[...] = (here[...].astype(F32) + mine[...].astype(F32)).astype(BF16)

            _each(self._count(step), one)

    def _last(self, j, slot):
        return self.got[j].at[self._base(self.me.bits - 1), slot]

    def _z(self, j, slot, number, to):
        return remote(
            self._last(j, slot), self.gotz[j].at[number], self.z_send.at[j, number], self.z_recv.at[j, number], to
        )

    def start_z(self, j):
        self._z(j, 1 - self.me.slot, 0, self.me.neighbour()).start()

    def pass_z(self, j):
        me = self.me
        copy = self._z(j, me.slot, 0, me.neighbour())

        @pl.when(jnp.logical_not(me.home))
        def _():
            copy.wait_recv()
            here = self._last(j, me.slot)
            here[...] = (here[...].astype(F32) + self.gotz[j][0].astype(F32)).astype(BF16)
            self._z(j, me.slot, 1, me.opposite()).start()

    def _hand(self, j):
        return remote(self.stage[j], self.g_out[j], self.f_send.at[j], self.f_recv.at[j], self.me.across())

    def end_z(self, j):
        me = self.me

        @pl.when(me.home)
        def _():
            for number in range(2):
                self._z(j, me.slot, number, me.neighbour()).wait_recv()

            def total(core):
                value = self.kinds[j].half(self._last(j, me.slot), core)[...].astype(F32)
                for number in range(2):
                    value = value + self.kinds[j].half(self.gotz[j].at[number], core)[...].astype(F32)
                return value

            self.stage[j][...] = total(1 - me.core)
            self._hand(j).start()
            self.g_out[j][...] = total(me.core)

    def finish(self, j):
        me = self.me
        for step in range(0 if self.before[j] is None else 1, me.bits):
            for slot in range(2):
                _each(self._count(step), lambda m: self._copy(j, step, slot, m).wait_send())
        self._z(j, 1 - me.slot, 0, me.neighbour()).wait_send()
        far = self._z(j, me.slot, 1, me.opposite())
        pl.when(jnp.logical_not(me.home))(far.wait_send)
        hand = self._hand(j)
        pl.when(me.home)(hand.wait_send)
        pl.when(jnp.logical_not(me.home))(hand.wait_recv)


class Sums:
    def __init__(self, me, v_sum, v_got, v_all, out, sems):
        self.me, self.v_sum, self.v_got, self.v_all, self.out = me, v_sum, v_got, v_all, out
        self.b_send, self.b_recv, self.z_send, self.z_recv, self.f_send, self.f_recv = sems

    @staticmethod
    def semaphores(sizes):
        dma = pltpu.SemaphoreType.DMA
        bits = (sizes[0] // 2).bit_length() - 1
        return [dma((bits,)), dma((bits,)), dma((sizes[1],)), dma((sizes[1],)), dma((1,)), dma((1,))]

    @staticmethod
    def scratch(shape, sizes):
        bits = (sizes[0] // 2).bit_length() - 1
        return [
            pltpu.VMEM((bits + 2,) + shape, F32),
            pltpu.VMEM((bits,) + shape, F32),
            pltpu.VMEM((sizes[1],) + shape, F32),
        ]

    def _bit(self, step):
        return remote(
            self.v_sum.at[step], self.v_got.at[step], self.b_send.at[step], self.b_recv.at[step], self.me.beside(step)
        )

    def _z(self, s):
        me = self.me
        return remote(
            self.v_sum.at[me.bits], self.v_all.at[me.z], self.z_send.at[s], self.z_recv.at[me.z], me.shifted(s)
        )

    def _last(self):
        me = self.me
        return remote(self.v_sum.at[me.bits + 1], self.out.at[me.core], self.f_send.at[0], self.f_recv.at[0], me.across())

    def phases(self):
        me = self.me
        self._bit(0).start()
        yield
        for step in range(1, me.bits + 1):
            self._bit(step - 1).wait_recv()
            self.v_sum[step] = self.v_sum[step - 1] + self.v_got[step - 1]
            if step < me.bits:
                self._bit(step).start()
                yield
        for s in range(1, me.nz):
            self._z(s).start()
        self.v_all[me.z] = self.v_sum[me.bits]
        yield
        for s in range(1, me.nz):
            slab = self.v_all.at[lax.rem(me.z + s, me.nz)]
            place = lax.rem(me.z + s, me.nz)
            remote(slab, slab, self.z_send.at[0], self.z_recv.at[place], me.across()).wait_recv()
        value = self.v_all[0]
        for s in range(1, me.nz):
            value = value + self.v_all[s]
        self.v_sum[me.bits + 1] = value
        self._last().start()
        self.out[me.core] = value
        yield
        there = self.out.at[1 - me.core]
        remote(there, there, self.f_send.at[0], self.f_recv.at[0], me.across()).wait_recv()
        for step in range(me.bits):
            self._bit(step).wait_send()
        for s in range(1, me.nz):
            self._z(s).wait_send()
        self._last().wait_send()


class Outward:
    def __init__(self, me, src, dst, sems):
        self.me, self.src, self.dst = me, src, dst
        self.send, self.recv, self.loc = sems

    @staticmethod
    def semaphores(sizes):
        dma = pltpu.SemaphoreType.DMA
        return [dma((sizes[1],)), dma((2,)), dma((1,))]

    def _copy(self, place):
        me = self.me
        return remote(
            self.src.at[place], self.dst.at[me.slot], self.send.at[place], self.recv.at[me.slot], (me.dp, place)
        )

    def _stay(self, place):
        return pltpu.make_async_copy(self.src.at[place], self.dst.at[self.me.slot], self.loc.at[0])

    def start(self, place):
        me = self.me
        pl.when(jnp.logical_and(me.home, place != me.z))(lambda: self._copy(place).start())
        pl.when(jnp.logical_and(me.home, place == me.z))(lambda: self._stay(place).start())

    def finish(self):
        me = self.me
        for place in range(me.nz):
            pl.when(jnp.logical_and(me.home, place != me.z))(lambda place=place: self._copy(place).wait_send())
            pl.when(jnp.logical_and(me.home, place == me.z))(lambda place=place: self._stay(place).wait())
        for slot in range(2):
            row = self.dst.at[slot]
            copy = remote(row, row, self.send.at[0], self.recv.at[slot], me.across())
            pl.when(me.core * (me.nz // 2) + slot != me.z)(copy.wait_recv)


def send_first(kind, grad, sizes):
    n_dp, nz = sizes
    chips = n_dp // 2
    bits = chips.bit_length() - 1
    chip = lax.axis_index("dp") // 2
    grad = kind.cut(grad)
    a, b = kind.shard
    came = []
    for slot in range(2):
        bit = bits - 1 if slot == 0 else 0
        parts = []
        for m in range(chips // 2):
            there = lax.bitwise_xor(chip, m + (1 << bit) if slot == 0 else 2 * m + 1)
            if kind.by_rows:
                parts.append(lax.dynamic_slice(grad, (there * (2 * a), slot * b), kind.two))
            else:
                parts.append(lax.dynamic_slice(grad, (slot * a, there * (2 * b)), kind.two))
        pairs = [(i, (i // nz ^ (2 << bit)) * nz + i % nz) for i in range(n_dp * nz)]
        came.append(lax.ppermute(jnp.stack(parts), ("dp", "tensor"), pairs))
    return came


KEYS = 1152
TILE = 272
COLS = 384


def _turn(x, cos, sin_up, sin_down):
    quarter = HEAD // 4
    return (
        x * cos
        + pltpu.roll(x, 2 * HEAD - quarter, 1) * sin_up
        + pltpu.roll(x, quarter, 1) * sin_down
    )


def front_kernel(
    kinds, sizes,
    tok_in, cot_in, pack_in, base_in, a_in, b_in, o_in, g_in, u_in, d_in,
    gain_ref, bias_ref, cos_ref, up_ref, down_ref, out_bias, gain2_ref, bias2_ref,
    tok_out, cot, pack, base, a_out, b_out, w_o, w_g, w_u, w_d, normed_out, qa_out, ka_out, va_out, mix_out,
    mid_out, normed2_out, gate_out, up_out, hidden_out, totals,
    tok, w_a, w_b, normed, qa_ref, ka_ref, va_ref, mix_ref, normed2, hidden, done_sem,
    wo_v, wg_v, wu_v, part, theirs, mid_v, gate_v, up_v, act_v, own_sums, their_sums, p_send, p_recv, r_send, r_recv, out_sem, w_sem,
    *sems,
):
    me = Place(*sizes)
    nz = sizes[1]
    gather = Gather(me, kinds, (a_in, b_in, o_in, g_in, u_in, d_in), (w_a, w_b, w_o, w_g, w_u, w_d), sems[:7])
    tokens = Inward(me, tok_in, tok, sems[7:12])
    cots = Inward(me, cot_in, cot, sems[12:17])
    packs = Packs(me, pack_in, pack, base_in, base, sems[17:20])
    n_w = len(kinds)
    leaving = []

    def leave(src, dst):
        copy = pltpu.make_async_copy(src, dst, done_sem.at[len(leaving)])
        copy.start()
        leaving.append(copy)

    me.barrier()
    for j in range(n_w):
        gather.first_hop(j)
    for j in (0, 1, 3, 2):
        gather.start_z(j)
    packs.start()

    def flow(j):
        gather.wait_z(j)
        gather.start_bits(j, 0)
        yield
        for step in range(1, me.bits):
            gather.wait_bits(j, step - 1)
            gather.start_bits(j, step)
        yield

    flows = [flow(j) for j in range(n_w)]
    gather.pass_z(0)
    next(flows[0])
    gather.pass_z(1)
    next(flows[1])
    next(flows[0])
    gather.pass_z(3)
    next(flows[1])
    next(flows[3])
    gather.pass_z(2)
    tokens.start()
    for j in (4, 5):
        gather.start_z(j)
    next(flows[2])
    next(flows[3])
    tokens.pass_on()
    tokens.ready()
    packs.ready()
    gather.pass_z(4)
    next(flows[2])

    block = tok.shape[1]
    rows = block * nz
    width = tok.shape[2]
    lanes = 2 * HEAD
    lane = lax.broadcasted_iota(jnp.int32, (block, lanes), 1)
    low = lane < HEAD
    one = jnp.where(lane == HEAD, 1.0, 0.0)
    ones = jnp.where((lane >= HEAD) & (lane < HEAD + 3), 1.0, 0.0)

    @pl.loop(0, nz)
    def _(t):
        x = tok[t].astype(F32)
        mean = jnp.sum(x, axis=1, keepdims=True) * (1.0 / width)
        x = x - mean
        var = jnp.sum(x * x, axis=1, keepdims=True) * (1.0 / width)
        x = x * lax.rsqrt(var + EPS)
        normed[pl.ds(pl.multiple_of(t * block, block), block), :] = (x * gain_ref[...] + bias_ref[...]).astype(BF16)

    gather.wait_bits(0, me.bits - 1)
    gather.wait_bits(1, me.bits - 1)
    leave(tok, tok_out)
    leave(w_a, a_out)
    leave(w_b, b_out)
    leave(normed, normed_out)
    pairs = mix_ref.shape[1] // lanes
    sub = pairs // 2

    def project(g):
        weight = (w_a, w_b)[g % sub]

        def column(part):
            at = ((g // sub) * 3 + part) * lanes
            return weight[:, at : at + lanes]

        q_bias = pack[g // sub, 0:1, (g % sub) * lanes : (g % sub + 1) * lanes]
        v_bias = pack[g // sub, 1:2, (g % sub) * lanes : (g % sub + 1) * lanes]

        @pl.loop(0, nz)
        def _(t):
            here = pl.ds(pl.multiple_of(t * block, block), block)
            x = normed[here, :]
            both = matmul(x, jnp.concatenate([column(0), column(1)], axis=1))
            tables = (cos_ref[here, :], up_ref[here, :], down_ref[here, :])
            query = _turn(both[:, :lanes] + q_bias, *tables) * (SCALE * LOG2E)
            key = _turn(both[:, lanes:], *tables)
            value = matmul(x, column(2)) + v_bias
            mask = base[here, :].astype(F32)
            for h in range(2):
                if h:
                    query, key, value = (pltpu.roll(v, HEAD, 1) for v in (query, key, value))
                qa_ref[2 * g + h, here, :] = jnp.where(low, query, one).astype(BF16)
                ka_ref[2 * g + h, here, :] = jnp.where(low, key, mask).astype(BF16)
                va_ref[2 * g + h, here, :] = jnp.where(low, value, ones).astype(BF16)

        rest = pl.ds(rows, KEYS - rows)
        for h in range(2):
            qa_ref[2 * g + h, rest, :] = jnp.zeros((KEYS - rows, lanes), BF16)
            va_ref[2 * g + h, rest, :] = jnp.zeros((KEYS - rows, lanes), BF16)
            ka_ref[2 * g + h, rest, :] = base[rest, :]

    def attend(g):
        @pl.loop(0, nz)
        def _(t):
            here = pl.ds(pl.multiple_of(t * block, block), block)
            outs = []
            for h in range(2):
                q = qa_ref[2 * g + h, here, :]
                s = matmul_right_t(q, ka_ref[2 * g + h])
                top = jnp.max(s, axis=1, keepdims=True)
                p = jnp.exp2(s - top).astype(BF16)
                o = matmul(p, va_ref[2 * g + h])
                total = o[:, HEAD : HEAD + 1]
                outs.append(o / total)
                log = -(top + jnp.log2(total))
                first = log.astype(BF16)
                left = log - first.astype(F32)
                second = left.astype(BF16)
                third = (left - second.astype(F32)).astype(BF16)
                logs = jnp.where(
                    lane == HEAD + 1,
                    first.astype(F32),
                    jnp.where(lane == HEAD + 2, second.astype(F32), third.astype(F32)),
                )
                inside = (lane > HEAD) & (lane <= HEAD + 3)
                qa_ref[2 * g + h, here, :] = jnp.where(inside, logs, q.astype(F32)).astype(BF16)
            mix_ref[here, g * lanes : (g + 1) * lanes] = jnp.where(
                low, outs[0], pltpu.roll(outs[1], HEAD, 1)
            ).astype(BF16)

        for src, dst in ((qa_ref, qa_out), (ka_ref, ka_out), (va_ref, va_out)):
            leave(src.at[pl.ds(2 * g, 2)], dst.at[pl.ds(2 * g, 2)])

    project(0)
    next(flows[4])
    gather.pass_z(5)
    attend(0)
    next(flows[5])
    project(1)
    attend(1)
    next(flows[4])
    project(2)
    attend(2)
    next(flows[5])
    cots.start()
    project(3)
    attend(3)

    def load(j, there):
        gather.wait_bits(j, me.bits - 1)
        copy = pltpu.make_async_copy(gather.w_out[j], there, w_sem.at[j])
        copy.start()
        return copy

    def swap(t):
        return remote(part.at[t], theirs.at[t], p_send.at[t], p_recv.at[t], me.across())

    def swap_sums(t):
        return remote(own_sums.at[t], their_sums.at[t], r_send.at[t], r_recv.at[t], me.across())

    def save(t):
        slot = t % 2
        return [
            pltpu.make_async_copy(mid_v.at[slot], mid_out.at[t], out_sem.at[0, slot]),
            pltpu.make_async_copy(gate_v.at[slot], gate_out.at[t], out_sem.at[1, slot]),
            pltpu.make_async_copy(up_v.at[slot], up_out.at[t], out_sem.at[2, slot]),
        ]

    leave(mix_ref, mix_out)
    loads = [load(2, wo_v), load(3, wg_v)]
    loads[0].wait()
    for t in range(nz):
        mixed = mix_ref[t * block : (t + 1) * block, :]
        product = matmul_right_t(mixed, wo_v[...]) if kinds[2].turn else matmul(mixed, wo_v[...])
        part[t] = product.astype(BF16)
        swap(t).start()

    ff = hidden.shape[1] // 2
    wide = up_to(ff, LANES)
    place = lax.broadcasted_iota(jnp.int32, (1, 2 * wide), 1)

    def row(n):
        blank = jnp.zeros((1, wide), F32)
        first = jnp.concatenate([pack[0, n : n + 1, :wide], blank], axis=1)
        second = jnp.concatenate([pack[1, n : n + 1, :wide], blank], axis=1)
        return jnp.where(place < ff, first, pltpu.roll(second, ff, 1))[:, : 2 * ff]

    g_bias, u_bias, inner_gain, inner_shift, columns = (row(n) for n in range(2, 7))
    count = float(FF - PADCOLS)

    def finish_tile(t):
        slot = t % 2
        swap_sums(t).wait_recv()
        total = own_sums[t] + their_sums[t]
        totals[t] = total
        mean = total[:, 0:1] / count
        var = total[:, 1:2] / count - mean * mean
        nhat = (act_v[slot] - mean) * lax.rsqrt(var + EPS)
        here = pl.ds(t * block, block)
        hidden[here, :] = (columns * (nhat * inner_gain + inner_shift)).astype(BF16)
        leave(hidden.at[here], hidden_out.at[here])
        leave(normed2.at[here], normed2_out.at[here])

    for t in range(nz):
        slot = t % 2
        if t >= 2:
            for copy in save(t - 2):
                copy.wait()
        swap(t).wait_recv()
        x = tok[t].astype(F32) + (part[t].astype(F32) + theirs[t].astype(F32)) + out_bias[...]
        mid_v[slot] = x
        x = x - jnp.sum(x, axis=1, keepdims=True) * (1.0 / width)
        var = jnp.sum(x * x, axis=1, keepdims=True) * (1.0 / width)
        x = (x * lax.rsqrt(var + EPS) * gain2_ref[...] + bias2_ref[...]).astype(BF16)
        normed2[t * block : (t + 1) * block, :] = x
        if t == 0:
            loads.append(load(4, wu_v))
            loads[1].wait()
        gate = (matmul(x, wg_v[...]) if kinds[3].turn else matmul_right_t(x, wg_v[...])) + g_bias
        gate_v[slot] = gate
        if t == 0:
            loads[2].wait()
        up = (matmul(x, wu_v[...]) if kinds[4].turn else matmul_right_t(x, wu_v[...])) + u_bias
        up_v[slot] = up
        gate = gate_v[slot]
        act = gate * (1.0 / (1.0 + jnp.exp(-gate))) * up
        act_v[slot] = act
        live = act * columns
        first = jnp.sum(live, axis=1, keepdims=True)
        second = jnp.sum(live * act, axis=1, keepdims=True)
        own_sums[t] = jnp.where(lane == 0, first, jnp.where(lane == 1, second, 0.0))
        swap_sums(t).start()
        for copy in save(t):
            copy.start()
        if t >= 1:
            finish_tile(t - 1)
    finish_tile(nz - 1)
    cots.pass_on()
    for t in range(nz - 2, nz):
        for copy in save(t):
            copy.wait()
    gather.wait_bits(5, me.bits - 1)
    for copy in leaving:
        copy.wait()
    for t in range(nz):
        swap(t).wait_send()
        swap_sums(t).wait_send()
    cots.ready()
    for j in range(n_w):
        gather.finish(j)
    tokens.finish()
    cots.finish()
    packs.finish()


def front(tokens, cotangent, pack, base, weights, kinds, gain, bias, tables, more, n_head, ff, sizes, cid):
    nz = sizes[1]
    block, width = tokens.shape[1:]
    rows = block * nz
    lanes = 2 * HEAD
    heads = 2 * n_head // HEAD
    hbm = pl.BlockSpec(memory_space=pltpu.HBM)
    vmem = pl.BlockSpec(memory_space=pltpu.VMEM)
    shape = jax.ShapeDtypeStruct
    weights = [k.enter(w) for k, w in zip(kinds, weights)]
    shapes = [
        shape((nz, block, width), BF16),
        shape((nz, block, width), BF16),
        shape((2,) + pack.shape, F32),
        shape(base.shape, BF16),
        *[shape(k.whole, BF16) for k in kinds],
        shape((rows, width), BF16),
        *[shape((heads, KEYS, lanes), BF16)] * 3,
        shape((rows, heads * HEAD), BF16),
        shape((nz, block, width), F32),
        shape((rows, width), BF16),
        shape((nz, block, 2 * ff), F32),
        shape((nz, block, 2 * ff), F32),
        shape((rows, 2 * ff), BF16),
        shape((nz, block, lanes), F32),
    ]
    dma = pltpu.SemaphoreType.DMA
    out = pl.pallas_call(
        functools.partial(front_kernel, kinds, sizes),
        out_shape=shapes,
        in_specs=[hbm] * 10 + [vmem] * 8,
        out_specs=[hbm, hbm, vmem, vmem] + [hbm] * 16 + [vmem],
        scratch_shapes=[
            pltpu.VMEM((nz, block, width), BF16),
            pltpu.VMEM(kinds[0].whole, BF16),
            pltpu.VMEM(kinds[1].whole, BF16),
            pltpu.VMEM((rows, width), BF16),
            *[pltpu.VMEM((heads, KEYS, lanes), BF16)] * 3,
            pltpu.VMEM((rows, heads * HEAD), BF16),
            pltpu.VMEM((rows, width), BF16),
            pltpu.VMEM((rows, 2 * ff), BF16),
            dma((5 + 3 * heads // 2 + 2 * nz,)),
        ]
        + [pltpu.VMEM(k.whole, BF16) for k in kinds[2:5]]
        + [pltpu.VMEM((nz, block, width), BF16)] * 2
        + [pltpu.VMEM((2, block, width), F32)]
        + [pltpu.VMEM((2, block, 2 * ff), F32)] * 3
        + [pltpu.VMEM((nz, block, lanes), F32)] * 2
        + [dma((nz,)), dma((nz,)), dma((nz,)), dma((nz,)), dma((3, 2)), dma((len(kinds),))]
        + Gather.semaphores(len(kinds), sizes)
        + Inward.semaphores(sizes)
        + Inward.semaphores(sizes)
        + Packs.semaphores(sizes),
        compiler_params=pltpu.CompilerParams(
            collective_id=cid, has_side_effects=True, vmem_limit_bytes=60 * 2**20
        ),
        name="front",
    )(tokens, cotangent, pack, base, *weights, gain[None], bias[None], *tables, *[v[None] for v in more])
    return out[:4], [k.join(w) for k, w in zip(kinds, out[4:10])], out[10:]


def back_kernel(
    kinds, sizes, n_late, n_before,
    out_in, g_d, g_g, g_u, g_o, qa_in, ka_in, va_in, do_in, mix_in, normed_in, wa_in, wb_in, x_in, dmid_in,
    cos_ref, up_ref, down_ref, gain_ref, vec_ref,
    *rest,
):
    me = Place(*sizes)
    nz, bits = me.nz, me.bits
    before = [rest[2 * j : 2 * j + 2] if j < n_before else None for j in range(len(kinds))]
    rest = rest[2 * n_before :]
    out_rows, in_rows, vec_out = rest[:3]
    g_out = rest[3 : 3 + len(kinds)]
    rest = rest[3 + len(kinds) :]
    n_w = len(kinds)
    keep = rest[: n_w - 2] + (None, None)
    rest = rest[n_w - 2 :]
    got, gotz, stage = (rest[i * n_w : (i + 1) * n_w] for i in range(3))
    rest = rest[3 * n_w :]
    v_sum, v_got, v_all = rest[:3]
    (qa, ka, va, do, mix, normed, w, x_ref, dmid, d_qkv, g_a, g_b, part, theirs, da, dq, dk, dv, dgain, dshift) = rest[3:23]
    sems = rest[23:]
    scatter = Scatter(
        me, kinds, (g_d, g_g, g_u, g_o, g_a, g_b), keep, got, gotz, stage, g_out, before, sems[:7]
    )
    sums = Sums(me, v_sum, v_got, v_all, vec_out, sems[7:13])
    outs = Outward(me, out_in, out_rows, sems[13:16])
    ins = Outward(me, theirs, in_rows, sems[16:19])
    pair_sem, late_sem, tile_sem, p_send, p_recv = sems[19:24]

    block, width = x_ref.shape[1:]
    rows = block * nz
    lanes = 2 * HEAD
    pairs = mix_in.shape[1] // lanes
    sub = pairs // 2
    lane = lax.broadcasted_iota(jnp.int32, (block, lanes), 1)
    low = lane < HEAD

    turns = [slot * sub + s for s in range(sub) for slot in range(pairs // sub)]

    def loads(n):
        slot = n % 2
        g = turns[n]
        heads = pl.ds(2 * g, 2)
        cols = pl.ds(g * lanes, lanes)
        return [
            pltpu.make_async_copy(qa_in.at[heads], qa.at[slot], pair_sem.at[slot, 0]),
            pltpu.make_async_copy(ka_in.at[heads], ka.at[slot], pair_sem.at[slot, 1]),
            pltpu.make_async_copy(va_in.at[heads], va.at[slot], pair_sem.at[slot, 2]),
            pltpu.make_async_copy(do_in.at[:, cols], do.at[slot], pair_sem.at[slot, 3]),
            pltpu.make_async_copy(mix_in.at[:, cols], mix.at[slot], pair_sem.at[slot, 4]),
        ]

    late = [
        pltpu.make_async_copy(normed_in, normed, late_sem.at[0]),
        pltpu.make_async_copy(wa_in, w.at[:, pl.ds(0, wa_in.shape[1])], late_sem.at[1]),
        pltpu.make_async_copy(wb_in, w.at[:, pl.ds(wa_in.shape[1], wa_in.shape[1])], late_sem.at[2]),
    ]

    def tile_loads(t):
        slot = t % 2
        return [
            pltpu.make_async_copy(x_in.at[t], x_ref.at[slot], tile_sem.at[slot, 0]),
            pltpu.make_async_copy(dmid_in.at[t], dmid.at[slot], tile_sem.at[slot, 1]),
        ]

    me.barrier()
    for j in range(n_w - 2):
        scatter.start(j, 0)
    for copy in loads(0):
        copy.start()
    for place in range(nz):
        outs.start(place)
    for copy in late:
        copy.start()
    for t in range(2):
        for copy in tile_loads(t):
            copy.start()
    v_sum[0] = vec_ref[...]

    def flow(j):
        for step in range(bits):
            scatter.add(j, step)
            if step + 1 < bits:
                scatter.start(j, step + 1)
            else:
                scatter.start_z(j)
            yield

    flows = [flow(j) for j in range(n_w)]

    def rest_of(j):
        for _ in flows[j]:
            pass

    def head(n, h):
        slot = n % 2

        @pl.loop(0, nz)
        def _(t):
            here = pl.ds(pl.multiple_of(t * block, block), block)
            d = do[slot, here, :].astype(F32)
            mine = low if h == 0 else jnp.logical_not(low)
            delta = -jnp.sum(
                jnp.where(mine, d * mix[slot, here, :].astype(F32), 0.0), axis=1, keepdims=True
            )
            if h:
                d = pltpu.roll(d, HEAD, 1)
            first = delta.astype(BF16)
            left = delta - first.astype(F32)
            second = left.astype(BF16)
            third = (left - second.astype(F32)).astype(BF16)
            logs = jnp.where(
                lane == HEAD,
                first.astype(F32),
                jnp.where(lane == HEAD + 1, second.astype(F32), third.astype(F32)),
            )
            da[here, :] = jnp.where(low, d, jnp.where(lane < HEAD + 3, logs, 0.0)).astype(BF16)

        dk[h] = jnp.zeros((KEYS, lanes), F32)
        dv[h] = jnp.zeros((KEYS, lanes), F32)

        @pl.loop(0, KEYS // COLS)
        def _(t):
            here = pl.ds(pl.multiple_of(t * COLS, COLS), COLS)
            q = qa[slot, h, here, :]
            d = da[here, :]
            p = jnp.exp2(matmul_right_t(ka[slot, h], q))
            ds = (p * matmul_right_t(va[slot, h], d)).astype(BF16)
            dv[h] += matmul(p.astype(BF16), d)
            dk[h] += matmul(ds, q)
            dq[h, here, :] = matmul_left_t(ds, ka[slot, h])

    def put(g, part_of, row, ref, factor, turn):
        at = ((g % sub) * (pairs // sub) * 3 + (g // sub) * 3 + part_of) * lanes

        def one(t, total):
            here = pl.ds(pl.multiple_of(t * block, block), block)
            value = jnp.where(low, ref[0, here, :], pltpu.roll(ref[1, here, :], HEAD, 1))
            if factor is not None:
                value = value * factor
            if turn:
                value = _turn(value, cos_ref[here, :], -up_ref[here, :], -down_ref[here, :])
            d_qkv[here, at : at + lanes] = value.astype(BF16)
            return total + jnp.sum(value, axis=0, keepdims=True)

        total = lax.fori_loop(0, nz, one, jnp.zeros((1, lanes), F32))
        if row is not None:
            v_sum[0, row : row + 1, :] = total

    da[pl.ds(rows, KEYS - rows), :] = jnp.zeros((KEYS - rows, lanes), BF16)

    def weight_gradient(s):
        into = (g_a, g_b)[s]
        columns = into.shape[1]
        grad = d_qkv[:, s * columns : (s + 1) * columns]
        step = max(kinds[-1].two[0], lanes)
        for c in range(width // step):
            left = normed[:, c * step : (c + 1) * step]
            into[c * step : (c + 1) * step, :] = matmul_left_t(left, grad).astype(BF16)

    def fetch(g):
        for copy in loads(g):
            copy.wait()
        if g + 1 < pairs:
            for copy in loads(g + 1):
                copy.start()

    def write(n):
        g = turns[n]
        base_row = n_late + (g // sub) * (2 * sub) + g % sub
        put(g, 0, base_row, dq, SCALE, True)
        put(g, 1, None, dk, LN2, True)
        put(g, 2, base_row + sub, dv, None, False)

    def swap(t):
        return remote(part.at[t], theirs.at[t], p_send.at[t], p_recv.at[t], me.across())

    def partial():
        for t in range(nz):
            here = slice(t * block, (t + 1) * block)
            part[t] = matmul_right_t(d_qkv[here, :], w[...]).astype(BF16)
            swap(t).start()

    def input_gradient():
        dgain[...] = jnp.zeros_like(dgain)
        dshift[...] = jnp.zeros_like(dshift)
        for t in range(nz):
            for copy in tile_loads(t):
                copy.wait()
            x = x_ref[t % 2].astype(F32)
            x = x - jnp.sum(x, axis=1, keepdims=True) * (1.0 / width)
            var = jnp.sum(x * x, axis=1, keepdims=True) * (1.0 / width)
            scale = lax.rsqrt(var + EPS)
            x = x * scale
            swap(t).wait_recv()
            dn = part[t].astype(F32) + theirs[t].astype(F32)
            dgain[...] += jnp.sum(dn * x, axis=0, keepdims=True)
            dshift[...] += jnp.sum(dn, axis=0, keepdims=True)
            v = dn * gain_ref[...]
            mean = jnp.sum(v, axis=1, keepdims=True) * (1.0 / width)
            along = jnp.sum(v * x, axis=1, keepdims=True) * (1.0 / width)
            theirs[t] = (dmid[t % 2] + scale * (v - mean - x * along)).astype(BF16)
            ins.start(t)
            if t + 2 < nz:
                for copy in tile_loads(t + 2):
                    copy.start()
        per = width // lanes
        for i in range(per):
            v_sum[0, i : i + 1, :] = dgain[:, i * lanes : (i + 1) * lanes]
            v_sum[0, per + i : per + i + 1, :] = dshift[:, i * lanes : (i + 1) * lanes]

    fetch(0)
    head(0, 0)
    head(0, 1)
    write(0)
    next(flows[0], None)
    next(flows[1], None)
    fetch(1)
    head(1, 0)
    head(1, 1)
    write(1)
    rest_of(0)
    rest_of(1)
    for copy in late:
        copy.wait()
    weight_gradient(0)
    next(flows[2], None)
    scatter.start(4, 0)
    scatter.pass_z(0)
    scatter.pass_z(1)
    fetch(2)
    head(2, 0)
    next(flows[3], None)
    rest_of(2)
    scatter.end_z(0)
    head(2, 1)
    write(2)
    next(flows[4], None)
    scatter.end_z(1)
    fetch(3)
    head(3, 0)
    rest_of(3)
    scatter.pass_z(2)
    head(3, 1)
    write(3)
    rest_of(4)
    weight_gradient(1)
    scatter.start(5, 0)
    scatter.pass_z(3)
    partial()
    next(flows[5], None)
    scatter.pass_z(4)
    scatter.end_z(2)
    input_gradient()
    rest_of(5)
    small = sums.phases()
    next(small, None)
    scatter.end_z(3)
    next(small, None)
    scatter.pass_z(5)
    scatter.end_z(4)
    for _ in small:
        pass
    scatter.end_z(5)
    for t in range(nz):
        swap(t).wait_send()
    outs.finish()
    ins.finish()
    for j in range(n_w):
        scatter.finish(j)


def back(out_act, grads, before, heads, d_mixed, mixed, normed, weights, x, dmid, tables, gain, vec, kinds, n_late, sizes, cid):
    n_dp, nz = sizes
    chips = n_dp // 2
    n_w = len(kinds)
    block, width = x.shape[1:]
    rows = block * nz
    lanes = 2 * HEAD
    hbm = pl.BlockSpec(memory_space=pltpu.HBM)
    vmem = pl.BlockSpec(memory_space=pltpu.VMEM)
    shape = jax.ShapeDtypeStruct
    dma = pltpu.SemaphoreType.DMA
    grads = [k.cut(g) for k, g in zip(kinds, grads)]
    out = pl.pallas_call(
        functools.partial(back_kernel, kinds, sizes, n_late, len(before)),
        out_shape=[shape((nz // 2, block, width), BF16)] * 2
        + [shape((2,) + vec.shape, F32)]
        + [shape(k.shard, F32) for k in kinds],
        in_specs=[hbm] * 15 + [vmem] * 5 + [hbm] * (2 * len(before)),
        out_specs=[hbm, hbm] + [vmem] * (1 + n_w),
        scratch_shapes=[pltpu.VMEM((2, chips // 2) + k.two, BF16) for k in kinds[:-2]]
        + [pltpu.VMEM((chips - 1, 2) + k.two, BF16) for k in kinds]
        + [pltpu.VMEM((2,) + k.two, BF16) for k in kinds]
        + [pltpu.VMEM(k.shard, F32) for k in kinds]
        + Sums.scratch(vec.shape, sizes)
        + [pltpu.VMEM((2, 2, KEYS, lanes), BF16)] * 3
        + [pltpu.VMEM((2, rows, lanes), BF16)] * 2
        + [
            pltpu.VMEM((rows, width), BF16),
            pltpu.VMEM((width, 2 * weights[0].shape[1]), BF16),
            pltpu.VMEM((2, block, width), BF16),
            pltpu.VMEM((2, block, width), F32),
            pltpu.VMEM((rows, 2 * weights[0].shape[1]), BF16),
            pltpu.VMEM((width, weights[0].shape[1]), BF16),
            pltpu.VMEM((width, weights[0].shape[1]), BF16),
            pltpu.VMEM((nz, block, width), BF16),
            pltpu.VMEM((nz, block, width), BF16),
            pltpu.VMEM((KEYS, lanes), BF16),
        ]
        + [pltpu.VMEM((2, KEYS, lanes), F32)] * 3
        + [pltpu.VMEM((1, width), F32)] * 2
        + Scatter.semaphores(n_w, sizes)
        + Sums.semaphores(sizes)
        + Outward.semaphores(sizes)
        + Outward.semaphores(sizes)
        + [dma((2, 5)), dma((3,)), dma((2, 2)), dma((nz,)), dma((nz,))],
        compiler_params=pltpu.CompilerParams(
            collective_id=cid, has_side_effects=True, vmem_limit_bytes=62 * 2**20
        ),
        name="back",
    )(out_act, *grads, *heads, d_mixed, mixed, normed, *weights, x, dmid, *tables, gain[None], vec, *[r for pair in before for r in pair])
    return out[:2], out[2], [k.leave(g) for k, g in zip(kinds, out[3:])]


def shards(
    tokens_in, cotangent, image_flag, key_mask, column_mask,
    attention_norm_gain, attention_norm_bias, w_query, w_key, w_value, query_bias, value_bias, w_out, out_bias,
    feedforward_norm_gain, feedforward_norm_bias, w_gate, gate_bias, w_up, up_bias, inner_gain, inner_shift,
    w_down, down_bias,
):
    n_dp, n_tensor = lax.axis_size("dp"), lax.axis_size("tensor")
    sizes = (n_dp, n_tensor)
    dp, z = lax.axis_index("dp"), lax.axis_index("tensor")
    core = dp % 2
    block = tokens_in.shape[1]
    width = tokens_in.shape[2]
    length = block * n_tensor
    block_pad = up_to(block, 16)
    rows = block_pad * n_tensor
    n_head = w_query.shape[1]
    n_ff = w_gate.shape[1]
    ff = up_to(n_ff, 16 if w_down.shape[1] % LANES == 0 else LANES)
    count_live = float(FF - PADCOLS)
    swap = [(i, (i // n_tensor ^ 1) * n_tensor + i % n_tensor) for i in range(n_dp * n_tensor)]

    def other(value):
        return lax.ppermute(value, ("dp", "tensor"), swap)

    pair = 2 * HEAD
    shard_a, shard_b = (
        jnp.concatenate([v[:, s * pair : (s + 1) * pair] for v in (w_query, w_key, w_value)], axis=1) for s in range(2)
    )
    kind_p = Kind(True, shard_a.shape, n_dp)
    kind_o = Kind(False, w_out.shape, n_dp)
    kind_f = Kind(False, (ff, w_down.shape[1]), n_dp)

    def turned(weight):
        return jnp.pad(weight.T, ((0, ff - n_ff), (0, 0)))

    def pad_rows(value):
        return jnp.pad(value, ((0, 0), (0, block_pad - block), (0, 0)))

    wide = up_to(ff, LANES)
    small = jnp.stack(
        [
            jnp.pad(v, (0, wide - v.shape[0]))
            for v in (query_bias, value_bias, gate_bias, up_bias, inner_gain, inner_shift, column_mask.astype(F32))
        ]
        + [jnp.zeros((wide,), F32)]
    )
    own_image = z % (n_tensor // 2)
    live = lax.dynamic_index_in_dim(key_mask, own_image, 0, False)
    live = jnp.pad(live.reshape(n_tensor, block), ((0, 0), (0, block_pad - block))).reshape(rows)
    live = jnp.pad(live, (0, KEYS - rows))
    lane = jnp.arange(LANES)[None, :]
    base = jnp.where(
        lane == HEAD,
        jnp.where(live > 0, 0.0, -1e30)[:, None],
        jnp.where(
            (lane > HEAD) & (lane <= HEAD + 3),
            1.0,
            jnp.where(lane == LANES - 1, lax.dynamic_index_in_dim(image_flag, own_image, 0, False).astype(F32), 0.0),
        ),
    ).astype(BF16)
    tables = lane_tables(length, HEAD // 4, block, block_pad)

    (image, cot, packs, base), full, kept = front(
        pad_rows(tokens_in),
        pad_rows(cotangent),
        small,
        base,
        [shard_a, shard_b, w_out, turned(w_gate), turned(w_up), jnp.pad(w_down, ((0, ff - n_ff), (0, 0)))],
        [kind_p, kind_p, kind_o, kind_f, kind_f, kind_f],
        attention_norm_gain,
        attention_norm_bias,
        tables,
        (out_bias, feedforward_norm_gain, feedforward_norm_bias),
        n_head,
        ff,
        sizes,
        0,
    )
    normed, qa, ka, va, mixed, middle, normed2, gate, up, hidden, sums = kept
    full_a, full_b, full_o, full_g, full_u, full_d = full
    gain, shift, columns = (packs[:, n, :ff].reshape(-1) for n in range(4, 7))
    flag = base[0, LANES - 1].astype(F32)
    middle = middle.reshape(rows, width)
    xhat2, s2 = norm_pieces(middle)
    gate, up = gate.reshape(rows, -1), up.reshape(rows, -1)
    sig = jax.nn.sigmoid(gate)
    act = gate * sig * up
    sums = sums.reshape(rows, -1)
    mean = sums[:, 0:1] / count_live
    var = sums[:, 1:2] / count_live - mean * mean
    r = lax.rsqrt(var + EPS)
    nhat = (act - mean) * r
    part = matmul(hidden, full_d).astype(BF16)
    output = (middle + (part.astype(F32) + other(part).astype(F32)) + down_bias).astype(BF16)

    grad = cot.reshape(rows, width).astype(F32) * flag
    grad_low = grad.astype(BF16)
    g_down = matmul_left_t(hidden, grad_low).astype(BF16)
    dn = columns * lax.dot_general(
        grad_low, full_d, (((1,), (1,)), ((), ())), preferred_element_type=F32
    )
    g_gain = jnp.sum(dn * nhat, axis=0)
    g_shift = jnp.sum(dn, axis=0)
    dnh = dn * gain
    rsums = jnp.stack([jnp.sum(dnh, axis=-1), jnp.sum(dnh * nhat, axis=-1)])
    rsums = rsums + other(rsums)
    dact = r * (dnh - columns * (rsums[0][:, None] + nhat * rsums[1][:, None]) / count_live)
    dgate = dact * up * sig * (1.0 + gate * (1.0 - sig))
    dup = dact * gate * sig
    g_gate_bias = jnp.sum(dgate, axis=0)
    g_up_bias = jnp.sum(dup, axis=0)
    gate_low = dgate.astype(BF16)
    up_low = dup.astype(BF16)
    g_gate = matmul_left_t(gate_low, normed2).astype(BF16)
    g_up = matmul_left_t(up_low, normed2).astype(BF16)
    part = (matmul(gate_low, full_g) + matmul(up_low, full_u)).astype(BF16)
    dnormed2 = part.astype(F32) + other(part).astype(F32)
    g_mlp_gain = jnp.sum(dnormed2 * xhat2, axis=0)
    g_mlp_shift = jnp.sum(dnormed2, axis=0)
    dmiddle = grad + norm_backward(dnormed2, xhat2, s2, feedforward_norm_gain)
    g_out_bias = jnp.sum(dmiddle, axis=0)
    g_down_bias = jnp.sum(grad, axis=0)
    dmid_low = dmiddle.astype(BF16)
    g_out = matmul_left_t(mixed, dmid_low).astype(BF16)
    d_mixed = matmul_right_t(dmid_low, full_o).astype(BF16)
    early = jnp.concatenate([g_out_bias, g_mlp_gain, g_mlp_shift, g_down_bias])
    late_rows = 2 * width // LANES
    qv_rows = 4 * n_head // LANES
    tall = jnp.concatenate(
        [v.reshape(2, -1) for v in (g_gate_bias, g_up_bias, g_gain, g_shift)], axis=1
    ).reshape(-1)
    vec = jnp.concatenate([jnp.zeros(((late_rows + qv_rows) * LANES,), F32), early, tall])
    vec_rows = up_to(up_to(vec.shape[0], LANES) // LANES, 8)
    vec = jnp.pad(vec, (0, vec_rows * LANES - vec.shape[0])).reshape(vec_rows, LANES)
    (out_rows, in_rows), vec, (s_down, s_gate, s_up, s_out, s_a, s_b) = back(
        output.reshape(n_tensor, block_pad, width),
        [g_down, g_gate, g_up, g_out],
        [send_first(kind_f, g, sizes) for g in (g_down, g_gate)],
        [qa, ka, va],
        d_mixed,
        mixed,
        normed,
        [full_a, full_b],
        image,
        dmiddle.reshape(n_tensor, block_pad, width),
        tables,
        attention_norm_gain,
        vec,
        [kind_f, kind_f, kind_f, kind_o, kind_p, kind_p],
        late_rows,
        sizes,
        1,
    )
    out_rows, in_rows = out_rows[:, :block], in_rows[:, :block]
    vec = vec.reshape(2, -1)
    owner = z // (n_tensor // 2)
    mine = lax.dynamic_index_in_dim(vec, owner, 0, False)
    d_at = (late_rows + qv_rows) * LANES
    wide = jnp.concatenate([vec[0, : 2 * width], vec[0, d_at : d_at + 4 * width]]).reshape(6, width)
    qv = lax.dynamic_index_in_dim(mine[late_rows * LANES : d_at].reshape(2, -1), z % (n_tensor // 2), 0, False)
    tall = mine[d_at + 4 * width : d_at + 4 * width + 8 * ff].reshape(2, -1)
    tall = lax.dynamic_index_in_dim(tall, z % (n_tensor // 2), 0, False)
    pieces, at = [qv[:n_head], qv[n_head:]], 0
    for size in [ff] * 4:
        pieces.append(tall[at : at + size])
        at += size
    return (
        out_rows,
        in_rows.astype(F32),
        wide[0],
        wide[1],
        *[jnp.concatenate([v[:, n * pair : (n + 1) * pair] for v in (s_a, s_b)], axis=1) for n in range(3)],
        pieces[0],
        pieces[1],
        s_out,
        wide[2],
        wide[3],
        wide[4],
        s_gate[:n_ff].T,
        pieces[2][:n_ff],
        s_up[:n_ff].T,
        pieces[3][:n_ff],
        pieces[4][:n_ff],
        pieces[5][:n_ff],
        s_down[:n_ff],
        wide[5],
    )


def solution(mesh):
    act, row, col, vec = P("dp", "tensor", None), P("dp", "tensor"), P("tensor", "dp"), P("tensor")
    in_specs = (
        act, act, P("dp"), P("dp", None), vec, P(), P(), row, row, row, vec, vec, col, P(), P(), P(),
        row, vec, row, vec, vec, vec, col, P(),
    )
    out_specs = (
        act, act, P(), P(), row, row, row, vec, vec, col, P(), P(), P(), row, vec, row, vec, vec, vec, col, P(),
    )
    return jax.shard_map(shards, mesh=mesh, in_specs=in_specs, out_specs=out_specs, check_vma=False)
```

```python
import functools
import math

import jax
import jax.numpy as jnp
import numpy as np
from jax import lax
from jax.experimental import pallas as pl
from jax.experimental.pallas import tpu as pltpu
from jax.sharding import PartitionSpec as P

HEAD = 64
FF = 2736
PADCOLS = 6
GRID = 32
EPS = 1e-06
ROPE_BASE = 10000.0
LANES = 128
MESH = pl.DeviceIdType.MESH
LOG2E = math.log2(math.e)
LN2 = math.log(2.0)
SCALE = HEAD ** (-0.5)
F32 = jnp.float32
BF16 = jnp.bfloat16


def up_to(size, unit):
    return -(-size // unit) * unit


def rotary_tables(length, head):
    quarter = head // 4
    place = np.arange(length, dtype=np.int32)
    inside = (place >= 1) & (place <= GRID * GRID)
    cell = np.maximum(place - 1, 0)
    row_pos = np.where(inside, cell // GRID, 0).astype(np.float32)
    col_pos = np.where(inside, cell % GRID, 0).astype(np.float32)
    freq = ROPE_BASE ** (-np.arange(quarter, dtype=np.float32) / quarter)
    angle = np.concatenate(
        [row_pos[:, None] * freq[None, :], col_pos[:, None] * freq[None, :]], axis=1
    )
    return np.cos(angle), np.sin(angle)


def lane_tables(length, quarter, block, rows_padded):
    cosv, sinv = rotary_tables(length, HEAD)

    def lay(first, second):
        one = np.concatenate(
            [first[:, :quarter], second[:, :quarter], first[:, quarter:], second[:, quarter:]], axis=1
        )
        two = np.concatenate([one, one], axis=1)
        cut = two.reshape(length // block, block, 2 * HEAD)
        return np.pad(cut, ((0, 0), (0, rows_padded - block), (0, 0))).reshape(-1, 2 * HEAD)

    zero = np.zeros_like(sinv)
    return [jnp.asarray(t, F32) for t in (lay(cosv, cosv), lay(-sinv, zero), lay(zero, sinv))]


def norm_backward(incoming_gradient, centered_normalized, inverse_scale, norm_gain):
    inner = incoming_gradient * norm_gain
    return inverse_scale * (
        inner
        - jnp.mean(inner, axis=-1, keepdims=True)
        - centered_normalized * jnp.mean(inner * centered_normalized, axis=-1, keepdims=True)
    )


def matmul(left, right):
    return jnp.dot(left, right, preferred_element_type=F32)


def matmul_right_t(left, right):
    return lax.dot_general(left, right, (((1,), (1,)), ((), ())), preferred_element_type=F32)


def matmul_left_t(left, right):
    return lax.dot_general(left, right, (((0,), (0,)), ((), ())), preferred_element_type=F32)


class Kind:
    def __init__(self, by_rows, shard, n_dp):
        self.given = shard
        self.n_dp = n_dp
        self.turn = not by_rows and shard[1] % LANES != 0
        if self.turn:
            shard = (shard[1], up_to(shard[0], LANES))
        self.by_rows = by_rows or self.turn
        self.shard = shard
        a, b = shard
        if self.by_rows:
            self.whole, self.two = (n_dp * a, 2 * b), (2 * a, b)
        else:
            self.whole, self.two = (2 * a, n_dp * b), (a, 2 * b)

    def piece(self, ref, slot, chip):
        a, b = self.shard
        if self.by_rows:
            return ref.at[pl.ds(_mult(chip, 2 * a), 2 * a), pl.ds(_mult(slot, b), b)]
        return ref.at[pl.ds(_mult(slot, a), a), pl.ds(_mult(chip, 2 * b), 2 * b)]

    def half(self, two, core):
        a, b = self.shard
        if self.by_rows:
            return two.at[pl.ds(_mult(core, a), a)]
        return two.at[:, pl.ds(_mult(core, b), b)]

    def one(self, ref, slot, chip, core):
        a, b = self.shard
        if self.by_rows:
            return ref.at[pl.ds(_mult(chip * 2 + core, a), a), pl.ds(_mult(slot, b), b)]
        return ref.at[pl.ds(_mult(slot, a), a), pl.ds(_mult(chip * 2 + core, b), b)]

    def enter(self, shard):
        if not self.turn:
            return shard
        return jnp.pad(shard.T, ((0, 0), (0, self.shard[1] - self.given[0])))

    def leave(self, shard):
        return shard[:, : self.given[0]].T if self.turn else shard

    def join(self, whole):
        if not self.turn:
            return whole
        a, b = self.shard
        whole = whole.reshape(self.n_dp * a, 2, b)[:, :, : self.given[0]]
        return whole.transpose(1, 2, 0).reshape(2 * self.given[0], self.n_dp * a)

    def cut(self, whole):
        if not self.turn:
            return whole
        a, b = self.shard
        whole = whole.reshape(2, self.given[0], self.n_dp * a).transpose(2, 0, 1)
        return jnp.pad(whole, ((0, 0), (0, 0), (0, b - self.given[0]))).reshape(self.whole)


def _mult(index, size):
    return index * size if isinstance(index, int) else pl.multiple_of(index * size, size)


class Place:
    def __init__(self, n_dp, n_tensor):
        self.dp = lax.axis_index("dp")
        self.z = lax.axis_index("tensor")
        self.core = lax.rem(self.dp, 2)
        self.chip = lax.div(self.dp, 2)
        self.nz = n_tensor
        self.chips = n_dp // 2
        self.bits = self.chips.bit_length() - 1
        self.home = self.core == lax.div(self.z, n_tensor // 2)
        self.slot = lax.rem(self.z, n_tensor // 2)

    def flip(self, bit):
        low = lax.rem(lax.div(self.chip, 1 << bit), 2)
        return self.chip + (1 - 2 * low) * (1 << bit)

    def across(self):
        return (self.dp + 1 - 2 * self.core, self.z)

    def beside(self, bit):
        return (self.flip(bit) * 2 + self.core, self.z)

    def shifted(self, by):
        return (self.dp, lax.rem(self.z + by, self.nz))

    def opposite(self):
        return (self.dp, lax.rem(self.z + self.nz // 2, self.nz))

    def neighbour(self):
        return (self.dp, self.z + 1 - 2 * self.slot)

    def barrier(self):
        everyone = [self.across()]
        everyone += [self.shifted(s) for s in range(1, self.nz)]
        everyone += [self.beside(b) for b in range(self.bits)]
        bar = pltpu.get_barrier_semaphore()
        for one in everyone:
            pl.semaphore_signal(bar, inc=1, device_id=one, device_id_type=MESH)
        pl.semaphore_wait(bar, len(everyone))


def remote(src, dst, send, recv, to):
    return pltpu.make_async_remote_copy(
        src_ref=src, dst_ref=dst, send_sem=send, recv_sem=recv, device_id=to, device_id_type=MESH
    )


def flipped(chip, value):
    return lax.bitwise_xor(chip, value)


class Gather:
    def __init__(self, me, kinds, w_in, w_out, sems):
        self.me, self.kinds, self.w_in, self.w_out = me, kinds, w_in, w_out
        self.s_send, self.s_recv, self.z_send, self.z_recv, self.b_send, self.b_recv, self.loc = sems

    @staticmethod
    def semaphores(n_w, sizes):
        dma = pltpu.SemaphoreType.DMA
        bits = (sizes[0] // 2).bit_length() - 1
        most = max(1 << max(bits - 1, 0), 1)
        return [
            dma((n_w,)),
            dma((n_w,)),
            dma((n_w, 2)),
            dma((n_w, 2)),
            dma((n_w, bits, 2, most)),
            dma((n_w, bits, 2, most)),
            dma((n_w,)),
        ]

    def _hop(self, j):
        me = self.me
        mine = self.kinds[j].one(self.w_out[j], me.slot, me.chip, me.core)
        return (
            pltpu.make_async_copy(self.w_in[j], mine, self.loc.at[j]),
            remote(self.w_in[j], mine, self.s_send.at[j], self.s_recv.at[j], me.across()),
        )

    def first_hop(self, j):
        stay, leave = self._hop(j)
        pl.when(self.me.home)(stay.start)
        pl.when(jnp.logical_not(self.me.home))(leave.start)

    def _along(self, j, slot, number, to):
        src = self.kinds[j].piece(self.w_out[j], slot, self.me.chip)
        return remote(src, src, self.z_send.at[j, number], self.z_recv.at[j, slot], to)

    def start_z(self, j):
        me = self.me

        @pl.when(me.home)
        def _():
            stay, leave = self._hop(j)
            stay.wait()
            leave.wait_recv()
            self._along(j, me.slot, 0, me.opposite()).start()
            self._along(j, me.slot, 1, me.neighbour()).start()

    def pass_z(self, j):
        me = self.me

        @pl.when(jnp.logical_not(me.home))
        def _():
            self._along(j, me.slot, 0, me.neighbour()).wait_recv()
            self._along(j, me.slot, 0, me.neighbour()).start()

    def wait_z(self, j):
        self._along(j, 1 - self.me.slot, 0, self.me.neighbour()).wait_recv()

    def _bits(self, j, step, slot):
        me = self.me
        bit = step if slot == 0 else me.bits - 1 - step
        low = 1 if slot == 0 else 1 << (me.bits - step)

        def send(m):
            src = self.kinds[j].piece(self.w_out[j], slot, flipped(me.chip, m * low))
            return remote(
                src, src, self.b_send.at[j, step, slot, m], self.b_recv.at[j, step, slot, m], me.beside(bit)
            )

        return send

    def start_bits(self, j, step):
        for slot in range(2):
            send = self._bits(j, step, slot)
            _each(1 << step, lambda m: send(m).start())

    def wait_bits(self, j, step):
        for slot in range(2):
            send = self._bits(j, step, slot)
            _each(1 << step, lambda m: send(m).wait_recv())

    def finish(self, j):
        me = self.me
        pl.when(jnp.logical_not(me.home))(self._hop(j)[1].wait_send)
        copy = self._along(j, me.slot, 0, me.neighbour())
        copy.wait_send()
        copy = self._along(j, me.slot, 1, me.neighbour())
        pl.when(me.home)(copy.wait_send)
        for step in range(me.bits):
            for slot in range(2):
                send = self._bits(j, step, slot)
                _each(1 << step, lambda m: send(m).wait_send())


class Inward:
    def __init__(self, me, src, dst, sems):
        self.me, self.src, self.dst = me, src, dst
        self.send, self.recv, self.fwd, self.back, self.loc = sems

    @staticmethod
    def semaphores(sizes):
        dma = pltpu.SemaphoreType.DMA
        return [dma((sizes[1],)), dma((sizes[1],)), dma((sizes[1],)), dma((sizes[1],)), dma((1,))]

    def _copy(self, i):
        me = self.me
        target = me.nz // 2 * me.core + i
        return target, remote(
            self.src.at[i], self.dst.at[me.z], self.send.at[i], self.recv.at[me.z], (me.dp, target)
        )

    def _stay(self, i):
        return pltpu.make_async_copy(self.src.at[i], self.dst.at[self.me.z], self.loc.at[0])

    def _onward(self, place):
        slab = self.dst.at[place]
        return remote(slab, slab, self.fwd.at[place], self.back.at[place], self.me.across())

    def start(self):
        for i in range(self.me.nz // 2):
            target, copy = self._copy(i)
            pl.when(target != self.me.z)(copy.start)
            pl.when(target == self.me.z)(self._stay(i).start)

    def pass_on(self):
        me = self.me

        @pl.when(me.home)
        def _():
            for s in range(me.nz):
                place = lax.rem(me.z + s, me.nz)
                if s == 0:
                    self._stay(0).wait()
                else:
                    slab = self.dst.at[place]
                    remote(slab, slab, self.send.at[0], self.recv.at[place], me.across()).wait_recv()
                self._onward(place).start()

    def ready(self):
        for place in range(self.me.nz):
            pl.when(jnp.logical_not(self.me.home))(self._onward(place).wait_recv)

    def finish(self):
        for i in range(self.me.nz // 2):
            target, copy = self._copy(i)
            pl.when(target != self.me.z)(copy.wait_send)
        for place in range(self.me.nz):
            pl.when(self.me.home)(self._onward(place).wait_send)


class Packs:
    def __init__(self, me, src, dst, pair_src, pair_dst, sems):
        self.me, self.src, self.dst, self.pair_src, self.pair_dst = me, src, dst, pair_src, pair_dst
        self.send, self.recv, self.loc = sems

    @staticmethod
    def semaphores(sizes):
        dma = pltpu.SemaphoreType.DMA
        return [dma((sizes[1],)), dma((3,)), dma((2,))]

    def _copy(self, s):
        me = self.me
        return remote(self.src, self.dst.at[me.slot], self.send.at[s], self.recv.at[me.slot], me.shifted(s))

    def _stay(self):
        return pltpu.make_async_copy(self.src, self.dst.at[self.me.slot], self.loc.at[0])

    def _pair(self):
        return (
            pltpu.make_async_copy(self.pair_src, self.pair_dst, self.loc.at[1]),
            remote(self.pair_src, self.pair_dst, self.send.at[0], self.recv.at[2], self.me.across()),
        )

    def start(self):
        @pl.when(self.me.home)
        def _():
            self._stay().start()
            for s in range(1, self.me.nz):
                self._copy(s).start()
            stay, there = self._pair()
            stay.start()
            there.start()

    def ready(self):
        me = self.me
        for slot in range(2):
            row = self.dst.at[slot]
            copy = remote(row, row, self.send.at[0], self.recv.at[slot], me.across())
            pl.when(me.core * (me.nz // 2) + slot != me.z)(copy.wait_recv)
        stay, there = self._pair()

        @pl.when(me.home)
        def _():
            self._stay().wait()
            stay.wait()

        pl.when(jnp.logical_not(me.home))(there.wait_recv)

    def finish(self):
        @pl.when(self.me.home)
        def _():
            for s in range(1, self.me.nz):
                self._copy(s).wait_send()
            self._pair()[1].wait_send()


def _each(count, act):
    if count <= 4:
        for m in range(count):
            act(m)
    else:

        @pl.loop(0, count)
        def _(m):
            act(m)


class Scatter:
    def __init__(self, me, kinds, g_in, keep, got, gotz, stage, g_out, before, sems):
        self.me, self.kinds, self.g_in, self.keep, self.got = me, kinds, g_in, keep, got
        self.before = before
        self.gotz, self.stage, self.g_out = gotz, stage, g_out
        self.b_send, self.b_recv, self.z_send, self.z_recv, self.f_send, self.f_recv, self.loc = sems

    @staticmethod
    def semaphores(n_w, sizes):
        dma = pltpu.SemaphoreType.DMA
        chips = sizes[0] // 2
        bits = chips.bit_length() - 1
        return [
            dma((n_w, bits, 2, chips // 2)),
            dma((n_w, bits, 2, chips // 2)),
            dma((n_w, 2)),
            dma((n_w, 2)),
            dma((n_w,)),
            dma((n_w,)),
            dma((n_w, 2, chips // 2)),
        ]

    def _count(self, step):
        return 1 << (self.me.bits - 1 - step)

    def _base(self, step):
        return sum(self._count(s) for s in range(step))

    def _first(self, j, slot, m, sent):
        bits = self.me.bits
        if slot == 0:
            flip = m + (1 << (bits - 1)) * sent
        else:
            flip = m * 2 + sent
        return self.kinds[j].piece(self.g_in[j], slot, flipped(self.me.chip, flip))

    def _held(self, j, step, slot, m, sent):
        index = m + self._count(step) * sent if slot == 0 else 2 * m + sent
        return self.got[j].at[self._base(step - 1) + index, slot]

    def _copy(self, j, step, slot, m):
        me = self.me
        bit = me.bits - 1 - step if slot == 0 else step
        src = self._first(j, slot, m, 1) if step == 0 else self._held(j, step, slot, m, 1)
        return remote(
            src,
            self.got[j].at[self._base(step) + m, slot],
            self.b_send.at[j, step, slot, m],
            self.b_recv.at[j, step, slot, m],
            me.beside(bit),
        )

    def _came(self, j, slot, m):
        return pltpu.make_async_copy(
            self.before[j][slot].at[m], self.got[j].at[m, slot], self.b_recv.at[j, 0, slot, m]
        )

    def _load(self, j, slot, m):
        return pltpu.make_async_copy(self._first(j, slot, m, 0), self.keep[j].at[slot, m], self.loc.at[j, slot, m])

    def start(self, j, step):
        for slot in range(2):
            if step == 0 and self.before[j] is not None:
                _each(self._count(step), lambda m: self._came(j, slot, m).start())
            else:
                _each(self._count(step), lambda m: self._copy(j, step, slot, m).start())
        if step == 0 and self.keep[j] is not None:
            for slot in range(2):
                _each(self._count(step), lambda m: self._load(j, slot, m).start())

    def add(self, j, step):
        for slot in range(2):

            def one(m):
                if step == 0 and self.before[j] is not None:
                    self._came(j, slot, m).wait()
                else:
                    self._copy(j, step, slot, m).wait_recv()
                if step > 0:
                    mine = self._held(j, step, slot, m, 0)
                elif self.keep[j] is not None:
                    self._load(j, slot, m).wait()
                    mine = self.keep[j].at[slot, m]
                else:
                    mine = self._first(j, slot, m, 0)
                here = self.got[j].at[self._base(step) + m, slot]
                here[...] = (here[...].astype(F32) + mine[...].astype(F32)).astype(BF16)

            _each(self._count(step), one)

    def _last(self, j, slot):
        return self.got[j].at[self._base(self.me.bits - 1), slot]

    def _z(self, j, slot, number, to):
        return remote(
            self._last(j, slot), self.gotz[j].at[number], self.z_send.at[j, number], self.z_recv.at[j, number], to
        )

    def start_z(self, j):
        self._z(j, 1 - self.me.slot, 0, self.me.neighbour()).start()

    def pass_z(self, j):
        me = self.me
        copy = self._z(j, me.slot, 0, me.neighbour())

        @pl.when(jnp.logical_not(me.home))
        def _():
            copy.wait_recv()
            here = self._last(j, me.slot)
            here[...] = (here[...].astype(F32) + self.gotz[j][0].astype(F32)).astype(BF16)
            self._z(j, me.slot, 1, me.opposite()).start()

    def _hand(self, j):
        return remote(self.stage[j], self.g_out[j], self.f_send.at[j], self.f_recv.at[j], self.me.across())

    def end_z(self, j):
        me = self.me

        @pl.when(me.home)
        def _():
            for number in range(2):
                self._z(j, me.slot, number, me.neighbour()).wait_recv()

            def total(core):
                value = self.kinds[j].half(self._last(j, me.slot), core)[...].astype(F32)
                for number in range(2):
                    value = value + self.kinds[j].half(self.gotz[j].at[number], core)[...].astype(F32)
                return value

            self.stage[j][...] = total(1 - me.core)
            self._hand(j).start()
            self.g_out[j][...] = total(me.core)

    def finish(self, j):
        me = self.me
        for step in range(0 if self.before[j] is None else 1, me.bits):
            for slot in range(2):
                _each(self._count(step), lambda m: self._copy(j, step, slot, m).wait_send())
        self._z(j, 1 - me.slot, 0, me.neighbour()).wait_send()
        far = self._z(j, me.slot, 1, me.opposite())
        pl.when(jnp.logical_not(me.home))(far.wait_send)
        hand = self._hand(j)
        pl.when(me.home)(hand.wait_send)
        pl.when(jnp.logical_not(me.home))(hand.wait_recv)


class Sums:
    def __init__(self, me, v_sum, v_got, v_all, out, sems):
        self.me, self.v_sum, self.v_got, self.v_all, self.out = me, v_sum, v_got, v_all, out
        self.b_send, self.b_recv, self.z_send, self.z_recv, self.f_send, self.f_recv = sems

    @staticmethod
    def semaphores(sizes):
        dma = pltpu.SemaphoreType.DMA
        bits = (sizes[0] // 2).bit_length() - 1
        return [dma((bits,)), dma((bits,)), dma((sizes[1],)), dma((sizes[1],)), dma((1,)), dma((1,))]

    @staticmethod
    def scratch(shape, sizes):
        bits = (sizes[0] // 2).bit_length() - 1
        return [
            pltpu.VMEM((bits + 2,) + shape, F32),
            pltpu.VMEM((bits,) + shape, F32),
            pltpu.VMEM((sizes[1],) + shape, F32),
        ]

    def _bit(self, step):
        return remote(
            self.v_sum.at[step], self.v_got.at[step], self.b_send.at[step], self.b_recv.at[step], self.me.beside(step)
        )

    def _z(self, s):
        me = self.me
        return remote(
            self.v_sum.at[me.bits], self.v_all.at[me.z], self.z_send.at[s], self.z_recv.at[me.z], me.shifted(s)
        )

    def _last(self):
        me = self.me
        return remote(self.v_sum.at[me.bits + 1], self.out.at[me.core], self.f_send.at[0], self.f_recv.at[0], me.across())

    def phases(self):
        me = self.me
        self._bit(0).start()
        yield
        for step in range(1, me.bits + 1):
            self._bit(step - 1).wait_recv()
            self.v_sum[step] = self.v_sum[step - 1] + self.v_got[step - 1]
            if step < me.bits:
                self._bit(step).start()
                yield
        for s in range(1, me.nz):
            self._z(s).start()
        self.v_all[me.z] = self.v_sum[me.bits]
        yield
        for s in range(1, me.nz):
            slab = self.v_all.at[lax.rem(me.z + s, me.nz)]
            place = lax.rem(me.z + s, me.nz)
            remote(slab, slab, self.z_send.at[0], self.z_recv.at[place], me.across()).wait_recv()
        value = self.v_all[0]
        for s in range(1, me.nz):
            value = value + self.v_all[s]
        self.v_sum[me.bits + 1] = value
        self._last().start()
        self.out[me.core] = value
        yield
        there = self.out.at[1 - me.core]
        remote(there, there, self.f_send.at[0], self.f_recv.at[0], me.across()).wait_recv()
        for step in range(me.bits):
            self._bit(step).wait_send()
        for s in range(1, me.nz):
            self._z(s).wait_send()
        self._last().wait_send()


class Outward:
    def __init__(self, me, src, dst, sems):
        self.me, self.src, self.dst = me, src, dst
        self.send, self.recv, self.loc = sems

    @staticmethod
    def semaphores(sizes):
        dma = pltpu.SemaphoreType.DMA
        return [dma((sizes[1],)), dma((2,)), dma((1,))]

    def _copy(self, place):
        me = self.me
        return remote(
            self.src.at[place], self.dst.at[me.slot], self.send.at[place], self.recv.at[me.slot], (me.dp, place)
        )

    def _stay(self, place):
        return pltpu.make_async_copy(self.src.at[place], self.dst.at[self.me.slot], self.loc.at[0])

    def start(self, place):
        me = self.me
        pl.when(jnp.logical_and(me.home, place != me.z))(lambda: self._copy(place).start())
        pl.when(jnp.logical_and(me.home, place == me.z))(lambda: self._stay(place).start())

    def finish(self):
        me = self.me
        for place in range(me.nz):
            pl.when(jnp.logical_and(me.home, place != me.z))(lambda place=place: self._copy(place).wait_send())
            pl.when(jnp.logical_and(me.home, place == me.z))(lambda place=place: self._stay(place).wait())
        for slot in range(2):
            row = self.dst.at[slot]
            copy = remote(row, row, self.send.at[0], self.recv.at[slot], me.across())
            pl.when(me.core * (me.nz // 2) + slot != me.z)(copy.wait_recv)


def send_first(kind, grad, sizes):
    n_dp, nz = sizes
    chips = n_dp // 2
    bits = chips.bit_length() - 1
    chip = lax.axis_index("dp") // 2
    grad = kind.cut(grad)
    a, b = kind.shard
    came = []
    for slot in range(2):
        bit = bits - 1 if slot == 0 else 0
        parts = []
        for m in range(chips // 2):
            there = lax.bitwise_xor(chip, m + (1 << bit) if slot == 0 else 2 * m + 1)
            if kind.by_rows:
                parts.append(lax.dynamic_slice(grad, (there * (2 * a), slot * b), kind.two))
            else:
                parts.append(lax.dynamic_slice(grad, (slot * a, there * (2 * b)), kind.two))
        pairs = [(i, (i // nz ^ (2 << bit)) * nz + i % nz) for i in range(n_dp * nz)]
        came.append(lax.ppermute(jnp.stack(parts), ("dp", "tensor"), pairs))
    return came


KEYS = 1152
STRIP = 272
COLS = 384


def _turn(x, cos, sin_up, sin_down):
    quarter = HEAD // 4
    return (
        x * cos
        + pltpu.roll(x, 2 * HEAD - quarter, 1) * sin_up
        + pltpu.roll(x, quarter, 1) * sin_down
    )


def front_kernel(
    kinds, sizes,
    tok_in, cot_in, pack_in, base_in, a_in, b_in, o_in, g_in, u_in, d_in,
    gain_ref, bias_ref, cos_ref, up_ref, down_ref, out_bias, gain2_ref, bias2_ref,
    tok_out, cot, pack, base, a_out, b_out, w_o, w_g, w_u, w_d, normed_out, qa_out, ka_out, va_out, mix_out,
    mid_out, hat_out, normed2_out, gate_out, up_out, hidden_out, totals,
    tok, w_a, w_b, normed, qa_ref, ka_ref, va_ref, mix_ref, normed2, hidden, done_sem,
    wo_v, wg_v, wu_v, part, theirs, mid_v, hat_v, gate_v, up_v, act_v, own_sums, their_sums, p_send, p_recv, r_send, r_recv, out_sem, w_sem,
    *sems,
):
    me = Place(*sizes)
    nz = sizes[1]
    gather = Gather(me, kinds, (a_in, b_in, o_in, g_in, u_in, d_in), (w_a, w_b, w_o, w_g, w_u, w_d), sems[:7])
    tokens = Inward(me, tok_in, tok, sems[7:12])
    cots = Inward(me, cot_in, cot, sems[12:17])
    packs = Packs(me, pack_in, pack, base_in, base, sems[17:20])
    n_w = len(kinds)
    leaving = []

    def leave(src, dst):
        copy = pltpu.make_async_copy(src, dst, done_sem.at[len(leaving)])
        copy.start()
        leaving.append(copy)

    me.barrier()
    for j in range(n_w):
        gather.first_hop(j)
    for j in (0, 1, 3, 2):
        gather.start_z(j)
    packs.start()

    def flow(j):
        gather.wait_z(j)
        gather.start_bits(j, 0)
        yield
        for step in range(1, me.bits):
            gather.wait_bits(j, step - 1)
            gather.start_bits(j, step)
        yield

    flows = [flow(j) for j in range(n_w)]
    gather.pass_z(0)
    next(flows[0])
    gather.pass_z(1)
    next(flows[1])
    next(flows[0])
    gather.pass_z(3)
    next(flows[1])
    next(flows[3])
    gather.pass_z(2)
    tokens.start()
    for j in (4, 5):
        gather.start_z(j)
    next(flows[2])
    next(flows[3])
    tokens.pass_on()
    tokens.ready()
    packs.ready()
    gather.pass_z(4)
    next(flows[2])

    block = tok.shape[1]
    rows = block * nz
    width = tok.shape[2]
    lanes = 2 * HEAD
    lane = lax.broadcasted_iota(jnp.int32, (block, lanes), 1)
    low = lane < HEAD
    one = jnp.where(lane == HEAD, 1.0, 0.0)
    ones = jnp.where((lane >= HEAD) & (lane < HEAD + 3), 1.0, 0.0)

    @pl.loop(0, nz)
    def _(t):
        x = tok[t].astype(F32)
        mean = jnp.sum(x, axis=1, keepdims=True) * (1.0 / width)
        x = x - mean
        var = jnp.sum(x * x, axis=1, keepdims=True) * (1.0 / width)
        x = x * lax.rsqrt(var + EPS)
        normed[pl.ds(pl.multiple_of(t * block, block), block), :] = (x * gain_ref[...] + bias_ref[...]).astype(BF16)

    gather.wait_bits(0, me.bits - 1)
    gather.wait_bits(1, me.bits - 1)
    leave(tok, tok_out)
    leave(w_a, a_out)
    leave(w_b, b_out)
    leave(normed, normed_out)
    pairs = mix_ref.shape[1] // lanes
    sub = pairs // 2

    def project(g):
        weight = (w_a, w_b)[g % sub]

        def column(part):
            at = ((g // sub) * 3 + part) * lanes
            return weight[:, at : at + lanes]

        q_bias = pack[g // sub, 0:1, (g % sub) * lanes : (g % sub + 1) * lanes]
        v_bias = pack[g // sub, 1:2, (g % sub) * lanes : (g % sub + 1) * lanes]

        @pl.loop(0, nz)
        def _(t):
            here = pl.ds(pl.multiple_of(t * block, block), block)
            x = normed[here, :]
            both = matmul(x, jnp.concatenate([column(0), column(1)], axis=1))
            tables = (cos_ref[here, :], up_ref[here, :], down_ref[here, :])
            query = _turn(both[:, :lanes] + q_bias, *tables) * (SCALE * LOG2E)
            key = _turn(both[:, lanes:], *tables)
            value = matmul(x, column(2)) + v_bias
            mask = base[here, :].astype(F32)
            for h in range(2):
                if h:
                    query, key, value = (pltpu.roll(v, HEAD, 1) for v in (query, key, value))
                qa_ref[2 * g + h, here, :] = jnp.where(low, query, one).astype(BF16)
                ka_ref[2 * g + h, here, :] = jnp.where(low, key, mask).astype(BF16)
                va_ref[2 * g + h, here, :] = jnp.where(low, value, ones).astype(BF16)

        rest = pl.ds(rows, KEYS - rows)
        for h in range(2):
            qa_ref[2 * g + h, rest, :] = jnp.zeros((KEYS - rows, lanes), BF16)
            va_ref[2 * g + h, rest, :] = jnp.zeros((KEYS - rows, lanes), BF16)
            ka_ref[2 * g + h, rest, :] = base[rest, :]

    def attend(g):
        @pl.loop(0, nz)
        def _(t):
            here = pl.ds(pl.multiple_of(t * block, block), block)
            outs = []
            for h in range(2):
                q = qa_ref[2 * g + h, here, :]
                s = matmul_right_t(q, ka_ref[2 * g + h])
                top = jnp.max(s, axis=1, keepdims=True)
                p = jnp.exp2(s - top).astype(BF16)
                o = matmul(p, va_ref[2 * g + h])
                total = o[:, HEAD : HEAD + 1]
                outs.append(o / total)
                log = -(top + jnp.log2(total))
                first = log.astype(BF16)
                left = log - first.astype(F32)
                second = left.astype(BF16)
                third = (left - second.astype(F32)).astype(BF16)
                logs = jnp.where(
                    lane == HEAD + 1,
                    first.astype(F32),
                    jnp.where(lane == HEAD + 2, second.astype(F32), third.astype(F32)),
                )
                inside = (lane > HEAD) & (lane <= HEAD + 3)
                qa_ref[2 * g + h, here, :] = jnp.where(inside, logs, q.astype(F32)).astype(BF16)
            mix_ref[here, g * lanes : (g + 1) * lanes] = jnp.where(
                low, outs[0], pltpu.roll(outs[1], HEAD, 1)
            ).astype(BF16)

        for src, dst in ((qa_ref, qa_out), (ka_ref, ka_out), (va_ref, va_out)):
            leave(src.at[pl.ds(2 * g, 2)], dst.at[pl.ds(2 * g, 2)])

    project(0)
    next(flows[4])
    gather.pass_z(5)
    attend(0)
    next(flows[5])
    project(1)
    attend(1)
    next(flows[4])
    project(2)
    attend(2)
    next(flows[5])
    cots.start()
    project(3)
    attend(3)

    def load(j, there):
        gather.wait_bits(j, me.bits - 1)
        copy = pltpu.make_async_copy(gather.w_out[j], there, w_sem.at[j])
        copy.start()
        return copy

    def swap(t):
        return remote(part.at[t], theirs.at[t], p_send.at[t], p_recv.at[t], me.across())

    def swap_sums(t):
        return remote(own_sums.at[t], their_sums.at[t], r_send.at[t], r_recv.at[t], me.across())

    def save(t):
        slot = t % 2
        return [
            pltpu.make_async_copy(mid_v.at[slot], mid_out.at[t], out_sem.at[0, slot]),
            pltpu.make_async_copy(gate_v.at[slot], gate_out.at[t], out_sem.at[1, slot]),
            pltpu.make_async_copy(up_v.at[slot], up_out.at[t], out_sem.at[2, slot]),
            pltpu.make_async_copy(hat_v.at[slot], hat_out.at[t], out_sem.at[3, slot]),
        ]

    leave(mix_ref, mix_out)
    loads = [load(2, wo_v), load(3, wg_v)]
    loads[0].wait()
    for t in range(nz):
        mixed = mix_ref[t * block : (t + 1) * block, :]
        product = matmul_right_t(mixed, wo_v[...]) if kinds[2].turn else matmul(mixed, wo_v[...])
        part[t] = product.astype(BF16)
        swap(t).start()

    ff = hidden.shape[1] // 2
    wide = up_to(ff, LANES)
    place = lax.broadcasted_iota(jnp.int32, (1, 2 * wide), 1)

    def row(n):
        blank = jnp.zeros((1, wide), F32)
        first = jnp.concatenate([pack[0, n : n + 1, :wide], blank], axis=1)
        second = jnp.concatenate([pack[1, n : n + 1, :wide], blank], axis=1)
        return jnp.where(place < ff, first, pltpu.roll(second, ff, 1))[:, : 2 * ff]

    g_bias, u_bias, inner_gain, inner_shift, columns = (row(n) for n in range(2, 7))
    count = float(FF - PADCOLS)

    def finish_tile(t):
        slot = t % 2
        swap_sums(t).wait_recv()
        total = own_sums[t] + their_sums[t]
        totals[t] = jnp.where(lane < 2, total, totals[t])
        mean = total[:, 0:1] / count
        var = total[:, 1:2] / count - mean * mean
        nhat = (act_v[slot] - mean) * lax.rsqrt(var + EPS)
        here = pl.ds(t * block, block)
        hidden[here, :] = (columns * (nhat * inner_gain + inner_shift)).astype(BF16)
        leave(hidden.at[here], hidden_out.at[here])
        leave(normed2.at[here], normed2_out.at[here])

    for t in range(nz):
        slot = t % 2
        if t >= 2:
            for copy in save(t - 2):
                copy.wait()
        swap(t).wait_recv()
        x = tok[t].astype(F32) + (part[t].astype(F32) + theirs[t].astype(F32)) + out_bias[...]
        mid_v[slot] = x
        x = x - jnp.sum(x, axis=1, keepdims=True) * (1.0 / width)
        var = jnp.sum(x * x, axis=1, keepdims=True) * (1.0 / width)
        scale = lax.rsqrt(var + EPS)
        totals[t] = jnp.broadcast_to(scale, (block, lanes))
        x = x * scale
        hat_v[slot] = x
        x = (x * gain2_ref[...] + bias2_ref[...]).astype(BF16)
        normed2[t * block : (t + 1) * block, :] = x
        if t == 0:
            loads.append(load(4, wu_v))
            loads[1].wait()
        gate = (matmul(x, wg_v[...]) if kinds[3].turn else matmul_right_t(x, wg_v[...])) + g_bias
        gate_v[slot] = gate
        if t == 0:
            loads[2].wait()
        up = (matmul(x, wu_v[...]) if kinds[4].turn else matmul_right_t(x, wu_v[...])) + u_bias
        up_v[slot] = up
        gate = gate_v[slot]
        act = gate * (1.0 / (1.0 + jnp.exp(-gate))) * up
        act_v[slot] = act
        live = act * columns
        first = jnp.sum(live, axis=1, keepdims=True)
        second = jnp.sum(live * act, axis=1, keepdims=True)
        own_sums[t] = jnp.where(lane == 0, first, jnp.where(lane == 1, second, 0.0))
        swap_sums(t).start()
        for copy in save(t):
            copy.start()
        if t >= 1:
            finish_tile(t - 1)
    finish_tile(nz - 1)
    cots.pass_on()
    for t in range(nz - 2, nz):
        for copy in save(t):
            copy.wait()
    gather.wait_bits(5, me.bits - 1)
    for copy in leaving:
        copy.wait()
    for t in range(nz):
        swap(t).wait_send()
        swap_sums(t).wait_send()
    cots.ready()
    for j in range(n_w):
        gather.finish(j)
    tokens.finish()
    cots.finish()
    packs.finish()


def front(tokens, cotangent, pack, base, weights, kinds, gain, bias, tables, more, n_head, ff, sizes, cid):
    nz = sizes[1]
    block, width = tokens.shape[1:]
    rows = block * nz
    lanes = 2 * HEAD
    heads = 2 * n_head // HEAD
    hbm = pl.BlockSpec(memory_space=pltpu.HBM)
    vmem = pl.BlockSpec(memory_space=pltpu.VMEM)
    shape = jax.ShapeDtypeStruct
    weights = [k.enter(w) for k, w in zip(kinds, weights)]
    shapes = [
        shape((nz, block, width), BF16),
        shape((nz, block, width), BF16),
        shape((2,) + pack.shape, F32),
        shape(base.shape, BF16),
        *[shape(k.whole, BF16) for k in kinds],
        shape((rows, width), BF16),
        *[shape((heads, KEYS, lanes), BF16)] * 3,
        shape((rows, heads * HEAD), BF16),
        shape((nz, block, width), F32),
        shape((nz, block, width), F32),
        shape((rows, width), BF16),
        shape((nz, block, 2 * ff), F32),
        shape((nz, block, 2 * ff), F32),
        shape((rows, 2 * ff), BF16),
        shape((nz, block, lanes), F32),
    ]
    dma = pltpu.SemaphoreType.DMA
    out = pl.pallas_call(
        functools.partial(front_kernel, kinds, sizes),
        out_shape=shapes,
        in_specs=[hbm] * 10 + [vmem] * 8,
        out_specs=[hbm, hbm, vmem, vmem] + [hbm] * 17 + [vmem],
        scratch_shapes=[
            pltpu.VMEM((nz, block, width), BF16),
            pltpu.VMEM(kinds[0].whole, BF16),
            pltpu.VMEM(kinds[1].whole, BF16),
            pltpu.VMEM((rows, width), BF16),
            *[pltpu.VMEM((heads, KEYS, lanes), BF16)] * 3,
            pltpu.VMEM((rows, heads * HEAD), BF16),
            pltpu.VMEM((rows, width), BF16),
            pltpu.VMEM((rows, 2 * ff), BF16),
            dma((5 + 3 * heads // 2 + 2 * nz,)),
        ]
        + [pltpu.VMEM(k.whole, BF16) for k in kinds[2:5]]
        + [pltpu.VMEM((nz, block, width), BF16)] * 2
        + [pltpu.VMEM((2, block, width), F32)] * 2
        + [pltpu.VMEM((2, block, 2 * ff), F32)] * 3
        + [pltpu.VMEM((nz, block, lanes), F32)] * 2
        + [dma((nz,)), dma((nz,)), dma((nz,)), dma((nz,)), dma((4, 2)), dma((len(kinds),))]
        + Gather.semaphores(len(kinds), sizes)
        + Inward.semaphores(sizes)
        + Inward.semaphores(sizes)
        + Packs.semaphores(sizes),
        compiler_params=pltpu.CompilerParams(
            collective_id=cid, has_side_effects=True, vmem_limit_bytes=60 * 2**20
        ),
        name="front",
    )(tokens, cotangent, pack, base, *weights, gain[None], bias[None], *tables, *[v[None] for v in more])
    return out[:4], [k.join(w) for k, w in zip(kinds, out[4:10])], out[10:]


def back_kernel(
    kinds, sizes, n_late, n_before,
    out_in, g_d, g_g, g_u, g_o, qa_in, ka_in, va_in, do_in, mix_in, normed_in, wa_in, wb_in, x_in, dmid_in,
    cos_ref, up_ref, down_ref, gain_ref, vec_ref,
    *rest,
):
    me = Place(*sizes)
    nz, bits = me.nz, me.bits
    before = [rest[2 * j : 2 * j + 2] if j < n_before else None for j in range(len(kinds))]
    rest = rest[2 * n_before :]
    out_rows, in_rows, vec_out = rest[:3]
    g_out = rest[3 : 3 + len(kinds)]
    rest = rest[3 + len(kinds) :]
    n_w = len(kinds)
    keep = rest[: n_w - 2] + (None, None)
    rest = rest[n_w - 2 :]
    got, gotz, stage = (rest[i * n_w : (i + 1) * n_w] for i in range(3))
    rest = rest[3 * n_w :]
    v_sum, v_got, v_all = rest[:3]
    (qa, ka, va, do, mix, normed, w, x_ref, dmid, d_qkv, g_a, g_b, part, theirs, da, dq, dk, dv, dgain, dshift) = rest[3:23]
    sems = rest[23:]
    scatter = Scatter(
        me, kinds, (g_d, g_g, g_u, g_o, g_a, g_b), keep, got, gotz, stage, g_out, before, sems[:7]
    )
    sums = Sums(me, v_sum, v_got, v_all, vec_out, sems[7:13])
    outs = Outward(me, out_in, out_rows, sems[13:16])
    ins = Outward(me, theirs, in_rows, sems[16:19])
    pair_sem, late_sem, tile_sem, p_send, p_recv = sems[19:24]

    block, width = x_ref.shape[1:]
    rows = block * nz
    lanes = 2 * HEAD
    pairs = mix_in.shape[1] // lanes
    sub = pairs // 2
    lane = lax.broadcasted_iota(jnp.int32, (block, lanes), 1)
    low = lane < HEAD

    turns = [slot * sub + s for s in range(sub) for slot in range(pairs // sub)]

    def loads(n):
        slot = n % 2
        g = turns[n]
        heads = pl.ds(2 * g, 2)
        cols = pl.ds(g * lanes, lanes)
        return [
            pltpu.make_async_copy(qa_in.at[heads], qa.at[slot], pair_sem.at[slot, 0]),
            pltpu.make_async_copy(ka_in.at[heads], ka.at[slot], pair_sem.at[slot, 1]),
            pltpu.make_async_copy(va_in.at[heads], va.at[slot], pair_sem.at[slot, 2]),
            pltpu.make_async_copy(do_in.at[:, cols], do.at[slot], pair_sem.at[slot, 3]),
            pltpu.make_async_copy(mix_in.at[:, cols], mix.at[slot], pair_sem.at[slot, 4]),
        ]

    late = [
        pltpu.make_async_copy(normed_in, normed, late_sem.at[0]),
        pltpu.make_async_copy(wa_in, w.at[:, pl.ds(0, wa_in.shape[1])], late_sem.at[1]),
        pltpu.make_async_copy(wb_in, w.at[:, pl.ds(wa_in.shape[1], wa_in.shape[1])], late_sem.at[2]),
    ]

    def tile_loads(t):
        slot = t % 2
        return [
            pltpu.make_async_copy(x_in.at[t], x_ref.at[slot], tile_sem.at[slot, 0]),
            pltpu.make_async_copy(dmid_in.at[t], dmid.at[slot], tile_sem.at[slot, 1]),
        ]

    me.barrier()
    for j in range(n_w - 2):
        scatter.start(j, 0)
    for copy in loads(0):
        copy.start()
    for place in range(nz):
        outs.start(place)
    for copy in late:
        copy.start()
    for t in range(2):
        for copy in tile_loads(t):
            copy.start()
    v_sum[0] = vec_ref[...]

    def flow(j):
        for step in range(bits):
            scatter.add(j, step)
            if step + 1 < bits:
                scatter.start(j, step + 1)
            else:
                scatter.start_z(j)
            yield

    flows = [flow(j) for j in range(n_w)]

    def rest_of(j):
        for _ in flows[j]:
            pass

    def head(n, h):
        slot = n % 2

        @pl.loop(0, nz)
        def _(t):
            here = pl.ds(pl.multiple_of(t * block, block), block)
            d = do[slot, here, :].astype(F32)
            mine = low if h == 0 else jnp.logical_not(low)
            delta = -jnp.sum(
                jnp.where(mine, d * mix[slot, here, :].astype(F32), 0.0), axis=1, keepdims=True
            )
            if h:
                d = pltpu.roll(d, HEAD, 1)
            first = delta.astype(BF16)
            left = delta - first.astype(F32)
            second = left.astype(BF16)
            third = (left - second.astype(F32)).astype(BF16)
            logs = jnp.where(
                lane == HEAD,
                first.astype(F32),
                jnp.where(lane == HEAD + 1, second.astype(F32), third.astype(F32)),
            )
            da[here, :] = jnp.where(low, d, jnp.where(lane < HEAD + 3, logs, 0.0)).astype(BF16)

        dk[h] = jnp.zeros((KEYS, lanes), F32)
        dv[h] = jnp.zeros((KEYS, lanes), F32)

        def some(here):
            q = qa[slot, h, here, :]
            d = da[here, :]
            p = jnp.exp2(matmul_right_t(ka[slot, h], q))
            ds = (p * matmul_right_t(va[slot, h], d)).astype(BF16)
            dv[h] += matmul(p.astype(BF16), d)
            dk[h] += matmul(ds, q)
            dq[h, here, :] = matmul_left_t(ds, ka[slot, h])

        @pl.loop(0, KEYS // COLS)
        def _(t):
            some(pl.ds(pl.multiple_of(t * COLS, COLS), COLS))

        if KEYS % COLS:
            some(pl.ds(KEYS - KEYS % COLS, KEYS % COLS))

    def put(g, part_of, row, ref, factor, turn):
        at = ((g % sub) * (pairs // sub) * 3 + (g // sub) * 3 + part_of) * lanes

        def one(t, total):
            here = pl.ds(pl.multiple_of(t * block, block), block)
            value = jnp.where(low, ref[0, here, :], pltpu.roll(ref[1, here, :], HEAD, 1))
            if factor is not None:
                value = value * factor
            if turn:
                value = _turn(value, cos_ref[here, :], -up_ref[here, :], -down_ref[here, :])
            d_qkv[here, at : at + lanes] = value.astype(BF16)
            return total + jnp.sum(value, axis=0, keepdims=True)

        total = lax.fori_loop(0, nz, one, jnp.zeros((1, lanes), F32))
        if row is not None:
            v_sum[0, row : row + 1, :] = total

    da[pl.ds(rows, KEYS - rows), :] = jnp.zeros((KEYS - rows, lanes), BF16)

    def weight_gradient(s):
        into = (g_a, g_b)[s]
        columns = into.shape[1]
        grad = d_qkv[:, s * columns : (s + 1) * columns]
        step = max(kinds[-1].two[0], lanes)
        for c in range(width // step):
            left = normed[:, c * step : (c + 1) * step]
            into[c * step : (c + 1) * step, :] = matmul_left_t(left, grad).astype(BF16)

    def fetch(g):
        for copy in loads(g):
            copy.wait()
        if g + 1 < pairs:
            for copy in loads(g + 1):
                copy.start()

    def write(n):
        g = turns[n]
        base_row = n_late + (g // sub) * (2 * sub) + g % sub
        put(g, 0, base_row, dq, SCALE, True)
        put(g, 1, None, dk, LN2, True)
        put(g, 2, base_row + sub, dv, None, False)

    def swap(t):
        return remote(part.at[t], theirs.at[t], p_send.at[t], p_recv.at[t], me.across())

    def partial():
        for t in range(nz):
            here = slice(t * block, (t + 1) * block)
            part[t] = matmul_right_t(d_qkv[here, :], w[...]).astype(BF16)
            swap(t).start()

    def input_gradient():
        dgain[...] = jnp.zeros_like(dgain)
        dshift[...] = jnp.zeros_like(dshift)
        for t in range(nz):
            for copy in tile_loads(t):
                copy.wait()
            swap(t).wait_recv()

            @pl.loop(0, block // STRIP)
            def _(i, t=t):
                here = pl.ds(pl.multiple_of(i * STRIP, STRIP), STRIP)
                x = x_ref[t % 2, here, :].astype(F32)
                x = x - jnp.sum(x, axis=1, keepdims=True) * (1.0 / width)
                var = jnp.sum(x * x, axis=1, keepdims=True) * (1.0 / width)
                scale = lax.rsqrt(var + EPS)
                x = x * scale
                dn = part[t, here, :].astype(F32) + theirs[t, here, :].astype(F32)
                dgain[...] += dn * x
                dshift[...] += dn
                v = dn * gain_ref[...]
                mean = jnp.sum(v, axis=1, keepdims=True) * (1.0 / width)
                along = jnp.sum(v * x, axis=1, keepdims=True) * (1.0 / width)
                theirs[t, here, :] = (dmid[t % 2, here, :] + scale * (v - mean - x * along)).astype(BF16)

            ins.start(t)
            if t + 2 < nz:
                for copy in tile_loads(t + 2):
                    copy.start()
        per = width // lanes
        whole_gain = jnp.sum(dgain[...], axis=0, keepdims=True)
        whole_shift = jnp.sum(dshift[...], axis=0, keepdims=True)
        for i in range(per):
            v_sum[0, i : i + 1, :] = whole_gain[:, i * lanes : (i + 1) * lanes]
            v_sum[0, per + i : per + i + 1, :] = whole_shift[:, i * lanes : (i + 1) * lanes]

    fetch(0)
    head(0, 0)
    head(0, 1)
    write(0)
    next(flows[0], None)
    next(flows[1], None)
    fetch(1)
    head(1, 0)
    head(1, 1)
    write(1)
    rest_of(0)
    rest_of(1)
    for copy in late:
        copy.wait()
    weight_gradient(0)
    next(flows[2], None)
    scatter.start(4, 0)
    scatter.pass_z(0)
    scatter.pass_z(1)
    fetch(2)
    head(2, 0)
    next(flows[3], None)
    rest_of(2)
    scatter.end_z(0)
    head(2, 1)
    write(2)
    next(flows[4], None)
    scatter.end_z(1)
    fetch(3)
    head(3, 0)
    rest_of(3)
    scatter.pass_z(2)
    head(3, 1)
    write(3)
    rest_of(4)
    weight_gradient(1)
    scatter.start(5, 0)
    scatter.pass_z(3)
    partial()
    next(flows[5], None)
    scatter.pass_z(4)
    scatter.end_z(2)
    input_gradient()
    rest_of(5)
    small = sums.phases()
    next(small, None)
    scatter.end_z(3)
    next(small, None)
    scatter.pass_z(5)
    scatter.end_z(4)
    for _ in small:
        pass
    scatter.end_z(5)
    for t in range(nz):
        swap(t).wait_send()
    outs.finish()
    ins.finish()
    for j in range(n_w):
        scatter.finish(j)


def back(out_act, grads, before, heads, d_mixed, mixed, normed, weights, x, dmid, tables, gain, vec, kinds, n_late, sizes, cid):
    n_dp, nz = sizes
    chips = n_dp // 2
    n_w = len(kinds)
    block, width = x.shape[1:]
    rows = block * nz
    lanes = 2 * HEAD
    hbm = pl.BlockSpec(memory_space=pltpu.HBM)
    vmem = pl.BlockSpec(memory_space=pltpu.VMEM)
    shape = jax.ShapeDtypeStruct
    dma = pltpu.SemaphoreType.DMA
    grads = [k.cut(g) for k, g in zip(kinds, grads)]
    out = pl.pallas_call(
        functools.partial(back_kernel, kinds, sizes, n_late, len(before)),
        out_shape=[shape((nz // 2, block, width), BF16)] * 2
        + [shape((2,) + vec.shape, F32)]
        + [shape(k.shard, F32) for k in kinds],
        in_specs=[hbm] * 15 + [vmem] * 5 + [hbm] * (2 * len(before)),
        out_specs=[hbm, hbm] + [vmem] * (1 + n_w),
        scratch_shapes=[pltpu.VMEM((2, chips // 2) + k.two, BF16) for k in kinds[:-2]]
        + [pltpu.VMEM((chips - 1, 2) + k.two, BF16) for k in kinds]
        + [pltpu.VMEM((2,) + k.two, BF16) for k in kinds]
        + [pltpu.VMEM(k.shard, F32) for k in kinds]
        + Sums.scratch(vec.shape, sizes)
        + [pltpu.VMEM((2, 2, KEYS, lanes), BF16)] * 3
        + [pltpu.VMEM((2, rows, lanes), BF16)] * 2
        + [
            pltpu.VMEM((rows, width), BF16),
            pltpu.VMEM((width, 2 * weights[0].shape[1]), BF16),
            pltpu.VMEM((2, block, width), BF16),
            pltpu.VMEM((2, block, width), F32),
            pltpu.VMEM((rows, 2 * weights[0].shape[1]), BF16),
            pltpu.VMEM((width, weights[0].shape[1]), BF16),
            pltpu.VMEM((width, weights[0].shape[1]), BF16),
            pltpu.VMEM((nz, block, width), BF16),
            pltpu.VMEM((nz, block, width), BF16),
            pltpu.VMEM((KEYS, lanes), BF16),
        ]
        + [pltpu.VMEM((2, KEYS, lanes), F32)] * 3
        + [pltpu.VMEM((STRIP, width), F32)] * 2
        + Scatter.semaphores(n_w, sizes)
        + Sums.semaphores(sizes)
        + Outward.semaphores(sizes)
        + Outward.semaphores(sizes)
        + [dma((2, 5)), dma((3,)), dma((2, 2)), dma((nz,)), dma((nz,))],
        compiler_params=pltpu.CompilerParams(
            collective_id=cid, has_side_effects=True, vmem_limit_bytes=62 * 2**20
        ),
        name="back",
    )(out_act, *grads, *heads, d_mixed, mixed, normed, *weights, x, dmid, *tables, gain[None], vec, *[r for pair in before for r in pair])
    return out[:2], out[2], [k.leave(g) for k, g in zip(kinds, out[3:])]


def shards(
    tokens_in, cotangent, image_flag, key_mask, column_mask,
    attention_norm_gain, attention_norm_bias, w_query, w_key, w_value, query_bias, value_bias, w_out, out_bias,
    feedforward_norm_gain, feedforward_norm_bias, w_gate, gate_bias, w_up, up_bias, inner_gain, inner_shift,
    w_down, down_bias,
):
    n_dp, n_tensor = lax.axis_size("dp"), lax.axis_size("tensor")
    sizes = (n_dp, n_tensor)
    dp, z = lax.axis_index("dp"), lax.axis_index("tensor")
    core = dp % 2
    block = tokens_in.shape[1]
    width = tokens_in.shape[2]
    length = block * n_tensor
    block_pad = up_to(block, 16)
    rows = block_pad * n_tensor
    n_head = w_query.shape[1]
    n_ff = w_gate.shape[1]
    ff = up_to(n_ff, 16 if w_down.shape[1] % LANES == 0 else LANES)
    count_live = float(FF - PADCOLS)
    swap = [(i, (i // n_tensor ^ 1) * n_tensor + i % n_tensor) for i in range(n_dp * n_tensor)]

    def other(value):
        return lax.ppermute(value, ("dp", "tensor"), swap)

    pair = 2 * HEAD
    shard_a, shard_b = (
        jnp.concatenate([v[:, s * pair : (s + 1) * pair] for v in (w_query, w_key, w_value)], axis=1) for s in range(2)
    )
    kind_p = Kind(True, shard_a.shape, n_dp)
    kind_o = Kind(False, w_out.shape, n_dp)
    kind_f = Kind(False, (ff, w_down.shape[1]), n_dp)

    def turned(weight):
        return jnp.pad(weight.T, ((0, ff - n_ff), (0, 0)))

    def pad_rows(value):
        return jnp.pad(value, ((0, 0), (0, block_pad - block), (0, 0)))

    wide = up_to(ff, LANES)
    small = jnp.stack(
        [
            jnp.pad(v, (0, wide - v.shape[0]))
            for v in (query_bias, value_bias, gate_bias, up_bias, inner_gain, inner_shift, column_mask.astype(F32))
        ]
        + [jnp.zeros((wide,), F32)]
    )
    own_image = z % (n_tensor // 2)
    live = lax.dynamic_index_in_dim(key_mask, own_image, 0, False)
    live = jnp.pad(live.reshape(n_tensor, block), ((0, 0), (0, block_pad - block))).reshape(rows)
    live = jnp.pad(live, (0, KEYS - rows))
    lane = jnp.arange(LANES)[None, :]
    base = jnp.where(
        lane == HEAD,
        jnp.where(live > 0, 0.0, -1e30)[:, None],
        jnp.where(
            (lane > HEAD) & (lane <= HEAD + 3),
            1.0,
            jnp.where(lane == LANES - 1, lax.dynamic_index_in_dim(image_flag, own_image, 0, False).astype(F32), 0.0),
        ),
    ).astype(BF16)
    tables = lane_tables(length, HEAD // 4, block, block_pad)

    (image, cot, packs, base), full, kept = front(
        pad_rows(tokens_in),
        pad_rows(cotangent),
        small,
        base,
        [shard_a, shard_b, w_out, turned(w_gate), turned(w_up), jnp.pad(w_down, ((0, ff - n_ff), (0, 0)))],
        [kind_p, kind_p, kind_o, kind_f, kind_f, kind_f],
        attention_norm_gain,
        attention_norm_bias,
        tables,
        (out_bias, feedforward_norm_gain, feedforward_norm_bias),
        n_head,
        ff,
        sizes,
        0,
    )
    normed, qa, ka, va, mixed, middle, xhat2, normed2, gate, up, hidden, sums = kept
    full_a, full_b, full_o, full_g, full_u, full_d = full
    gain, shift, columns = (packs[:, n, :ff].reshape(-1) for n in range(4, 7))
    flag = base[0, LANES - 1].astype(F32)
    middle = middle.reshape(rows, width)
    xhat2 = xhat2.reshape(rows, width)
    gate, up = gate.reshape(rows, -1), up.reshape(rows, -1)
    sig = jax.nn.sigmoid(gate)
    act = gate * sig * up
    sums = sums.reshape(rows, -1)
    s2 = sums[:, 2:3]
    mean = sums[:, 0:1] / count_live
    var = sums[:, 1:2] / count_live - mean * mean
    r = lax.rsqrt(var + EPS)
    nhat = (act - mean) * r
    part = matmul(hidden, full_d).astype(BF16)
    output = (middle + (part.astype(F32) + other(part).astype(F32)) + down_bias).astype(BF16)

    grad = cot.reshape(rows, width).astype(F32) * flag
    grad_low = grad.astype(BF16)
    g_down = matmul_left_t(hidden, grad_low).astype(BF16)
    dn = columns * lax.dot_general(
        grad_low, full_d, (((1,), (1,)), ((), ())), preferred_element_type=F32
    )
    g_gain = jnp.sum(dn * nhat, axis=0)
    g_shift = jnp.sum(dn, axis=0)
    dnh = dn * gain
    rsums = jnp.stack([jnp.sum(dnh, axis=-1), jnp.sum(dnh * nhat, axis=-1)])
    rsums = rsums + other(rsums)
    dact = r * (dnh - columns * (rsums[0][:, None] + nhat * rsums[1][:, None]) / count_live)
    dgate = dact * up * sig * (1.0 + gate * (1.0 - sig))
    dup = dact * gate * sig
    g_gate_bias = jnp.sum(dgate, axis=0)
    g_up_bias = jnp.sum(dup, axis=0)
    gate_low = dgate.astype(BF16)
    up_low = dup.astype(BF16)
    g_gate = matmul_left_t(gate_low, normed2).astype(BF16)
    g_up = matmul_left_t(up_low, normed2).astype(BF16)
    part = (matmul(gate_low, full_g) + matmul(up_low, full_u)).astype(BF16)
    dnormed2 = part.astype(F32) + other(part).astype(F32)
    g_mlp_gain = jnp.sum(dnormed2 * xhat2, axis=0)
    g_mlp_shift = jnp.sum(dnormed2, axis=0)
    dmiddle = grad + norm_backward(dnormed2, xhat2, s2, feedforward_norm_gain)
    g_out_bias = jnp.sum(dmiddle, axis=0)
    g_down_bias = jnp.sum(grad, axis=0)
    dmid_low = dmiddle.astype(BF16)
    g_out = matmul_left_t(mixed, dmid_low).astype(BF16)
    d_mixed = matmul_right_t(dmid_low, full_o).astype(BF16)
    early = jnp.concatenate([g_out_bias, g_mlp_gain, g_mlp_shift, g_down_bias])
    late_rows = 2 * width // LANES
    qv_rows = 4 * n_head // LANES
    tall = jnp.concatenate(
        [v.reshape(2, -1) for v in (g_gate_bias, g_up_bias, g_gain, g_shift)], axis=1
    ).reshape(-1)
    vec = jnp.concatenate([jnp.zeros(((late_rows + qv_rows) * LANES,), F32), early, tall])
    vec_rows = up_to(up_to(vec.shape[0], LANES) // LANES, 8)
    vec = jnp.pad(vec, (0, vec_rows * LANES - vec.shape[0])).reshape(vec_rows, LANES)
    (out_rows, in_rows), vec, (s_down, s_gate, s_up, s_out, s_a, s_b) = back(
        output.reshape(n_tensor, block_pad, width),
        [g_down, g_gate, g_up, g_out],
        [send_first(kind_f, g, sizes) for g in (g_down, g_gate)],
        [qa, ka, va],
        d_mixed,
        mixed,
        normed,
        [full_a, full_b],
        image,
        dmiddle.reshape(n_tensor, block_pad, width),
        tables,
        attention_norm_gain,
        vec,
        [kind_f, kind_f, kind_f, kind_o, kind_p, kind_p],
        late_rows,
        sizes,
        1,
    )
    out_rows, in_rows = out_rows[:, :block], in_rows[:, :block]
    vec = vec.reshape(2, -1)
    owner = z // (n_tensor // 2)
    mine = lax.dynamic_index_in_dim(vec, owner, 0, False)
    d_at = (late_rows + qv_rows) * LANES
    wide = jnp.concatenate([vec[0, : 2 * width], vec[0, d_at : d_at + 4 * width]]).reshape(6, width)
    qv = lax.dynamic_index_in_dim(mine[late_rows * LANES : d_at].reshape(2, -1), z % (n_tensor // 2), 0, False)
    tall = mine[d_at + 4 * width : d_at + 4 * width + 8 * ff].reshape(2, -1)
    tall = lax.dynamic_index_in_dim(tall, z % (n_tensor // 2), 0, False)
    pieces, at = [qv[:n_head], qv[n_head:]], 0
    for size in [ff] * 4:
        pieces.append(tall[at : at + size])
        at += size
    return (
        out_rows,
        in_rows.astype(F32),
        wide[0],
        wide[1],
        *[jnp.concatenate([v[:, n * pair : (n + 1) * pair] for v in (s_a, s_b)], axis=1) for n in range(3)],
        pieces[0],
        pieces[1],
        s_out,
        wide[2],
        wide[3],
        wide[4],
        s_gate[:n_ff].T,
        pieces[2][:n_ff],
        s_up[:n_ff].T,
        pieces[3][:n_ff],
        pieces[4][:n_ff],
        pieces[5][:n_ff],
        s_down[:n_ff],
        wide[5],
    )


def solution(mesh):
    act, row, col, vec = P("dp", "tensor", None), P("dp", "tensor"), P("tensor", "dp"), P("tensor")
    in_specs = (
        act, act, P("dp"), P("dp", None), vec, P(), P(), row, row, row, vec, vec, col, P(), P(), P(),
        row, vec, row, vec, vec, vec, col, P(),
    )
    out_specs = (
        act, act, P(), P(), row, row, row, vec, vec, col, P(), P(), P(), row, vec, row, vec, vec, vec, col, P(),
    )
    return jax.shard_map(shards, mesh=mesh, in_specs=in_specs, out_specs=out_specs, check_vma=False)
```

```python
import functools
import math

import jax
import jax.numpy as jnp
import numpy as np
from jax import lax
from jax.experimental import pallas as pl
from jax.experimental.pallas import tpu as pltpu
from jax.sharding import PartitionSpec as P

HEAD = 64
FF = 2736
PADCOLS = 6
GRID = 32
EPS = 1e-06
ROPE_BASE = 10000.0
LANES = 128
MESH = pl.DeviceIdType.MESH
LOG2E = math.log2(math.e)
LN2 = math.log(2.0)
SCALE = HEAD ** (-0.5)
F32 = jnp.float32
BF16 = jnp.bfloat16


def up_to(size, unit):
    return -(-size // unit) * unit


def rotary_tables(length, head):
    quarter = head // 4
    place = np.arange(length, dtype=np.int32)
    inside = (place >= 1) & (place <= GRID * GRID)
    cell = np.maximum(place - 1, 0)
    row_pos = np.where(inside, cell // GRID, 0).astype(np.float32)
    col_pos = np.where(inside, cell % GRID, 0).astype(np.float32)
    freq = ROPE_BASE ** (-np.arange(quarter, dtype=np.float32) / quarter)
    angle = np.concatenate(
        [row_pos[:, None] * freq[None, :], col_pos[:, None] * freq[None, :]], axis=1
    )
    return np.cos(angle), np.sin(angle)


def lane_tables(length, quarter, block, rows_padded):
    cosv, sinv = rotary_tables(length, HEAD)

    def lay(first, second):
        one = np.concatenate(
            [first[:, :quarter], second[:, :quarter], first[:, quarter:], second[:, quarter:]], axis=1
        )
        two = np.concatenate([one, one], axis=1)
        cut = two.reshape(length // block, block, 2 * HEAD)
        return np.pad(cut, ((0, 0), (0, rows_padded - block), (0, 0))).reshape(-1, 2 * HEAD)

    zero = np.zeros_like(sinv)
    return [jnp.asarray(t, F32) for t in (lay(cosv, cosv), lay(-sinv, zero), lay(zero, sinv))]


def norm_backward(incoming_gradient, centered_normalized, inverse_scale, norm_gain):
    inner = incoming_gradient * norm_gain
    return inverse_scale * (
        inner
        - jnp.mean(inner, axis=-1, keepdims=True)
        - centered_normalized * jnp.mean(inner * centered_normalized, axis=-1, keepdims=True)
    )


def matmul(left, right):
    return jnp.dot(left, right, preferred_element_type=F32)


def matmul_right_t(left, right):
    return lax.dot_general(left, right, (((1,), (1,)), ((), ())), preferred_element_type=F32)


def matmul_left_t(left, right):
    return lax.dot_general(left, right, (((0,), (0,)), ((), ())), preferred_element_type=F32)


class Kind:
    def __init__(self, by_rows, shard, n_dp):
        self.given = shard
        self.n_dp = n_dp
        self.turn = not by_rows and shard[1] % LANES != 0
        if self.turn:
            shard = (shard[1], up_to(shard[0], LANES))
        self.by_rows = by_rows or self.turn
        self.shard = shard
        a, b = shard
        if self.by_rows:
            self.whole, self.two = (n_dp * a, 2 * b), (2 * a, b)
        else:
            self.whole, self.two = (2 * a, n_dp * b), (a, 2 * b)

    def piece(self, ref, slot, chip):
        a, b = self.shard
        if self.by_rows:
            return ref.at[pl.ds(_mult(chip, 2 * a), 2 * a), pl.ds(_mult(slot, b), b)]
        return ref.at[pl.ds(_mult(slot, a), a), pl.ds(_mult(chip, 2 * b), 2 * b)]

    def half(self, two, core):
        a, b = self.shard
        if self.by_rows:
            return two.at[pl.ds(_mult(core, a), a)]
        return two.at[:, pl.ds(_mult(core, b), b)]

    def one(self, ref, slot, chip, core):
        a, b = self.shard
        if self.by_rows:
            return ref.at[pl.ds(_mult(chip * 2 + core, a), a), pl.ds(_mult(slot, b), b)]
        return ref.at[pl.ds(_mult(slot, a), a), pl.ds(_mult(chip * 2 + core, b), b)]

    def enter(self, shard):
        if not self.turn:
            return shard
        return jnp.pad(shard.T, ((0, 0), (0, self.shard[1] - self.given[0])))

    def leave(self, shard):
        return shard[:, : self.given[0]].T if self.turn else shard

    def join(self, whole):
        if not self.turn:
            return whole
        a, b = self.shard
        whole = whole.reshape(self.n_dp * a, 2, b)[:, :, : self.given[0]]
        return whole.transpose(1, 2, 0).reshape(2 * self.given[0], self.n_dp * a)

    def cut(self, whole):
        if not self.turn:
            return whole
        a, b = self.shard
        whole = whole.reshape(2, self.given[0], self.n_dp * a).transpose(2, 0, 1)
        return jnp.pad(whole, ((0, 0), (0, 0), (0, b - self.given[0]))).reshape(self.whole)


def _mult(index, size):
    return index * size if isinstance(index, int) else pl.multiple_of(index * size, size)


class Place:
    def __init__(self, n_dp, n_tensor):
        self.dp = lax.axis_index("dp")
        self.z = lax.axis_index("tensor")
        self.core = lax.rem(self.dp, 2)
        self.chip = lax.div(self.dp, 2)
        self.nz = n_tensor
        self.chips = n_dp // 2
        self.bits = self.chips.bit_length() - 1
        self.home = self.core == lax.div(self.z, n_tensor // 2)
        self.slot = lax.rem(self.z, n_tensor // 2)

    def flip(self, bit):
        low = lax.rem(lax.div(self.chip, 1 << bit), 2)
        return self.chip + (1 - 2 * low) * (1 << bit)

    def across(self):
        return (self.dp + 1 - 2 * self.core, self.z)

    def beside(self, bit):
        return (self.flip(bit) * 2 + self.core, self.z)

    def shifted(self, by):
        return (self.dp, lax.rem(self.z + by, self.nz))

    def opposite(self):
        return (self.dp, lax.rem(self.z + self.nz // 2, self.nz))

    def neighbour(self):
        return (self.dp, self.z + 1 - 2 * self.slot)

    def barrier(self):
        everyone = [self.across()]
        everyone += [self.shifted(s) for s in range(1, self.nz)]
        everyone += [self.beside(b) for b in range(self.bits)]
        bar = pltpu.get_barrier_semaphore()
        for one in everyone:
            pl.semaphore_signal(bar, inc=1, device_id=one, device_id_type=MESH)
        pl.semaphore_wait(bar, len(everyone))


def remote(src, dst, send, recv, to):
    return pltpu.make_async_remote_copy(
        src_ref=src, dst_ref=dst, send_sem=send, recv_sem=recv, device_id=to, device_id_type=MESH
    )


def flipped(chip, value):
    return lax.bitwise_xor(chip, value)


class Gather:
    def __init__(self, me, kinds, w_in, w_out, sems):
        self.me, self.kinds, self.w_in, self.w_out = me, kinds, w_in, w_out
        self.s_send, self.s_recv, self.z_send, self.z_recv, self.b_send, self.b_recv, self.loc = sems

    @staticmethod
    def semaphores(n_w, sizes):
        dma = pltpu.SemaphoreType.DMA
        bits = (sizes[0] // 2).bit_length() - 1
        most = max(1 << max(bits - 1, 0), 1)
        return [
            dma((n_w,)),
            dma((n_w,)),
            dma((n_w, 2)),
            dma((n_w, 2)),
            dma((n_w, bits, 2, most)),
            dma((n_w, bits, 2, most)),
            dma((n_w,)),
        ]

    def _hop(self, j):
        me = self.me
        mine = self.kinds[j].one(self.w_out[j], me.slot, me.chip, me.core)
        return (
            pltpu.make_async_copy(self.w_in[j], mine, self.loc.at[j]),
            remote(self.w_in[j], mine, self.s_send.at[j], self.s_recv.at[j], me.across()),
        )

    def first_hop(self, j):
        stay, leave = self._hop(j)
        pl.when(self.me.home)(stay.start)
        pl.when(jnp.logical_not(self.me.home))(leave.start)

    def _along(self, j, slot, number, to):
        src = self.kinds[j].piece(self.w_out[j], slot, self.me.chip)
        return remote(src, src, self.z_send.at[j, number], self.z_recv.at[j, slot], to)

    def start_z(self, j):
        me = self.me

        @pl.when(me.home)
        def _():
            stay, leave = self._hop(j)
            stay.wait()
            leave.wait_recv()
            self._along(j, me.slot, 0, me.opposite()).start()
            self._along(j, me.slot, 1, me.neighbour()).start()

    def pass_z(self, j):
        me = self.me

        @pl.when(jnp.logical_not(me.home))
        def _():
            self._along(j, me.slot, 0, me.neighbour()).wait_recv()
            self._along(j, me.slot, 0, me.neighbour()).start()

    def wait_z(self, j):
        self._along(j, 1 - self.me.slot, 0, self.me.neighbour()).wait_recv()

    def _bits(self, j, step, slot):
        me = self.me
        bit = step if slot == 0 else me.bits - 1 - step
        low = 1 if slot == 0 else 1 << (me.bits - step)

        def send(m):
            src = self.kinds[j].piece(self.w_out[j], slot, flipped(me.chip, m * low))
            return remote(
                src, src, self.b_send.at[j, step, slot, m], self.b_recv.at[j, step, slot, m], me.beside(bit)
            )

        return send

    def start_bits(self, j, step):
        for slot in range(2):
            send = self._bits(j, step, slot)
            _each(1 << step, lambda m: send(m).start())

    def wait_bits(self, j, step):
        for slot in range(2):
            send = self._bits(j, step, slot)
            _each(1 << step, lambda m: send(m).wait_recv())

    def finish(self, j):
        me = self.me
        pl.when(jnp.logical_not(me.home))(self._hop(j)[1].wait_send)
        copy = self._along(j, me.slot, 0, me.neighbour())
        copy.wait_send()
        copy = self._along(j, me.slot, 1, me.neighbour())
        pl.when(me.home)(copy.wait_send)
        for step in range(me.bits):
            for slot in range(2):
                send = self._bits(j, step, slot)
                _each(1 << step, lambda m: send(m).wait_send())


class Inward:
    def __init__(self, me, src, dst, sems):
        self.me, self.src, self.dst = me, src, dst
        self.send, self.recv, self.fwd, self.back, self.loc = sems

    @staticmethod
    def semaphores(sizes):
        dma = pltpu.SemaphoreType.DMA
        return [dma((sizes[1],)), dma((sizes[1],)), dma((sizes[1],)), dma((sizes[1],)), dma((1,))]

    def _copy(self, i):
        me = self.me
        target = me.nz // 2 * me.core + i
        return target, remote(
            self.src.at[i], self.dst.at[me.z], self.send.at[i], self.recv.at[me.z], (me.dp, target)
        )

    def _stay(self, i):
        return pltpu.make_async_copy(self.src.at[i], self.dst.at[self.me.z], self.loc.at[0])

    def _onward(self, place):
        slab = self.dst.at[place]
        return remote(slab, slab, self.fwd.at[place], self.back.at[place], self.me.across())

    def start(self):
        for i in range(self.me.nz // 2):
            target, copy = self._copy(i)
            pl.when(target != self.me.z)(copy.start)
            pl.when(target == self.me.z)(self._stay(i).start)

    def pass_on(self):
        me = self.me

        @pl.when(me.home)
        def _():
            for s in range(me.nz):
                place = lax.rem(me.z + s, me.nz)
                if s == 0:
                    self._stay(0).wait()
                else:
                    slab = self.dst.at[place]
                    remote(slab, slab, self.send.at[0], self.recv.at[place], me.across()).wait_recv()
                self._onward(place).start()

    def ready(self):
        for place in range(self.me.nz):
            pl.when(jnp.logical_not(self.me.home))(self._onward(place).wait_recv)

    def finish(self):
        for i in range(self.me.nz // 2):
            target, copy = self._copy(i)
            pl.when(target != self.me.z)(copy.wait_send)
        for place in range(self.me.nz):
            pl.when(self.me.home)(self._onward(place).wait_send)


class Packs:
    def __init__(self, me, src, dst, pair_src, pair_dst, sems):
        self.me, self.src, self.dst, self.pair_src, self.pair_dst = me, src, dst, pair_src, pair_dst
        self.send, self.recv, self.loc = sems

    @staticmethod
    def semaphores(sizes):
        dma = pltpu.SemaphoreType.DMA
        return [dma((sizes[1],)), dma((3,)), dma((2,))]

    def _copy(self, s):
        me = self.me
        return remote(self.src, self.dst.at[me.slot], self.send.at[s], self.recv.at[me.slot], me.shifted(s))

    def _stay(self):
        return pltpu.make_async_copy(self.src, self.dst.at[self.me.slot], self.loc.at[0])

    def _pair(self):
        return (
            pltpu.make_async_copy(self.pair_src, self.pair_dst, self.loc.at[1]),
            remote(self.pair_src, self.pair_dst, self.send.at[0], self.recv.at[2], self.me.across()),
        )

    def start(self):
        @pl.when(self.me.home)
        def _():
            self._stay().start()
            for s in range(1, self.me.nz):
                self._copy(s).start()
            stay, there = self._pair()
            stay.start()
            there.start()

    def ready(self):
        me = self.me
        for slot in range(2):
            row = self.dst.at[slot]
            copy = remote(row, row, self.send.at[0], self.recv.at[slot], me.across())
            pl.when(me.core * (me.nz // 2) + slot != me.z)(copy.wait_recv)
        stay, there = self._pair()

        @pl.when(me.home)
        def _():
            self._stay().wait()
            stay.wait()

        pl.when(jnp.logical_not(me.home))(there.wait_recv)

    def finish(self):
        @pl.when(self.me.home)
        def _():
            for s in range(1, self.me.nz):
                self._copy(s).wait_send()
            self._pair()[1].wait_send()


def _each(count, act):
    if count <= 4:
        for m in range(count):
            act(m)
    else:

        @pl.loop(0, count)
        def _(m):
            act(m)


class Scatter:
    def __init__(self, me, kinds, g_in, keep, got, gotz, stage, g_out, before, sems):
        self.me, self.kinds, self.g_in, self.keep, self.got = me, kinds, g_in, keep, got
        self.before = before
        self.gotz, self.stage, self.g_out = gotz, stage, g_out
        self.b_send, self.b_recv, self.z_send, self.z_recv, self.f_send, self.f_recv, self.loc = sems

    @staticmethod
    def semaphores(n_w, sizes):
        dma = pltpu.SemaphoreType.DMA
        chips = sizes[0] // 2
        bits = chips.bit_length() - 1
        return [
            dma((n_w, bits, 2, chips // 2)),
            dma((n_w, bits, 2, chips // 2)),
            dma((n_w, 2)),
            dma((n_w, 2)),
            dma((n_w,)),
            dma((n_w,)),
            dma((n_w, 2, chips // 2)),
        ]

    def _count(self, step):
        return 1 << (self.me.bits - 1 - step)

    def _base(self, step):
        return sum(self._count(s) for s in range(step))

    def _first(self, j, slot, m, sent):
        bits = self.me.bits
        if slot == 0:
            flip = m + (1 << (bits - 1)) * sent
        else:
            flip = m * 2 + sent
        return self.kinds[j].piece(self.g_in[j], slot, flipped(self.me.chip, flip))

    def _held(self, j, step, slot, m, sent):
        index = m + self._count(step) * sent if slot == 0 else 2 * m + sent
        return self.got[j].at[self._base(step - 1) + index, slot]

    def _copy(self, j, step, slot, m):
        me = self.me
        bit = me.bits - 1 - step if slot == 0 else step
        src = self._first(j, slot, m, 1) if step == 0 else self._held(j, step, slot, m, 1)
        return remote(
            src,
            self.got[j].at[self._base(step) + m, slot],
            self.b_send.at[j, step, slot, m],
            self.b_recv.at[j, step, slot, m],
            me.beside(bit),
        )

    def _came(self, j, slot, m):
        return pltpu.make_async_copy(
            self.before[j][slot].at[m], self.got[j].at[m, slot], self.b_recv.at[j, 0, slot, m]
        )

    def _load(self, j, slot, m):
        return pltpu.make_async_copy(self._first(j, slot, m, 0), self.keep[j].at[slot, m], self.loc.at[j, slot, m])

    def start(self, j, step):
        for slot in range(2):
            if step == 0 and self.before[j] is not None:
                _each(self._count(step), lambda m: self._came(j, slot, m).start())
            else:
                _each(self._count(step), lambda m: self._copy(j, step, slot, m).start())
        if step == 0 and self.keep[j] is not None:
            for slot in range(2):
                _each(self._count(step), lambda m: self._load(j, slot, m).start())

    def add(self, j, step):
        for slot in range(2):

            def one(m):
                if step == 0 and self.before[j] is not None:
                    self._came(j, slot, m).wait()
                else:
                    self._copy(j, step, slot, m).wait_recv()
                if step > 0:
                    mine = self._held(j, step, slot, m, 0)
                elif self.keep[j] is not None:
                    self._load(j, slot, m).wait()
                    mine = self.keep[j].at[slot, m]
                else:
                    mine = self._first(j, slot, m, 0)
                here = self.got[j].at[self._base(step) + m, slot]
                here[...] = (here[...].astype(F32) + mine[...].astype(F32)).astype(BF16)

            _each(self._count(step), one)

    def _last(self, j, slot):
        return self.got[j].at[self._base(self.me.bits - 1), slot]

    def _z(self, j, slot, number, to):
        return remote(
            self._last(j, slot), self.gotz[j].at[number], self.z_send.at[j, number], self.z_recv.at[j, number], to
        )

    def start_z(self, j):
        self._z(j, 1 - self.me.slot, 0, self.me.neighbour()).start()

    def pass_z(self, j):
        me = self.me
        copy = self._z(j, me.slot, 0, me.neighbour())

        @pl.when(jnp.logical_not(me.home))
        def _():
            copy.wait_recv()
            here = self._last(j, me.slot)
            here[...] = (here[...].astype(F32) + self.gotz[j][0].astype(F32)).astype(BF16)
            self._z(j, me.slot, 1, me.opposite()).start()

    def _hand(self, j):
        return remote(self.stage[j], self.g_out[j], self.f_send.at[j], self.f_recv.at[j], self.me.across())

    def end_z(self, j):
        me = self.me

        @pl.when(me.home)
        def _():
            for number in range(2):
                self._z(j, me.slot, number, me.neighbour()).wait_recv()

            def total(core):
                value = self.kinds[j].half(self._last(j, me.slot), core)[...].astype(F32)
                for number in range(2):
                    value = value + self.kinds[j].half(self.gotz[j].at[number], core)[...].astype(F32)
                return value

            self.stage[j][...] = total(1 - me.core)
            self._hand(j).start()
            self.g_out[j][...] = total(me.core)

    def finish(self, j):
        me = self.me
        for step in range(0 if self.before[j] is None else 1, me.bits):
            for slot in range(2):
                _each(self._count(step), lambda m: self._copy(j, step, slot, m).wait_send())
        self._z(j, 1 - me.slot, 0, me.neighbour()).wait_send()
        far = self._z(j, me.slot, 1, me.opposite())
        pl.when(jnp.logical_not(me.home))(far.wait_send)
        hand = self._hand(j)
        pl.when(me.home)(hand.wait_send)
        pl.when(jnp.logical_not(me.home))(hand.wait_recv)


class Sums:
    def __init__(self, me, v_sum, v_got, v_all, out, sems):
        self.me, self.v_sum, self.v_got, self.v_all, self.out = me, v_sum, v_got, v_all, out
        self.b_send, self.b_recv, self.z_send, self.z_recv, self.f_send, self.f_recv = sems

    @staticmethod
    def semaphores(sizes):
        dma = pltpu.SemaphoreType.DMA
        bits = (sizes[0] // 2).bit_length() - 1
        return [dma((bits,)), dma((bits,)), dma((sizes[1],)), dma((sizes[1],)), dma((1,)), dma((1,))]

    @staticmethod
    def scratch(shape, sizes):
        bits = (sizes[0] // 2).bit_length() - 1
        return [
            pltpu.VMEM((bits + 2,) + shape, F32),
            pltpu.VMEM((bits,) + shape, F32),
            pltpu.VMEM((sizes[1],) + shape, F32),
        ]

    def _bit(self, step):
        return remote(
            self.v_sum.at[step], self.v_got.at[step], self.b_send.at[step], self.b_recv.at[step], self.me.beside(step)
        )

    def _z(self, s):
        me = self.me
        return remote(
            self.v_sum.at[me.bits], self.v_all.at[me.z], self.z_send.at[s], self.z_recv.at[me.z], me.shifted(s)
        )

    def _last(self):
        me = self.me
        return remote(self.v_sum.at[me.bits + 1], self.out.at[me.core], self.f_send.at[0], self.f_recv.at[0], me.across())

    def phases(self):
        me = self.me
        self._bit(0).start()
        yield
        for step in range(1, me.bits + 1):
            self._bit(step - 1).wait_recv()
            self.v_sum[step] = self.v_sum[step - 1] + self.v_got[step - 1]
            if step < me.bits:
                self._bit(step).start()
                yield
        for s in range(1, me.nz):
            self._z(s).start()
        self.v_all[me.z] = self.v_sum[me.bits]
        yield
        for s in range(1, me.nz):
            slab = self.v_all.at[lax.rem(me.z + s, me.nz)]
            place = lax.rem(me.z + s, me.nz)
            remote(slab, slab, self.z_send.at[0], self.z_recv.at[place], me.across()).wait_recv()
        value = self.v_all[0]
        for s in range(1, me.nz):
            value = value + self.v_all[s]
        self.v_sum[me.bits + 1] = value
        self._last().start()
        self.out[me.core] = value
        yield
        there = self.out.at[1 - me.core]
        remote(there, there, self.f_send.at[0], self.f_recv.at[0], me.across()).wait_recv()
        for step in range(me.bits):
            self._bit(step).wait_send()
        for s in range(1, me.nz):
            self._z(s).wait_send()
        self._last().wait_send()


class Outward:
    def __init__(self, me, src, dst, sems):
        self.me, self.src, self.dst = me, src, dst
        self.send, self.recv, self.loc = sems

    @staticmethod
    def semaphores(sizes):
        dma = pltpu.SemaphoreType.DMA
        return [dma((sizes[1],)), dma((2,)), dma((1,))]

    def _copy(self, place):
        me = self.me
        return remote(
            self.src.at[place], self.dst.at[me.slot], self.send.at[place], self.recv.at[me.slot], (me.dp, place)
        )

    def _stay(self, place):
        return pltpu.make_async_copy(self.src.at[place], self.dst.at[self.me.slot], self.loc.at[0])

    def start(self, place):
        me = self.me
        pl.when(jnp.logical_and(me.home, place != me.z))(lambda: self._copy(place).start())
        pl.when(jnp.logical_and(me.home, place == me.z))(lambda: self._stay(place).start())

    def finish(self):
        me = self.me
        for place in range(me.nz):
            pl.when(jnp.logical_and(me.home, place != me.z))(lambda place=place: self._copy(place).wait_send())
            pl.when(jnp.logical_and(me.home, place == me.z))(lambda place=place: self._stay(place).wait())
        for slot in range(2):
            row = self.dst.at[slot]
            copy = remote(row, row, self.send.at[0], self.recv.at[slot], me.across())
            pl.when(me.core * (me.nz // 2) + slot != me.z)(copy.wait_recv)


def send_first(kind, grad, sizes):
    n_dp, nz = sizes
    chips = n_dp // 2
    bits = chips.bit_length() - 1
    chip = lax.axis_index("dp") // 2
    grad = kind.cut(grad)
    a, b = kind.shard
    came = []
    for slot in range(2):
        bit = bits - 1 if slot == 0 else 0
        parts = []
        for m in range(chips // 2):
            there = lax.bitwise_xor(chip, m + (1 << bit) if slot == 0 else 2 * m + 1)
            if kind.by_rows:
                parts.append(lax.dynamic_slice(grad, (there * (2 * a), slot * b), kind.two))
            else:
                parts.append(lax.dynamic_slice(grad, (slot * a, there * (2 * b)), kind.two))
        pairs = [(i, (i // nz ^ (2 << bit)) * nz + i % nz) for i in range(n_dp * nz)]
        came.append(lax.ppermute(jnp.stack(parts), ("dp", "tensor"), pairs))
    return came


KEYS = 1152
STRIP = 272
COLS = 384


def _turn(x, cos, sin_up, sin_down):
    quarter = HEAD // 4
    return (
        x * cos
        + pltpu.roll(x, 2 * HEAD - quarter, 1) * sin_up
        + pltpu.roll(x, quarter, 1) * sin_down
    )


def front_kernel(
    kinds, sizes,
    tok_in, cot_in, pack_in, base_in, a_in, b_in, o_in, g_in, u_in, d_in,
    gain_ref, bias_ref, cos_ref, up_ref, down_ref, out_bias, gain2_ref, bias2_ref,
    tok_out, cot, pack, base, a_out, b_out, w_o, w_g, w_u, w_d, normed_out, qa_out, ka_out, va_out, mix_out,
    mid_out, hat_out, normed2_out, gate_out, up_out, hidden_out, totals,
    tok, w_a, w_b, normed, qa_ref, ka_ref, va_ref, mix_ref, normed2, hidden, done_sem,
    wo_v, wg_v, wu_v, part, theirs, mid_v, hat_v, gate_v, up_v, act_v, own_sums, their_sums, p_send, p_recv, r_send, r_recv, out_sem, w_sem,
    *sems,
):
    me = Place(*sizes)
    nz = sizes[1]
    gather = Gather(me, kinds, (a_in, b_in, o_in, g_in, u_in, d_in), (w_a, w_b, w_o, w_g, w_u, w_d), sems[:7])
    tokens = Inward(me, tok_in, tok, sems[7:12])
    cots = Inward(me, cot_in, cot, sems[12:17])
    packs = Packs(me, pack_in, pack, base_in, base, sems[17:20])
    n_w = len(kinds)
    leaving = []

    def leave(src, dst):
        copy = pltpu.make_async_copy(src, dst, done_sem.at[len(leaving)])
        copy.start()
        leaving.append(copy)

    me.barrier()
    for j in range(n_w):
        gather.first_hop(j)
    for j in (0, 1, 3, 2):
        gather.start_z(j)
    packs.start()

    def flow(j):
        gather.wait_z(j)
        gather.start_bits(j, 0)
        yield
        for step in range(1, me.bits):
            gather.wait_bits(j, step - 1)
            gather.start_bits(j, step)
        yield

    flows = [flow(j) for j in range(n_w)]
    gather.pass_z(0)
    next(flows[0])
    gather.pass_z(1)
    next(flows[1])
    next(flows[0])
    gather.pass_z(3)
    next(flows[1])
    next(flows[3])
    gather.pass_z(2)
    tokens.start()
    for j in (4, 5):
        gather.start_z(j)
    next(flows[2])
    next(flows[3])
    tokens.pass_on()
    tokens.ready()
    packs.ready()
    gather.pass_z(4)
    next(flows[2])

    block = tok.shape[1]
    rows = block * nz
    width = tok.shape[2]
    lanes = 2 * HEAD
    lane = lax.broadcasted_iota(jnp.int32, (block, lanes), 1)
    low = lane < HEAD
    one = jnp.where(lane == HEAD, 1.0, 0.0)
    ones = jnp.where((lane >= HEAD) & (lane < HEAD + 3), 1.0, 0.0)

    @pl.loop(0, nz)
    def _(t):
        x = tok[t].astype(F32)
        mean = jnp.sum(x, axis=1, keepdims=True) * (1.0 / width)
        x = x - mean
        var = jnp.sum(x * x, axis=1, keepdims=True) * (1.0 / width)
        x = x * lax.rsqrt(var + EPS)
        normed[pl.ds(pl.multiple_of(t * block, block), block), :] = (x * gain_ref[...] + bias_ref[...]).astype(BF16)

    gather.wait_bits(0, me.bits - 1)
    gather.wait_bits(1, me.bits - 1)
    leave(tok, tok_out)
    leave(w_a, a_out)
    leave(w_b, b_out)
    leave(normed, normed_out)
    pairs = mix_ref.shape[1] // lanes
    sub = pairs // 2

    def project(g):
        weight = (w_a, w_b)[g % sub]

        def column(part):
            at = ((g // sub) * 3 + part) * lanes
            return weight[:, at : at + lanes]

        q_bias = pack[g // sub, 0:1, (g % sub) * lanes : (g % sub + 1) * lanes]
        v_bias = pack[g // sub, 1:2, (g % sub) * lanes : (g % sub + 1) * lanes]

        @pl.loop(0, nz)
        def _(t):
            here = pl.ds(pl.multiple_of(t * block, block), block)
            x = normed[here, :]
            both = matmul(x, jnp.concatenate([column(0), column(1)], axis=1))
            tables = (cos_ref[here, :], up_ref[here, :], down_ref[here, :])
            query = _turn(both[:, :lanes] + q_bias, *tables) * (SCALE * LOG2E)
            key = _turn(both[:, lanes:], *tables)
            value = matmul(x, column(2)) + v_bias
            mask = base[here, :].astype(F32)
            for h in range(2):
                if h:
                    query, key, value = (pltpu.roll(v, HEAD, 1) for v in (query, key, value))
                qa_ref[2 * g + h, here, :] = jnp.where(low, query, one).astype(BF16)
                ka_ref[2 * g + h, here, :] = jnp.where(low, key, mask).astype(BF16)
                va_ref[2 * g + h, here, :] = jnp.where(low, value, ones).astype(BF16)

        rest = pl.ds(rows, KEYS - rows)
        for h in range(2):
            qa_ref[2 * g + h, rest, :] = jnp.zeros((KEYS - rows, lanes), BF16)
            va_ref[2 * g + h, rest, :] = jnp.zeros((KEYS - rows, lanes), BF16)
            ka_ref[2 * g + h, rest, :] = base[rest, :]

    def attend(g):
        @pl.loop(0, nz)
        def _(t):
            here = pl.ds(pl.multiple_of(t * block, block), block)
            outs = []
            for h in range(2):
                q = qa_ref[2 * g + h, here, :]
                s = matmul_right_t(q, ka_ref[2 * g + h])
                top = jnp.max(s, axis=1, keepdims=True)
                p = jnp.exp2(s - top).astype(BF16)
                o = matmul(p, va_ref[2 * g + h])
                total = o[:, HEAD : HEAD + 1]
                outs.append(o / total)
                log = -(top + jnp.log2(total))
                first = log.astype(BF16)
                left = log - first.astype(F32)
                second = left.astype(BF16)
                third = (left - second.astype(F32)).astype(BF16)
                logs = jnp.where(
                    lane == HEAD + 1,
                    first.astype(F32),
                    jnp.where(lane == HEAD + 2, second.astype(F32), third.astype(F32)),
                )
                inside = (lane > HEAD) & (lane <= HEAD + 3)
                qa_ref[2 * g + h, here, :] = jnp.where(inside, logs, q.astype(F32)).astype(BF16)
            mix_ref[here, g * lanes : (g + 1) * lanes] = jnp.where(
                low, outs[0], pltpu.roll(outs[1], HEAD, 1)
            ).astype(BF16)

        for src, dst in ((qa_ref, qa_out), (ka_ref, ka_out), (va_ref, va_out)):
            leave(src.at[pl.ds(2 * g, 2)], dst.at[pl.ds(2 * g, 2)])

    project(0)
    next(flows[4])
    gather.pass_z(5)
    attend(0)
    next(flows[5])
    project(1)
    attend(1)
    next(flows[4])
    project(2)
    attend(2)
    next(flows[5])
    cots.start()
    project(3)
    attend(3)

    def load(j, there):
        gather.wait_bits(j, me.bits - 1)
        copy = pltpu.make_async_copy(gather.w_out[j], there, w_sem.at[j])
        copy.start()
        return copy

    def swap(t):
        return remote(part.at[t], theirs.at[t], p_send.at[t], p_recv.at[t], me.across())

    def swap_sums(t):
        return remote(own_sums.at[t], their_sums.at[t], r_send.at[t], r_recv.at[t], me.across())

    def save(t):
        slot = t % 2
        return [
            pltpu.make_async_copy(mid_v.at[slot], mid_out.at[t], out_sem.at[0, slot]),
            pltpu.make_async_copy(gate_v.at[slot], gate_out.at[t], out_sem.at[1, slot]),
            pltpu.make_async_copy(up_v.at[slot], up_out.at[t], out_sem.at[2, slot]),
            pltpu.make_async_copy(hat_v.at[slot], hat_out.at[t], out_sem.at[3, slot]),
        ]

    leave(mix_ref, mix_out)
    loads = [load(2, wo_v), load(3, wg_v)]
    loads[0].wait()
    for t in range(nz):
        mixed = mix_ref[t * block : (t + 1) * block, :]
        product = matmul_right_t(mixed, wo_v[...]) if kinds[2].turn else matmul(mixed, wo_v[...])
        part[t] = product.astype(BF16)
        swap(t).start()

    ff = hidden.shape[1] // 2
    wide = up_to(ff, LANES)
    place = lax.broadcasted_iota(jnp.int32, (1, 2 * wide), 1)

    def row(n):
        blank = jnp.zeros((1, wide), F32)
        first = jnp.concatenate([pack[0, n : n + 1, :wide], blank], axis=1)
        second = jnp.concatenate([pack[1, n : n + 1, :wide], blank], axis=1)
        return jnp.where(place < ff, first, pltpu.roll(second, ff, 1))[:, : 2 * ff]

    g_bias, u_bias, inner_gain, inner_shift, columns = (row(n) for n in range(2, 7))
    count = float(FF - PADCOLS)

    def finish_tile(t):
        slot = t % 2
        swap_sums(t).wait_recv()
        total = own_sums[t] + their_sums[t]
        totals[t] = jnp.where(lane < 2, total, totals[t])
        mean = total[:, 0:1] / count
        var = total[:, 1:2] / count - mean * mean
        nhat = (act_v[slot] - mean) * lax.rsqrt(var + EPS)
        here = pl.ds(t * block, block)
        hidden[here, :] = (columns * (nhat * inner_gain + inner_shift)).astype(BF16)
        leave(hidden.at[here], hidden_out.at[here])
        leave(normed2.at[here], normed2_out.at[here])

    for t in range(nz):
        slot = t % 2
        if t >= 2:
            for copy in save(t - 2):
                copy.wait()
        swap(t).wait_recv()
        x = tok[t].astype(F32) + (part[t].astype(F32) + theirs[t].astype(F32)) + out_bias[...]
        mid_v[slot] = x
        x = x - jnp.sum(x, axis=1, keepdims=True) * (1.0 / width)
        var = jnp.sum(x * x, axis=1, keepdims=True) * (1.0 / width)
        scale = lax.rsqrt(var + EPS)
        totals[t] = jnp.broadcast_to(scale, (block, lanes))
        x = x * scale
        hat_v[slot] = x
        x = (x * gain2_ref[...] + bias2_ref[...]).astype(BF16)
        normed2[t * block : (t + 1) * block, :] = x
        if t == 0:
            loads.append(load(4, wu_v))
            loads[1].wait()
        gate = (matmul(x, wg_v[...]) if kinds[3].turn else matmul_right_t(x, wg_v[...])) + g_bias
        gate_v[slot] = gate
        if t == 0:
            loads[2].wait()
        up = (matmul(x, wu_v[...]) if kinds[4].turn else matmul_right_t(x, wu_v[...])) + u_bias
        up_v[slot] = up
        gate = gate_v[slot]
        act = gate * (1.0 / (1.0 + jnp.exp(-gate))) * up
        act_v[slot] = act
        live = act * columns
        first = jnp.sum(live, axis=1, keepdims=True)
        second = jnp.sum(live * act, axis=1, keepdims=True)
        own_sums[t] = jnp.where(lane == 0, first, jnp.where(lane == 1, second, 0.0))
        swap_sums(t).start()
        for copy in save(t):
            copy.start()
        if t >= 1:
            finish_tile(t - 1)
    finish_tile(nz - 1)
    cots.pass_on()
    for t in range(nz - 2, nz):
        for copy in save(t):
            copy.wait()
    gather.wait_bits(5, me.bits - 1)
    for copy in leaving:
        copy.wait()
    for t in range(nz):
        swap(t).wait_send()
        swap_sums(t).wait_send()
    cots.ready()
    for j in range(n_w):
        gather.finish(j)
    tokens.finish()
    cots.finish()
    packs.finish()


def front(tokens, cotangent, pack, base, weights, kinds, gain, bias, tables, more, n_head, ff, sizes, cid):
    nz = sizes[1]
    block, width = tokens.shape[1:]
    rows = block * nz
    lanes = 2 * HEAD
    heads = 2 * n_head // HEAD
    hbm = pl.BlockSpec(memory_space=pltpu.HBM)
    vmem = pl.BlockSpec(memory_space=pltpu.VMEM)
    shape = jax.ShapeDtypeStruct
    weights = [k.enter(w) for k, w in zip(kinds, weights)]
    shapes = [
        shape((nz, block, width), BF16),
        shape((nz, block, width), BF16),
        shape((2,) + pack.shape, F32),
        shape(base.shape, BF16),
        *[shape(k.whole, BF16) for k in kinds],
        shape((rows, width), BF16),
        *[shape((heads, KEYS, lanes), BF16)] * 3,
        shape((rows, heads * HEAD), BF16),
        shape((nz, block, width), F32),
        shape((nz, block, width), F32),
        shape((rows, width), BF16),
        shape((nz, block, 2 * ff), F32),
        shape((nz, block, 2 * ff), F32),
        shape((rows, 2 * ff), BF16),
        shape((nz, block, lanes), F32),
    ]
    dma = pltpu.SemaphoreType.DMA
    out = pl.pallas_call(
        functools.partial(front_kernel, kinds, sizes),
        out_shape=shapes,
        in_specs=[hbm] * 10 + [vmem] * 8,
        out_specs=[hbm, hbm, vmem, vmem] + [hbm] * 17 + [vmem],
        scratch_shapes=[
            pltpu.VMEM((nz, block, width), BF16),
            pltpu.VMEM(kinds[0].whole, BF16),
            pltpu.VMEM(kinds[1].whole, BF16),
            pltpu.VMEM((rows, width), BF16),
            *[pltpu.VMEM((heads, KEYS, lanes), BF16)] * 3,
            pltpu.VMEM((rows, heads * HEAD), BF16),
            pltpu.VMEM((rows, width), BF16),
            pltpu.VMEM((rows, 2 * ff), BF16),
            dma((5 + 3 * heads // 2 + 2 * nz,)),
        ]
        + [pltpu.VMEM(k.whole, BF16) for k in kinds[2:5]]
        + [pltpu.VMEM((nz, block, width), BF16)] * 2
        + [pltpu.VMEM((2, block, width), F32)] * 2
        + [pltpu.VMEM((2, block, 2 * ff), F32)] * 3
        + [pltpu.VMEM((nz, block, lanes), F32)] * 2
        + [dma((nz,)), dma((nz,)), dma((nz,)), dma((nz,)), dma((4, 2)), dma((len(kinds),))]
        + Gather.semaphores(len(kinds), sizes)
        + Inward.semaphores(sizes)
        + Inward.semaphores(sizes)
        + Packs.semaphores(sizes),
        compiler_params=pltpu.CompilerParams(
            collective_id=cid, has_side_effects=True, vmem_limit_bytes=60 * 2**20
        ),
        name="front",
    )(tokens, cotangent, pack, base, *weights, gain[None], bias[None], *tables, *[v[None] for v in more])
    return out[:4], [k.join(w) for k, w in zip(kinds, out[4:10])], out[10:]


def back_kernel(
    kinds, sizes, n_late, n_before,
    out_in, g_d, g_g, g_u, g_o, qa_in, ka_in, va_in, do_in, mix_in, normed_in, wa_in, wb_in, x_in, dmid_in,
    cos_ref, up_ref, down_ref, gain_ref, vec_ref,
    *rest,
):
    me = Place(*sizes)
    nz, bits = me.nz, me.bits
    before = [rest[2 * j : 2 * j + 2] if j < n_before else None for j in range(len(kinds))]
    rest = rest[2 * n_before :]
    out_rows, in_rows, vec_out = rest[:3]
    g_out = rest[3 : 3 + len(kinds)]
    rest = rest[3 + len(kinds) :]
    n_w = len(kinds)
    keep = rest[: n_w - 2] + (None, None)
    rest = rest[n_w - 2 :]
    got, gotz, stage = (rest[i * n_w : (i + 1) * n_w] for i in range(3))
    rest = rest[3 * n_w :]
    v_sum, v_got, v_all = rest[:3]
    (qa, ka, va, do, mix, normed, w, x_ref, dmid, d_qkv, g_a, g_b, part, theirs, da, dq, dk, dv, dgain, dshift) = rest[3:23]
    sems = rest[23:]
    scatter = Scatter(
        me, kinds, (g_d, g_g, g_u, g_o, g_a, g_b), keep, got, gotz, stage, g_out, before, sems[:7]
    )
    sums = Sums(me, v_sum, v_got, v_all, vec_out, sems[7:13])
    outs = Outward(me, out_in, out_rows, sems[13:16])
    ins = Outward(me, theirs, in_rows, sems[16:19])
    pair_sem, late_sem, tile_sem, p_send, p_recv = sems[19:24]

    block, width = x_ref.shape[1:]
    rows = block * nz
    lanes = 2 * HEAD
    pairs = mix_in.shape[1] // lanes
    sub = pairs // 2
    lane = lax.broadcasted_iota(jnp.int32, (block, lanes), 1)
    low = lane < HEAD

    turns = [slot * sub + s for s in range(sub) for slot in range(pairs // sub)]

    def loads(n):
        slot = n % 2
        g = turns[n]
        heads = pl.ds(2 * g, 2)
        cols = pl.ds(g * lanes, lanes)
        return [
            pltpu.make_async_copy(qa_in.at[heads], qa.at[slot], pair_sem.at[slot, 0]),
            pltpu.make_async_copy(ka_in.at[heads], ka.at[slot], pair_sem.at[slot, 1]),
            pltpu.make_async_copy(va_in.at[heads], va.at[slot], pair_sem.at[slot, 2]),
            pltpu.make_async_copy(do_in.at[:, cols], do.at[slot], pair_sem.at[slot, 3]),
            pltpu.make_async_copy(mix_in.at[:, cols], mix.at[slot], pair_sem.at[slot, 4]),
        ]

    late = [
        pltpu.make_async_copy(normed_in, normed, late_sem.at[0]),
        pltpu.make_async_copy(wa_in, w.at[:, pl.ds(0, wa_in.shape[1])], late_sem.at[1]),
        pltpu.make_async_copy(wb_in, w.at[:, pl.ds(wa_in.shape[1], wa_in.shape[1])], late_sem.at[2]),
    ]

    def tile_loads(t):
        slot = t % 2
        return [
            pltpu.make_async_copy(x_in.at[t], x_ref.at[slot], tile_sem.at[slot, 0]),
            pltpu.make_async_copy(dmid_in.at[t], dmid.at[slot], tile_sem.at[slot, 1]),
        ]

    me.barrier()
    scatter.start(0, 0)
    scatter.start(1, 0)
    scatter.start(2, 0)
    for copy in loads(0):
        copy.start()
    for place in range(nz):
        outs.start(place)
    for copy in late:
        copy.start()
    for t in range(2):
        for copy in tile_loads(t):
            copy.start()
    v_sum[0] = vec_ref[...]

    def flow(j):
        for step in range(bits):
            scatter.add(j, step)
            if step + 1 < bits:
                scatter.start(j, step + 1)
            else:
                scatter.start_z(j)
            yield

    flows = [flow(j) for j in range(n_w)]

    def rest_of(j):
        for _ in flows[j]:
            pass

    def head(n, h):
        slot = n % 2

        @pl.loop(0, nz)
        def _(t):
            here = pl.ds(pl.multiple_of(t * block, block), block)
            d = do[slot, here, :].astype(F32)
            mine = low if h == 0 else jnp.logical_not(low)
            delta = -jnp.sum(
                jnp.where(mine, d * mix[slot, here, :].astype(F32), 0.0), axis=1, keepdims=True
            )
            if h:
                d = pltpu.roll(d, HEAD, 1)
            first = delta.astype(BF16)
            left = delta - first.astype(F32)
            second = left.astype(BF16)
            third = (left - second.astype(F32)).astype(BF16)
            logs = jnp.where(
                lane == HEAD,
                first.astype(F32),
                jnp.where(lane == HEAD + 1, second.astype(F32), third.astype(F32)),
            )
            da[here, :] = jnp.where(low, d, jnp.where(lane < HEAD + 3, logs, 0.0)).astype(BF16)

        dk[h] = jnp.zeros((KEYS, lanes), F32)
        dv[h] = jnp.zeros((KEYS, lanes), F32)

        def some(here):
            q = qa[slot, h, here, :]
            d = da[here, :]
            p = jnp.exp2(matmul_right_t(ka[slot, h], q))
            ds = (p * matmul_right_t(va[slot, h], d)).astype(BF16)
            dv[h] += matmul(p.astype(BF16), d)
            dk[h] += matmul(ds, q)
            dq[h, here, :] = matmul_left_t(ds, ka[slot, h])

        @pl.loop(0, KEYS // COLS)
        def _(t):
            some(pl.ds(pl.multiple_of(t * COLS, COLS), COLS))

        if KEYS % COLS:
            some(pl.ds(KEYS - KEYS % COLS, KEYS % COLS))

    def put(g, part_of, row, ref, factor, turn):
        at = ((g % sub) * (pairs // sub) * 3 + (g // sub) * 3 + part_of) * lanes

        def one(t, total):
            here = pl.ds(pl.multiple_of(t * block, block), block)
            value = jnp.where(low, ref[0, here, :], pltpu.roll(ref[1, here, :], HEAD, 1))
            if factor is not None:
                value = value * factor
            if turn:
                value = _turn(value, cos_ref[here, :], -up_ref[here, :], -down_ref[here, :])
            d_qkv[here, at : at + lanes] = value.astype(BF16)
            return total + jnp.sum(value, axis=0, keepdims=True)

        total = lax.fori_loop(0, nz, one, jnp.zeros((1, lanes), F32))
        if row is not None:
            v_sum[0, row : row + 1, :] = total

    da[pl.ds(rows, KEYS - rows), :] = jnp.zeros((KEYS - rows, lanes), BF16)

    def weight_gradient(s):
        into = (g_a, g_b)[s]
        columns = into.shape[1]
        grad = d_qkv[:, s * columns : (s + 1) * columns]
        step = max(kinds[-1].two[0], lanes)
        for c in range(width // step):
            left = normed[:, c * step : (c + 1) * step]
            into[c * step : (c + 1) * step, :] = matmul_left_t(left, grad).astype(BF16)

    def fetch(g):
        for copy in loads(g):
            copy.wait()
        if g + 1 < pairs:
            for copy in loads(g + 1):
                copy.start()

    def write(n):
        g = turns[n]
        base_row = n_late + (g // sub) * (2 * sub) + g % sub
        put(g, 0, base_row, dq, SCALE, True)
        put(g, 1, None, dk, LN2, True)
        put(g, 2, base_row + sub, dv, None, False)

    def swap(t):
        return remote(part.at[t], theirs.at[t], p_send.at[t], p_recv.at[t], me.across())

    def partial():
        for t in range(nz):
            here = slice(t * block, (t + 1) * block)
            part[t] = matmul_right_t(d_qkv[here, :], w[...]).astype(BF16)
            swap(t).start()

    def input_gradient():
        dgain[...] = jnp.zeros_like(dgain)
        dshift[...] = jnp.zeros_like(dshift)
        for t in range(nz):
            for copy in tile_loads(t):
                copy.wait()
            swap(t).wait_recv()

            @pl.loop(0, block // STRIP)
            def _(i, t=t):
                here = pl.ds(pl.multiple_of(i * STRIP, STRIP), STRIP)
                x = x_ref[t % 2, here, :].astype(F32)
                x = x - jnp.sum(x, axis=1, keepdims=True) * (1.0 / width)
                var = jnp.sum(x * x, axis=1, keepdims=True) * (1.0 / width)
                scale = lax.rsqrt(var + EPS)
                x = x * scale
                dn = part[t, here, :].astype(F32) + theirs[t, here, :].astype(F32)
                dgain[...] += dn * x
                dshift[...] += dn
                v = dn * gain_ref[...]
                mean = jnp.sum(v, axis=1, keepdims=True) * (1.0 / width)
                along = jnp.sum(v * x, axis=1, keepdims=True) * (1.0 / width)
                theirs[t, here, :] = (dmid[t % 2, here, :] + scale * (v - mean - x * along)).astype(BF16)

            ins.start(t)
            if t == 1:
                rest_of(5)
            if t + 2 < nz:
                for copy in tile_loads(t + 2):
                    copy.start()
        per = width // lanes
        whole_gain = jnp.sum(dgain[...], axis=0, keepdims=True)
        whole_shift = jnp.sum(dshift[...], axis=0, keepdims=True)
        for i in range(per):
            v_sum[0, i : i + 1, :] = whole_gain[:, i * lanes : (i + 1) * lanes]
            v_sum[0, per + i : per + i + 1, :] = whole_shift[:, i * lanes : (i + 1) * lanes]

    next(flows[0], None)
    next(flows[1], None)
    scatter.start(3, 0)
    fetch(0)
    head(0, 0)
    head(0, 1)
    write(0)
    next(flows[2], None)
    fetch(1)
    head(1, 0)
    rest_of(0)
    head(1, 1)
    write(1)
    rest_of(1)
    for copy in late:
        copy.wait()
    weight_gradient(0)
    scatter.start(4, 0)
    next(flows[3], None)
    scatter.pass_z(0)
    fetch(2)
    head(2, 0)
    rest_of(2)
    scatter.pass_z(1)
    head(2, 1)
    write(2)
    next(flows[4], None)
    scatter.end_z(0)
    fetch(3)
    head(3, 0)
    rest_of(3)
    scatter.pass_z(2)
    scatter.end_z(1)
    head(3, 1)
    write(3)
    rest_of(4)
    weight_gradient(1)
    scatter.start(5, 0)
    scatter.pass_z(3)
    partial()
    next(flows[5], None)
    scatter.pass_z(4)
    scatter.end_z(2)
    input_gradient()
    small = sums.phases()
    next(small, None)
    scatter.pass_z(5)
    next(small, None)
    scatter.end_z(3)
    next(small, None)
    scatter.end_z(4)
    for _ in small:
        pass
    scatter.end_z(5)
    for t in range(nz):
        swap(t).wait_send()
    outs.finish()
    ins.finish()
    for j in range(n_w):
        scatter.finish(j)


def back(out_act, grads, before, heads, d_mixed, mixed, normed, weights, x, dmid, tables, gain, vec, kinds, n_late, sizes, cid):
    n_dp, nz = sizes
    chips = n_dp // 2
    n_w = len(kinds)
    block, width = x.shape[1:]
    rows = block * nz
    lanes = 2 * HEAD
    hbm = pl.BlockSpec(memory_space=pltpu.HBM)
    vmem = pl.BlockSpec(memory_space=pltpu.VMEM)
    shape = jax.ShapeDtypeStruct
    dma = pltpu.SemaphoreType.DMA
    grads = [k.cut(g) for k, g in zip(kinds, grads)]
    out = pl.pallas_call(
        functools.partial(back_kernel, kinds, sizes, n_late, len(before)),
        out_shape=[shape((nz // 2, block, width), BF16)] * 2
        + [shape((2,) + vec.shape, F32)]
        + [shape(k.shard, F32) for k in kinds],
        in_specs=[hbm] * 15 + [vmem] * 5 + [hbm] * (2 * len(before)),
        out_specs=[hbm, hbm] + [vmem] * (1 + n_w),
        scratch_shapes=[pltpu.VMEM((2, chips // 2) + k.two, BF16) for k in kinds[:-2]]
        + [pltpu.VMEM((chips - 1, 2) + k.two, BF16) for k in kinds]
        + [pltpu.VMEM((2,) + k.two, BF16) for k in kinds]
        + [pltpu.VMEM(k.shard, F32) for k in kinds]
        + Sums.scratch(vec.shape, sizes)
        + [pltpu.VMEM((2, 2, KEYS, lanes), BF16)] * 3
        + [pltpu.VMEM((2, rows, lanes), BF16)] * 2
        + [
            pltpu.VMEM((rows, width), BF16),
            pltpu.VMEM((width, 2 * weights[0].shape[1]), BF16),
            pltpu.VMEM((2, block, width), BF16),
            pltpu.VMEM((2, block, width), F32),
            pltpu.VMEM((rows, 2 * weights[0].shape[1]), BF16),
            pltpu.VMEM((width, weights[0].shape[1]), BF16),
            pltpu.VMEM((width, weights[0].shape[1]), BF16),
            pltpu.VMEM((nz, block, width), BF16),
            pltpu.VMEM((nz, block, width), BF16),
            pltpu.VMEM((KEYS, lanes), BF16),
        ]
        + [pltpu.VMEM((2, KEYS, lanes), F32)] * 3
        + [pltpu.VMEM((STRIP, width), F32)] * 2
        + Scatter.semaphores(n_w, sizes)
        + Sums.semaphores(sizes)
        + Outward.semaphores(sizes)
        + Outward.semaphores(sizes)
        + [dma((2, 5)), dma((3,)), dma((2, 2)), dma((nz,)), dma((nz,))],
        compiler_params=pltpu.CompilerParams(
            collective_id=cid, has_side_effects=True, vmem_limit_bytes=62 * 2**20
        ),
        name="back",
    )(out_act, *grads, *heads, d_mixed, mixed, normed, *weights, x, dmid, *tables, gain[None], vec, *[r for pair in before for r in pair])
    return out[:2], out[2], [k.leave(g) for k, g in zip(kinds, out[3:])]


def shards(
    tokens_in, cotangent, image_flag, key_mask, column_mask,
    attention_norm_gain, attention_norm_bias, w_query, w_key, w_value, query_bias, value_bias, w_out, out_bias,
    feedforward_norm_gain, feedforward_norm_bias, w_gate, gate_bias, w_up, up_bias, inner_gain, inner_shift,
    w_down, down_bias,
):
    n_dp, n_tensor = lax.axis_size("dp"), lax.axis_size("tensor")
    sizes = (n_dp, n_tensor)
    dp, z = lax.axis_index("dp"), lax.axis_index("tensor")
    core = dp % 2
    block = tokens_in.shape[1]
    width = tokens_in.shape[2]
    length = block * n_tensor
    block_pad = up_to(block, 16)
    rows = block_pad * n_tensor
    n_head = w_query.shape[1]
    n_ff = w_gate.shape[1]
    ff = up_to(n_ff, 16 if w_down.shape[1] % LANES == 0 else LANES)
    count_live = float(FF - PADCOLS)
    swap = [(i, (i // n_tensor ^ 1) * n_tensor + i % n_tensor) for i in range(n_dp * n_tensor)]

    def other(value):
        return lax.ppermute(value, ("dp", "tensor"), swap)

    pair = 2 * HEAD
    shard_a, shard_b = (
        jnp.concatenate([v[:, s * pair : (s + 1) * pair] for v in (w_query, w_key, w_value)], axis=1) for s in range(2)
    )
    kind_p = Kind(True, shard_a.shape, n_dp)
    kind_o = Kind(False, w_out.shape, n_dp)
    kind_f = Kind(False, (ff, w_down.shape[1]), n_dp)

    def turned(weight):
        return jnp.pad(weight.T, ((0, ff - n_ff), (0, 0)))

    def pad_rows(value):
        return jnp.pad(value, ((0, 0), (0, block_pad - block), (0, 0)))

    wide = up_to(ff, LANES)
    small = jnp.stack(
        [
            jnp.pad(v, (0, wide - v.shape[0]))
            for v in (query_bias, value_bias, gate_bias, up_bias, inner_gain, inner_shift, column_mask.astype(F32))
        ]
        + [jnp.zeros((wide,), F32)]
    )
    own_image = z % (n_tensor // 2)
    live = lax.dynamic_index_in_dim(key_mask, own_image, 0, False)
    live = jnp.pad(live.reshape(n_tensor, block), ((0, 0), (0, block_pad - block))).reshape(rows)
    live = jnp.pad(live, (0, KEYS - rows))
    lane = jnp.arange(LANES)[None, :]
    base = jnp.where(
        lane == HEAD,
        jnp.where(live > 0, 0.0, -1e30)[:, None],
        jnp.where(
            (lane > HEAD) & (lane <= HEAD + 3),
            1.0,
            jnp.where(lane == LANES - 1, lax.dynamic_index_in_dim(image_flag, own_image, 0, False).astype(F32), 0.0),
        ),
    ).astype(BF16)
    tables = lane_tables(length, HEAD // 4, block, block_pad)

    (image, cot, packs, base), full, kept = front(
        pad_rows(tokens_in),
        pad_rows(cotangent),
        small,
        base,
        [shard_a, shard_b, w_out, turned(w_gate), turned(w_up), jnp.pad(w_down, ((0, ff - n_ff), (0, 0)))],
        [kind_p, kind_p, kind_o, kind_f, kind_f, kind_f],
        attention_norm_gain,
        attention_norm_bias,
        tables,
        (out_bias, feedforward_norm_gain, feedforward_norm_bias),
        n_head,
        ff,
        sizes,
        0,
    )
    normed, qa, ka, va, mixed, middle, xhat2, normed2, gate, up, hidden, sums = kept
    full_a, full_b, full_o, full_g, full_u, full_d = full
    gain, shift, columns = (packs[:, n, :ff].reshape(-1) for n in range(4, 7))
    flag = base[0, LANES - 1].astype(F32)
    middle = middle.reshape(rows, width)
    xhat2 = xhat2.reshape(rows, width)
    gate, up = gate.reshape(rows, -1), up.reshape(rows, -1)
    sig = jax.nn.sigmoid(gate)
    act = gate * sig * up
    sums = sums.reshape(rows, -1)
    s2 = sums[:, 2:3]
    mean = sums[:, 0:1] / count_live
    var = sums[:, 1:2] / count_live - mean * mean
    r = lax.rsqrt(var + EPS)
    nhat = (act - mean) * r
    part = matmul(hidden, full_d).astype(BF16)
    output = (middle + (part.astype(F32) + other(part).astype(F32)) + down_bias).astype(BF16)

    grad = cot.reshape(rows, width).astype(F32) * flag
    grad_low = grad.astype(BF16)
    g_down = matmul_left_t(hidden, grad_low).astype(BF16)
    dn = columns * lax.dot_general(
        grad_low, full_d, (((1,), (1,)), ((), ())), preferred_element_type=F32
    )
    g_gain = jnp.sum(dn * nhat, axis=0)
    g_shift = jnp.sum(dn, axis=0)
    dnh = dn * gain
    rsums = jnp.stack([jnp.sum(dnh, axis=-1), jnp.sum(dnh * nhat, axis=-1)])
    rsums = rsums + other(rsums)
    dact = r * (dnh - columns * (rsums[0][:, None] + nhat * rsums[1][:, None]) / count_live)
    dgate = dact * up * sig * (1.0 + gate * (1.0 - sig))
    dup = dact * gate * sig
    g_gate_bias = jnp.sum(dgate, axis=0)
    g_up_bias = jnp.sum(dup, axis=0)
    gate_low = dgate.astype(BF16)
    up_low = dup.astype(BF16)
    g_gate = matmul_left_t(gate_low, normed2).astype(BF16)
    g_up = matmul_left_t(up_low, normed2).astype(BF16)
    part = (matmul(gate_low, full_g) + matmul(up_low, full_u)).astype(BF16)
    dnormed2 = part.astype(F32) + other(part).astype(F32)
    g_mlp_gain = jnp.sum(dnormed2 * xhat2, axis=0)
    g_mlp_shift = jnp.sum(dnormed2, axis=0)
    dmiddle = grad + norm_backward(dnormed2, xhat2, s2, feedforward_norm_gain)
    g_out_bias = jnp.sum(dmiddle, axis=0)
    g_down_bias = jnp.sum(grad, axis=0)
    dmid_low = dmiddle.astype(BF16)
    g_out = matmul_left_t(mixed, dmid_low).astype(BF16)
    d_mixed = matmul_right_t(dmid_low, full_o).astype(BF16)
    early = jnp.concatenate([g_out_bias, g_mlp_gain, g_mlp_shift, g_down_bias])
    late_rows = 2 * width // LANES
    qv_rows = 4 * n_head // LANES
    tall = jnp.concatenate(
        [v.reshape(2, -1) for v in (g_gate_bias, g_up_bias, g_gain, g_shift)], axis=1
    ).reshape(-1)
    vec = jnp.concatenate([jnp.zeros(((late_rows + qv_rows) * LANES,), F32), early, tall])
    vec_rows = up_to(up_to(vec.shape[0], LANES) // LANES, 8)
    vec = jnp.pad(vec, (0, vec_rows * LANES - vec.shape[0])).reshape(vec_rows, LANES)
    (out_rows, in_rows), vec, (s_down, s_gate, s_up, s_out, s_a, s_b) = back(
        output.reshape(n_tensor, block_pad, width),
        [g_down, g_gate, g_up, g_out],
        [send_first(kind_f, g, sizes) for g in (g_down, g_gate)],
        [qa, ka, va],
        d_mixed,
        mixed,
        normed,
        [full_a, full_b],
        image,
        dmiddle.reshape(n_tensor, block_pad, width),
        tables,
        attention_norm_gain,
        vec,
        [kind_f, kind_f, kind_f, kind_o, kind_p, kind_p],
        late_rows,
        sizes,
        1,
    )
    out_rows, in_rows = out_rows[:, :block], in_rows[:, :block]
    vec = vec.reshape(2, -1)
    owner = z // (n_tensor // 2)
    mine = lax.dynamic_index_in_dim(vec, owner, 0, False)
    d_at = (late_rows + qv_rows) * LANES
    wide = jnp.concatenate([vec[0, : 2 * width], vec[0, d_at : d_at + 4 * width]]).reshape(6, width)
    qv = lax.dynamic_index_in_dim(mine[late_rows * LANES : d_at].reshape(2, -1), z % (n_tensor // 2), 0, False)
    tall = mine[d_at + 4 * width : d_at + 4 * width + 8 * ff].reshape(2, -1)
    tall = lax.dynamic_index_in_dim(tall, z % (n_tensor // 2), 0, False)
    pieces, at = [qv[:n_head], qv[n_head:]], 0
    for size in [ff] * 4:
        pieces.append(tall[at : at + size])
        at += size
    return (
        out_rows,
        in_rows.astype(F32),
        wide[0],
        wide[1],
        *[jnp.concatenate([v[:, n * pair : (n + 1) * pair] for v in (s_a, s_b)], axis=1) for n in range(3)],
        pieces[0],
        pieces[1],
        s_out,
        wide[2],
        wide[3],
        wide[4],
        s_gate[:n_ff].T,
        pieces[2][:n_ff],
        s_up[:n_ff].T,
        pieces[3][:n_ff],
        pieces[4][:n_ff],
        pieces[5][:n_ff],
        s_down[:n_ff],
        wide[5],
    )


def solution(mesh):
    act, row, col, vec = P("dp", "tensor", None), P("dp", "tensor"), P("tensor", "dp"), P("tensor")
    in_specs = (
        act, act, P("dp"), P("dp", None), vec, P(), P(), row, row, row, vec, vec, col, P(), P(), P(),
        row, vec, row, vec, vec, vec, col, P(),
    )
    out_specs = (
        act, act, P(), P(), row, row, row, vec, vec, col, P(), P(), P(), row, vec, row, vec, vec, vec, col, P(),
    )
    return jax.shard_map(shards, mesh=mesh, in_specs=in_specs, out_specs=out_specs, check_vma=False)
```
